128 devices in a mesh: rows: 8 (over x, core), cols: 16 (over y, z).
Axes of the slice: x: 4, y: 4, z: 4, core: 2. Of those that a mesh axis runs over, the one named last changes fastest.
Arguments:
- luminance: float32 [2048, 8192], P('rows', 'cols'), may hold values from 0 to 1
- grad_x: float32 [4, 2048, 8192], P(None, 'rows', 'cols'), may hold values from -0.6 to 0.6
- grad_y: float32 [4, 2048, 8192], P(None, 'rows', 'cols'), may hold values from -0.6 to 0.6
- labels: int32 [2048, 8192], P('rows', 'cols'), may hold values from 0 to 3
Outputs:
- stitched: float32 [2048, 8192], P('rows', 'cols')
The draws below stay inside these ranges and needn't reach their ends.
All inputs are finite; a program needn't handle non-finite values.
Results may differ from the reference program's by a relative error of at most 0.0003.
Values sent between devices are 32-bit elements; how exact they have to be, the bound alone decides.
A program may use at most 128 MiB of HBM per device.

```python
import math
import jax
import jax.numpy as jnp
from jax import lax

LENSES = 4
NU = 2
H = 2048
W = 8192


def touch_ends(result, own_key, low, top_value):
    index_at = [jax.random.randint(jax.random.fold_in(own_key, axis), (), 0, length) for axis, length in enumerate(result.shape)]
    longest = result.shape.index(max(result.shape))
    next_to = index_at[:longest] + [(index_at[longest] + 1) % result.shape[longest]] + index_at[longest + 1:]
    return result.at[tuple(index_at)].set(low).at[tuple(next_to)].set(top_value)


def block_scale(rng, extent, pieces, least, largest):
    loudness = 1.0
    for position, parts in pieces:
        heights = jax.random.uniform(jax.random.fold_in(jax.random.fold_in(rng, 6), position), (parts,), jnp.float32, least / len(pieces), largest / len(pieces))
        loudness = loudness * jnp.repeat(jnp.exp(heights), extent[position] // parts).reshape((-1,) + (1,) * (len(extent) - 1 - position))
    return loudness


def scatter_about(own_key, extent, deviation, reach, cuts=(), kind=jnp.bfloat16):
    loudness = block_scale(own_key, extent, cuts, -0.22, 0.18) if cuts else 1.0
    entries = jax.random.normal(own_key, extent, jnp.float32) * deviation * loudness
    return jnp.minimum(jnp.maximum(entries, -reach), reach).astype(kind)


def setup_inputs(seed: int = 0) -> dict:
    splits = jax.random.split(jax.random.key(seed), 5)
    luminance = jnp.clip(1.0 * jax.random.uniform(splits[0], (H, W), jnp.float32) ** block_scale(splits[0], (H, W), ((0, 8), (1, 16)), -0.2, 0.2), 0.0, 1.0)
    grad_x = scatter_about(splits[1], (LENSES, H, W), 0.1, 0.6, ((1, 8), (2, 16)), jnp.float32)
    grad_y = scatter_about(splits[2], (LENSES, H, W), 0.1, 0.6, ((1, 8), (2, 16)), jnp.float32)
    labels = touch_ends(jax.random.randint(splits[3], (H, W), 0, LENSES), jax.random.fold_in(splits[3], 1), 0, LENSES - 1).astype(jnp.int32)
    return dict(luminance=luminance, grad_x=grad_x, grad_y=grad_y, labels=labels)


screen_weight = 4e-06
omega = 0.8

def degree(nrows, ncols):
    row_ids = jnp.arange(nrows, dtype=jnp.int32)
    col_ids = jnp.arange(ncols, dtype=jnp.int32)
    row_part = (row_ids > 0).astype(jnp.float32) + (row_ids < nrows - 1).astype(jnp.float32)
    col_part = (col_ids > 0).astype(jnp.float32) + (col_ids < ncols - 1).astype(jnp.float32)
    return row_part[:, None] + col_part[None, :]

def apply_op(field, deg, coef):
    padded = jnp.pad(field, 1)
    beside = padded[2:, 1:-1] + padded[:-2, 1:-1] + padded[1:-1, 2:] + padded[1:-1, :-2]
    return screen_weight * field + coef * (deg * field - beside)

def smooth(field, rhs, deg, coef):
    diag = screen_weight + coef * deg
    for sweep in range(NU):
        field = field + omega * (rhs - apply_op(field, deg, coef)) / diag
    return field

def restrict(field):
    nrows, ncols = field.shape
    return field.reshape(nrows // 2, 2, ncols // 2, 2).sum(axis=(1, 3)) * 0.25

def prolong(field):
    return jnp.repeat(jnp.repeat(field, 2, axis=0), 2, axis=1)

def dct_table(count):
    freq = jnp.arange(count, dtype=jnp.int32)[:, None]
    place = jnp.arange(count, dtype=jnp.int32)[None, :]
    phase = (2 * place + 1) * freq % (4 * count)
    angle = phase.astype(jnp.float32) * (math.pi / (2 * count))
    scale = jnp.where(freq == 0, math.sqrt(1.0 / count), math.sqrt(2.0 / count))
    return scale * jnp.cos(angle)

def eigen_part(start, width, count):
    freq = (start + jnp.arange(width, dtype=jnp.int32)).astype(jnp.float32)
    sine = jnp.sin(freq * (math.pi / (2 * count)))
    return 4.0 * sine * sine

def reference(luminance, grad_x, grad_y, labels):
    nrows, ncols = luminance.shape
    lens_ids = jnp.arange(LENSES, dtype=jnp.int32)[:, None, None]
    chosen = labels[None] == lens_ids
    sel_x = lax.optimization_barrier(jnp.sum(jnp.where(chosen, grad_x, 0.0), axis=0))
    sel_y = lax.optimization_barrier(jnp.sum(jnp.where(chosen, grad_y, 0.0), axis=0))
    col_ids = jnp.arange(ncols, dtype=jnp.int32)[None, :]
    row_ids = jnp.arange(nrows, dtype=jnp.int32)[:, None]
    sel_x = jnp.where(col_ids < ncols - 1, sel_x, 0.0)
    sel_y = jnp.where(row_ids < nrows - 1, sel_y, 0.0)
    from_left = jnp.pad(sel_x[:, :-1], ((0, 0), (1, 0)))
    from_up = jnp.pad(sel_y[:-1, :], ((1, 0), (0, 0)))
    rhs = screen_weight * luminance + from_left - sel_x + from_up - sel_y
    deg0 = degree(nrows, ncols)
    field = smooth(luminance, rhs, deg0, 1.0)
    coarse_one = restrict(rhs - apply_op(field, deg0, 1.0))
    deg1 = degree(nrows // 2, ncols // 2)
    err_one = smooth(jnp.zeros_like(coarse_one), coarse_one, deg1, 0.5)
    coarse_two = restrict(coarse_one - apply_op(err_one, deg1, 0.5))
    crows, ccols = coarse_two.shape
    row_table = dct_table(crows)
    col_table = dct_table(ccols)
    lam = screen_weight + 0.25 * (eigen_part(0, crows, crows)[:, None] + eigen_part(0, ccols, ccols)[None, :])
    hp = lax.Precision.HIGHEST
    modes = jnp.dot(jnp.dot(row_table, coarse_two, precision=hp), col_table.T, precision=hp)
    err_two = jnp.dot(jnp.dot(row_table.T, modes / lam, precision=hp), col_table, precision=hp)
    err_one = smooth(err_one + prolong(err_two), coarse_one, deg1, 0.5)
    return smooth(field + prolong(err_one), rhs, deg0, 1.0)
```

```python
import functools
import math

import jax
import jax.numpy as jnp
import ml_dtypes
import numpy as np
from jax import lax
from jax.experimental import pallas as pl
from jax.experimental.pallas import tpu as pltpu
from jax.sharding import PartitionSpec as P

MESH = pl.DeviceIdType.MESH
SCREEN = 4e-06
OMEGA = 0.8
NR, NC = 8, 16
H0, W0 = 256, 512
QR, QC = 64, 128
ER, EC = 72, 256
BF, F32 = jnp.bfloat16, jnp.float32


def bf16_parts(x, parts):
    out = []
    rest = np.asarray(x, np.float64)
    for _ in range(parts):
        piece = rest.astype(ml_dtypes.bfloat16)
        out.append(piece)
        rest = rest - piece.astype(np.float64)
    return out


@functools.lru_cache(maxsize=None)
def tables():
    rows, cols = NR * QR, NC * QC
    perm = np.zeros((W0, W0), np.float32)
    q = np.arange(QC)
    for pc in range(4):
        perm[4 * q + pc, pc * QC + q] = 1
    side = np.zeros((128, W0), np.float32)
    for pc in range(4):
        for s in range(4):
            side[112 + 4 * s + pc, pc * 128 + 124 + s] = 1
            side[4 * s + pc, pc * 128 + s] = 1
    k = np.arange(rows)
    place = np.arange(rows)
    phase = ((2 * place[:, None] + 1) * k[None, :]) % (4 * rows)
    scale = np.where(k == 0, math.sqrt(1.0 / rows), math.sqrt(2.0 / rows))
    ct = np.zeros((rows + 32, rows))
    ct[16:-16] = scale[None, :] * np.cos(phase * (math.pi / (2 * rows)))
    ct = np.stack(bf16_parts(ct, 3))
    mu = SCREEN + 0.25 * 4 * np.sin(np.pi * k / (2 * rows)) ** 2
    half = 1 + 2 * mu
    rho = half - np.sqrt(4 * mu + 4 * mu * mu)
    g0 = 1 / (0.25 * (1 / rho - rho))
    t = np.arange(QC)
    from_left = rho[None, :] ** (t[:, None] + 1)
    from_right = rho[None, :] ** (QC - t[:, None])
    small = np.zeros((16, rows))
    for i in range(7):
        small[i] = rho ** (2**i)
    small[7] = g0
    small[8] = g0 * rho
    small[9] = rho ** (QC + 1)
    small[10] = 2 + 4 * mu
    tab = np.concatenate([from_left, from_right, small]).astype(np.float32)
    dist = g0 / (1 - rho ** (2 * cols)) * rho ** (QC * np.arange(32)[:, None])
    dist = dist.reshape(32, 4, 128)
    dist = np.concatenate([dist, dist], axis=1).astype(np.float32)
    return (
        perm.astype(ml_dtypes.bfloat16),
        perm.T.astype(ml_dtypes.bfloat16),
        side.astype(ml_dtypes.bfloat16),
        ct,
        tab,
        dist,
    )


def split2(x):
    hi = x.astype(BF)
    return hi, (x - hi.astype(F32)).astype(BF)


def split3(x):
    hi = x.astype(BF)
    rest = x - hi.astype(F32)
    mid = rest.astype(BF)
    return hi, mid, (rest - mid.astype(F32)).astype(BF)


def mm(a, b, dims=((1,), (0,))):
    return lax.dot_general(a, b, (dims, ((), ())), preferred_element_type=F32)


def permuted(x, table):
    hi, mid = split2(x)
    return mm(hi, table) + mm(mid, table)


def roll(x, shift, axis):
    return pltpu.roll(x, shift % x.shape[axis], axis)


def around(ref, pr, pc, n):
    up = ref[(pr - 1) * n + pc] if pr > 0 else roll(ref[(n - 1) * n + pc], 1, 0)
    down = ref[(pr + 1) * n + pc] if pr < n - 1 else roll(ref[pc], -1, 0)
    left = ref[pr * n + pc - 1] if pc > 0 else roll(ref[pr * n + n - 1], 1, 1)
    right = ref[pr * n + pc + 1] if pc < n - 1 else roll(ref[pr * n], -1, 1)
    return (up + down) + (left + right)


def klass(p, n):
    return 0 if p == 0 else (2 if p == n - 1 else 1)


def which(pr, pc, n):
    return 3 * klass(pr, n) + klass(pc, n)


def sweep(src, dst, f, w, n, c):
    for pr in range(n):
        for pc in range(n):
            i = pr * n + pc
            nb = around(src, pr, pc, n)
            nb = nb if c == 1.0 else c * nb
            dst[i] = (1 - OMEGA) * src[i] + w[which(pr, pc, n)] * (f[i] + nb)


def kernel(
    lum_h, gx_h, gy_h, lab_h, perm_h, permt_h, side_h, ct_h, tab_h, dist_h,
    out_h,
    gx, gy, lab, raw, perm, permt, side, ct, tab, dist,
    to_right, to_left, from_l, from_r, corner_l, corner_r,
    lum, selx, sely, rhs, fa, fb, w0, d0, w1, d1, f1, ea, eb, ec,
    strip, mom, xs, out,
    in_sem, const_sem, out_sem, h_send, h_recv, r_send, r_recv, c_send, c_recv,
):
    r = lax.axis_index("rows")
    c = lax.axis_index("cols")

    def row_peer(d):
        return lax.rem(r + d + NR, NR)

    def col_peer(d):
        return lax.rem(c + d + NC, NC)

    barrier = pltpu.get_barrier_semaphore()
    peers = [(d, 0) for d in range(1, NR)] + [(0, d) for d in range(1, NC)]
    peers += [(1, 1), (1, -1), (-1, 1), (-1, -1)]
    for dr, dc in peers:
        pl.semaphore_signal(
            barrier, inc=1, device_id=(row_peer(dr), col_peer(dc)), device_id_type=MESH
        )

    CH = 64
    loads = []
    for i in range(H0 // CH):
        rows = pl.ds(i * CH, CH)
        loads.append([
            pltpu.make_async_copy(gx_h.at[:, rows], gx.at[:, rows], in_sem.at[i, 0]),
            pltpu.make_async_copy(gy_h.at[:, rows], gy.at[:, rows], in_sem.at[i, 1]),
            pltpu.make_async_copy(lab_h.at[rows], lab.at[rows], in_sem.at[i, 2]),
        ] + [
            pltpu.make_async_copy(lum_h.at[rows, pl.ds(t * 128, 128)], raw.at[0, t, rows], in_sem.at[i, 3 + t])
            for t in range(4)
        ])
    for group in loads:
        for one in group:
            one.start()
    consts = [
        pltpu.make_async_copy(a, b, const_sem.at[i])
        for i, (a, b) in enumerate(
            [(perm_h, perm), (side_h, side), (ct_h, ct), (tab_h, tab), (dist_h, dist), (permt_h, permt)]
        )
    ]
    for one in consts:
        one.start()

    ri = lax.broadcasted_iota(jnp.int32, (ER, EC), 0)
    li = lax.broadcasted_iota(jnp.int32, (ER, EC), 1)
    out_rows = ((r == 0) & (ri >= 68)) | ((r == NR - 1) & (ri >= 64) & (ri < 68))
    out_cols = ((c == 0) & (li >= 192)) | ((c == NC - 1) & (li >= 128) & (li < 192))
    inside = jnp.where(out_rows | out_cols, 0.0, 1.0).astype(F32)
    edge_rows = [((r == 0) & (ri == 0)), None, ((r == NR - 1) & (ri == QR - 1))]
    edge_cols = [((c == 0) & (li == 0)), None, ((c == NC - 1) & (li == QC - 1))]
    for a in range(3):
        for b in range(3):
            deg = jnp.full((ER, EC), 4.0, F32)
            if a != 1:
                deg = deg - jnp.where(edge_rows[a], 1.0, 0.0)
            if b != 1:
                deg = deg - jnp.where(edge_cols[b], 1.0, 0.0)
            for wr, dr_, coef in ((w0, d0, 1.0), (w1, d1, 0.5)):
                if coef == 0.5 and (a == 1 or b == 1):
                    continue
                dr_[3 * a + b] = coef * deg
                wr[3 * a + b] = inside * (OMEGA / (SCREEN + coef * deg))
    xs[...] = jnp.zeros_like(xs)

    lane8 = lax.broadcasted_iota(jnp.int32, (8, W0), 1)
    sub8 = lax.broadcasted_iota(jnp.int32, (8, W0), 0)
    last_col = (c == NC - 1) & (lane8 == W0 - 1)
    for i in range(H0 // CH):
        for one in loads[i]:
            one.wait()

        def select(s, carry, i=i):
            row = pl.multiple_of(i * CH + s * 8, 8)
            rows = pl.ds(row, 8)
            lb = lab[rows, :]
            is0, is1, is2 = lb == 0, lb == 1, lb == 2
            sx = jnp.where(is0, gx[0, rows, :], jnp.where(is1, gx[1, rows, :], jnp.where(is2, gx[2, rows, :], gx[3, rows, :])))
            sy = jnp.where(is0, gy[0, rows, :], jnp.where(is1, gy[1, rows, :], jnp.where(is2, gy[2, rows, :], gy[3, rows, :])))
            sx = jnp.where(last_col, 0.0, sx)
            last_row = (r == NR - 1) & (sub8 + row == H0 - 1)
            sy = jnp.where(last_row, 0.0, sy)
            for t in range(4):
                raw[1, t, rows, :] = sx[:, t * 128:(t + 1) * 128]
                raw[2, t, rows, :] = sy[:, t * 128:(t + 1) * 128]
            return carry

        lax.fori_loop(0, CH // 8, select, 0, unroll=2)

    lane = lax.broadcasted_iota(jnp.int32, (QR, 128), 1)
    group = lane // 16
    for tile in range(2):
        packed_r = jnp.zeros((QR, 128), F32)
        packed_l = jnp.zeros((QR, 128), F32)
        for g in range(8):
            idx = tile * 8 + g
            if idx >= 12:
                break
            a, rp = divmod(idx, 4)
            edge = raw[a, 3, pl.ds(rp, QR, stride=4), :]
            packed_r = jnp.where(group == g, roll(edge, 16 * g - 112, 1), packed_r)
            edge = raw[a, 0, pl.ds(rp, QR, stride=4), :]
            packed_l = jnp.where(group == g, roll(edge, 16 * g, 1), packed_l)
        to_right[:, pl.ds(tile * 128, 128)] = packed_r
        to_left[:, pl.ds(tile * 128, 128)] = packed_l

    pl.semaphore_wait(barrier, len(peers))

    top, bottom = pl.ds(0, 16), pl.ds(H0 - 16, 16)
    halo = []
    for i, (src, dst, dr, dc) in enumerate([
        (to_right, from_l, 0, 1),
        (to_left, from_r, 0, -1),
        (raw.at[:, :, bottom], raw.at[:, :, pl.ds(H0 + 16, 16)], 1, 0),
        (raw.at[:, :, top], raw.at[:, :, pl.ds(H0, 16)], -1, 0),
        (raw.at[:, 3, bottom], corner_l.at[:, pl.ds(16, 16)], 1, 1),
        (raw.at[:, 0, bottom], corner_r.at[:, pl.ds(16, 16)], 1, -1),
        (raw.at[:, 3, top], corner_l.at[:, pl.ds(0, 16)], -1, 1),
        (raw.at[:, 0, top], corner_r.at[:, pl.ds(0, 16)], -1, -1),
    ]):
        copy = pltpu.make_async_remote_copy(
            src_ref=src, dst_ref=dst, send_sem=h_send.at[i], recv_sem=h_recv.at[i],
            device_id=(row_peer(dr), col_peer(dc)), device_id_type=MESH,
        )
        copy.start()
        halo.append(copy)

    fields = (lum, selx, sely)

    def by_phase(a, rows):
        return jnp.concatenate([raw[a, t, rows, :] for t in range(4)], axis=1)

    consts[0].wait()
    consts[1].wait()
    for a in range(3):
        x = jnp.concatenate([by_phase(a, pl.ds(rp, QR, stride=4)) for rp in range(4)], axis=0)
        y = permuted(x, perm[...])
        for rp in range(4):
            for pc in range(4):
                fields[a][rp * 4 + pc, pl.ds(0, QR), pl.ds(0, 128)] = y[rp * QR:(rp + 1) * QR, pc * 128:(pc + 1) * 128]

    for copy in halo:
        copy.wait()
    x = jnp.concatenate([by_phase(a, pl.ds(H0 + rp, 8, stride=4)) for a in range(3) for rp in range(4)], axis=0)
    y = permuted(x, perm[...])
    for a in range(3):
        for rp in range(4):
            i = (a * 4 + rp) * 8
            for pc in range(4):
                fields[a][rp * 4 + pc, pl.ds(QR, 8), pl.ds(0, 128)] = y[i:i + 8, pc * 128:(pc + 1) * 128]
    lane8 = lax.broadcasted_iota(jnp.int32, (8, 128), 1)
    for a in range(3):
        pieces = []
        for rp in range(4):
            tile, g = divmod(a * 4 + rp, 8)
            fl = roll(from_l[:, pl.ds(tile * 128, 128)], 112 - 16 * g, 1)
            fr = roll(from_r[:, pl.ds(tile * 128, 128)], -16 * g, 1)
            pieces.append(jnp.where(lane < 64, fr, fl))
            pieces.append(jnp.where(
                lane8 < 64,
                corner_r[a, pl.ds(rp, 8, stride=4), :],
                corner_l[a, pl.ds(rp, 8, stride=4), :],
            ))
        y = permuted(jnp.concatenate(pieces, axis=0), side[...])
        for rp in range(4):
            for pc in range(4):
                fields[a][rp * 4 + pc, :, pl.ds(128, 128)] = y[rp * ER:(rp + 1) * ER, pc * 128:(pc + 1) * 128]

    for i in range(16):
        lum[i] = lum[i] * inside
        if i % 4 == 3:
            selx[i] = selx[i] * inside
        if i // 4 == 3:
            sely[i] = sely[i] * inside
    for pr in range(4):
        for pc in range(4):
            i = pr * 4 + pc
            left = selx[i - 1] if pc > 0 else roll(selx[pr * 4 + 3], 1, 1)
            up = sely[i - 4] if pr > 0 else roll(sely[12 + pc], 1, 0)
            rhs[i] = SCREEN * lum[i] + (left - selx[i]) + (up - sely[i])

    sweep(lum, fa, rhs, w0, 4, 1.0)
    sweep(fa, fb, rhs, w0, 4, 1.0)
    for a in range(2):
        for b in range(2):
            total = None
            for pr in (2 * a, 2 * a + 1):
                for pc in (2 * b, 2 * b + 1):
                    i = pr * 4 + pc
                    res = (rhs[i] - SCREEN * fb[i]) + (around(fb, pr, pc, 4) - d0[which(pr, pc, 4)] * fb[i])
                    total = res if total is None else total + res
            f1[a * 2 + b] = 0.25 * total
            ea[a * 2 + b] = w1[which(a, b, 2)] * (0.25 * total)
    sweep(ea, eb, f1, w1, 2, 0.5)
    total = None
    for a in range(2):
        for b in range(2):
            i = a * 2 + b
            res = (f1[i] - SCREEN * eb[i]) + (0.5 * around(eb, a, b, 2) - d1[which(a, b, 2)] * eb[i])
            total = res if total is None else total + res
    strip[r] = 0.25 * total[0:QR, 0:QC]

    copies = []
    for d in range(1, NR):
        copy = pltpu.make_async_remote_copy(
            src_ref=strip.at[r], dst_ref=strip.at[r], send_sem=r_send.at[d], recv_sem=r_recv.at[d],
            device_id=(row_peer(d), c), device_id_type=MESH,
        )
        copy.start()
        copies.append(copy)
    for one in consts[2:]:
        one.wait()
    for copy in copies:
        copy.wait()

    whole = strip[...].reshape(NR * QR, QC)
    xh, xm, xl = split3(whole.T)
    inner = pl.ds(16, NR * QR)
    ch, cm, cl = ct[0, inner, :], ct[1, inner, :], ct[2, inner, :]
    g = mm(xh, ch) + ((mm(xh, cm) + mm(xm, ch)) + (mm(xm, cm) + (mm(xh, cl) + mm(xl, ch))))

    def small(i):
        return tab[pl.ds(2 * QC + i, 1), :]

    jrow = lax.broadcasted_iota(jnp.int32, (QC, NR * QR), 0)
    fwd, bwd = g, g
    for i, s in enumerate((1, 2, 4, 8, 16, 32, 64)):
        p = small(i)
        fwd = fwd + jnp.where(jrow >= s, roll(fwd, s, 0) * p, 0.0)
        bwd = bwd + jnp.where(jrow < QC - s, roll(bwd, -s, 0) * p, 0.0)
    lines = [fwd[QC - 1:QC], bwd[0:1], g[0:1], g[QC - 1:QC]]
    mom[c] = jnp.concatenate([x[:, t * 128:(t + 1) * 128] for x in lines for t in range(4)], axis=0)

    copies = []
    for d in range(1, NC):
        part = pl.ds(0, 16 if d in (1, NC - 1) else 8)
        copy = pltpu.make_async_remote_copy(
            src_ref=mom.at[c, part], dst_ref=mom.at[c, part], send_sem=c_send.at[d], recv_sem=c_recv.at[d],
            device_id=(r, col_peer(d)), device_id_type=MESH,
        )
        copy.start()
        copies.append(copy)
    own = small(7) * (fwd + bwd - g)
    for copy in copies:
        copy.wait()

    low = lax.broadcasted_iota(jnp.int32, (8, 128), 0) < 4
    sum_a = jnp.zeros((8, 128), F32)
    sum_b = jnp.zeros((8, 128), F32)
    for o in range(NC):
        m = mom[o, pl.ds(0, 8), :]
        sum_a = sum_a + m * jnp.where(low, dist[lax.rem(c - o + 63, 32)], dist[c + o])
        sum_b = sum_b + m * jnp.where(low, dist[lax.rem(62 - c - o, 32)], dist[lax.rem(o - c + 63, 32)])

    def as_row(x):
        x = x[0:4] + x[4:8]
        return jnp.concatenate([x[t:t + 1] for t in range(4)], axis=1)

    def line(o, i):
        x = mom[o, pl.ds(8, 8), :]
        return jnp.concatenate([x[4 * i + t:4 * i + t + 1] for t in range(4)], axis=1)

    a_in, b_in = as_row(sum_a), as_row(sum_b)
    own = own + tab[pl.ds(0, QC), :] * a_in + tab[pl.ds(QC, QC), :] * b_in
    xs[pl.ds(0, QC), :] = own
    left1 = a_in + small(8) * lines[1] + small(9) * b_in
    right1 = b_in + small(8) * lines[0] + small(9) * a_in
    left2 = small(10) * left1 - own[0:1] - 4.0 * line(col_peer(-1), 1)
    right2 = small(10) * right1 - own[QC - 1:QC] - 4.0 * line(col_peer(1), 0)
    zero6 = jnp.zeros((6, NR * QR), F32)
    xs[pl.ds(QC, 8), :] = jnp.concatenate([right1, right2, zero6], axis=0)
    xs[pl.ds(EC - 8, 8), :] = jnp.concatenate([zero6, left2, left1], axis=0)

    base = pl.multiple_of(r * QR, QR)
    sub16 = lax.broadcasted_iota(jnp.int32, (16, NR * QR), 0)
    back = []
    for i in range(3):
        tail = jnp.where(
            sub16 < 8,
            ct[i, pl.ds(base + QR + 16, 16), :].astype(F32),
            ct[i, pl.ds(base, 16), :].astype(F32),
        ).astype(BF)
        back.append(jnp.concatenate([ct[i, pl.ds(base + 16, QR), :], tail], axis=0))
    th, tm, tl = back
    xh, xm, xl = split3(xs[...])
    nt = ((1,), (1,))
    e2 = mm(th, xh, nt) + ((mm(th, xm, nt) + mm(tm, xh, nt)) + (mm(tm, xm, nt) + (mm(th, xl, nt) + mm(tl, xh, nt))))
    sub8 = lax.broadcasted_iota(jnp.int32, (8, EC), 0)
    e2 = jnp.concatenate([e2[0:QR], jnp.where(sub8 < 4, e2[QR:QR + 8], e2[QR + 8:QR + 16])], axis=0)
    e2 = e2 * inside

    for i in range(4):
        ea[i] = eb[i] + e2
    sweep(ea, ec, f1, w1, 2, 0.5)
    sweep(ec, ea, f1, w1, 2, 0.5)
    for pr in range(4):
        for pc in range(4):
            fa[pr * 4 + pc] = fb[pr * 4 + pc] + ea[(pr // 2) * 2 + pc // 2]
    sweep(fa, lum, rhs, w0, 4, 1.0)
    sweep(lum, fb, rhs, w0, 4, 1.0)
    x = jnp.concatenate([
        jnp.concatenate([fb[pr * 4 + pc, pl.ds(0, QR), pl.ds(0, QC)] for pc in range(4)], axis=1)
        for pr in range(4)
    ], axis=0)
    y = permuted(x, permt[...])
    for pr in range(4):
        for t in range(4):
            out[t, pl.ds(pr, QR, stride=4), :] = y[pr * QR:(pr + 1) * QR, t * 128:(t + 1) * 128]
    copies = [
        pltpu.make_async_copy(out.at[t], out_h.at[:, pl.ds(t * 128, 128)], out_sem.at[t]) for t in range(4)
    ]
    for copy in copies:
        copy.start()
    for copy in copies:
        copy.wait()


def shards(luminance, grad_x, grad_y, labels):
    consts = tables()
    vmem = pltpu.VMEM
    phases = vmem((16, ER, EC), F32)
    quarter = vmem((4, ER, EC), F32)
    nine = vmem((9, ER, EC), F32)
    dma = pltpu.SemaphoreType.DMA
    return pl.pallas_call(
        kernel,
        out_shape=jax.ShapeDtypeStruct((H0, W0), F32),
        in_specs=[pl.BlockSpec(memory_space=pl.ANY)] * 10,
        out_specs=pl.BlockSpec(memory_space=pl.ANY),
        scratch_shapes=[
            vmem((4, H0, W0), F32),
            vmem((4, H0, W0), F32),
            vmem((H0, W0), jnp.int32),
            vmem((3, 4, H0 + 32, 128), F32),
            vmem((W0, W0), BF),
            vmem((W0, W0), BF),
            vmem((128, W0), BF),
            vmem(consts[3].shape, BF),
            vmem(consts[4].shape, F32),
            vmem(consts[5].shape, F32),
            vmem((QR, 256), F32),
            vmem((QR, 256), F32),
            vmem((QR, 256), F32),
            vmem((QR, 256), F32),
            vmem((3, 32, 128), F32),
            vmem((3, 32, 128), F32),
            phases, phases, phases, phases, phases, phases,
            nine, nine, nine, nine,
            quarter, quarter, quarter, quarter,
            vmem((NR, QR, QC), F32),
            vmem((NC, 16, 128), F32),
            vmem((EC, NR * QR), F32),
            vmem((4, H0, 128), F32),
            dma((4, 7)),
            dma((6,)),
            dma((4,)),
            dma((8,)),
            dma((8,)),
            dma((NR,)),
            dma((NR,)),
            dma((NC,)),
            dma((NC,)),
        ],
        compiler_params=pltpu.CompilerParams(
            collective_id=0, has_side_effects=True, vmem_limit_bytes=56 * 1024 * 1024
        ),
    )(luminance, grad_x, grad_y, labels, *[jnp.asarray(x) for x in consts])


def solution(mesh):
    return jax.shard_map(
        shards,
        mesh=mesh,
        in_specs=(
            P("rows", "cols"),
            P(None, "rows", "cols"),
            P(None, "rows", "cols"),
            P("rows", "cols"),
        ),
        out_specs=P("rows", "cols"),
        check_vma=False,
    )
```

```python
import functools
import math

import jax
import jax.numpy as jnp
import ml_dtypes
import numpy as np
from jax import lax
from jax.experimental import pallas as pl
from jax.experimental.pallas import tpu as pltpu
from jax.sharding import PartitionSpec as P

MESH = pl.DeviceIdType.MESH
SCREEN = 4e-06
OMEGA = 0.8
NR, NC = 8, 16
H0, W0 = 256, 512
QR, QC = 64, 128
ER, EC = 72, 256
BF, F32 = jnp.bfloat16, jnp.float32


def bf16_parts(x, parts):
    out = []
    rest = np.asarray(x, np.float64)
    for _ in range(parts):
        piece = rest.astype(ml_dtypes.bfloat16)
        out.append(piece)
        rest = rest - piece.astype(np.float64)
    return out


@functools.lru_cache(maxsize=None)
def tables():
    rows, cols = NR * QR, NC * QC
    k = np.arange(rows)
    place = np.arange(rows)
    phase = ((2 * place[:, None] + 1) * k[None, :]) % (4 * rows)
    scale = np.where(k == 0, math.sqrt(1.0 / rows), math.sqrt(2.0 / rows))
    ct = np.zeros((rows + 32, rows))
    ct[16:-16] = scale[None, :] * np.cos(phase * (math.pi / (2 * rows)))
    ct = np.stack(bf16_parts(ct, 3))
    mu = SCREEN + 0.25 * 4 * np.sin(np.pi * k / (2 * rows)) ** 2
    half = 1 + 2 * mu
    rho = half - np.sqrt(4 * mu + 4 * mu * mu)
    g0 = 1 / (0.25 * (1 / rho - rho))
    t = np.arange(QC)
    from_left = rho[None, :] ** (t[:, None] + 1)
    from_right = rho[None, :] ** (QC - t[:, None])
    small = np.zeros((16, rows))
    for i in range(7):
        small[i] = rho ** (2**i)
    small[7] = g0
    small[8] = g0 * rho
    small[9] = rho ** (QC + 1)
    small[10] = 2 + 4 * mu
    small[11] = rho**QC
    small[12] = 1 / rho
    small[13] = rho**-2.0
    tab = np.concatenate([from_left, from_right, small]).astype(np.float32)
    dist = g0 / (1 - rho ** (2 * cols)) * rho ** (QC * np.arange(32)[:, None])
    dist = dist.reshape(32, 4, 128)
    dist = np.concatenate([dist, dist], axis=1).astype(np.float32)
    return ct, tab, dist


def split2(x):
    hi = x.astype(BF)
    return hi, (x - hi.astype(F32)).astype(BF)


def split3(x):
    hi = x.astype(BF)
    rest = x - hi.astype(F32)
    mid = rest.astype(BF)
    return hi, mid, (rest - mid.astype(F32)).astype(BF)


def mm(a, b, dims=((1,), (0,))):
    return lax.dot_general(a, b, (dims, ((), ())), preferred_element_type=F32)


def permuted(x, table):
    hi, mid = split2(x)
    return mm(hi, table) + mm(mid, table)


def roll(x, shift, axis):
    return pltpu.roll(x, shift % x.shape[axis], axis)


def around(ref, pr, pc, n):
    up = ref[(pr - 1) * n + pc] if pr > 0 else roll(ref[(n - 1) * n + pc], 1, 0)
    down = ref[(pr + 1) * n + pc] if pr < n - 1 else roll(ref[pc], -1, 0)
    left = ref[pr * n + pc - 1] if pc > 0 else roll(ref[pr * n + n - 1], 1, 1)
    right = ref[pr * n + pc + 1] if pc < n - 1 else roll(ref[pr * n], -1, 1)
    return (up + down) + (left + right)


def klass(p, n):
    return 0 if p == 0 else (2 if p == n - 1 else 1)


def which(pr, pc, n):
    return 3 * klass(pr, n) + klass(pc, n)


def sweep(src, dst, f, w, n, c):
    for pr in range(n):
        for pc in range(n):
            i = pr * n + pc
            nb = around(src, pr, pc, n)
            nb = nb if c == 1.0 else c * nb
            dst[i] = (1 - OMEGA) * src[i] + w[which(pr, pc, n)] * (f[i] + nb)


def kernel(
    lum_h, gx_h, gy_h, lab_h, ct_h, tab_h, dist_h,
    out_h,
    gx, gy, lab, raw, perm, permt, side, ct, tab, dist,
    to_right, to_left, from_l, from_r,
    lum, selx, sely, rhs, fa, fb, w0, d0, w1, d1, f1, ea, eb, ec,
    strip, mom, xs, out,
    in_sem, const_sem, out_sem, h_send, h_recv, r_send, r_recv, c_send, c_recv,
):
    r = lax.axis_index("rows")
    c = lax.axis_index("cols")

    def row_peer(d):
        return lax.rem(r + d + NR, NR)

    def col_peer(d):
        return lax.rem(c + d + NC, NC)

    sibling = r + 1 - 2 * lax.rem(r, 2)
    barrier = pltpu.get_barrier_semaphore()
    peers = [(d, 0) for d in (1, 2, 4, 6, 7)] + [(0, d) for d in range(1, NC)]
    peers += [(1, 1), (1, -1), (-1, 1), (-1, -1)]
    for dr, dc in peers:
        pl.semaphore_signal(
            barrier, inc=1, device_id=(row_peer(dr), col_peer(dc)), device_id_type=MESH
        )

    CH = 64
    loads = []
    for i in range(H0 // CH):
        rows = pl.ds(i * CH, CH)
        loads.append([
            pltpu.make_async_copy(gx_h.at[:, rows], gx.at[:, rows], in_sem.at[i, 0]),
            pltpu.make_async_copy(gy_h.at[:, rows], gy.at[:, rows], in_sem.at[i, 1]),
            pltpu.make_async_copy(lab_h.at[rows], lab.at[rows], in_sem.at[i, 2]),
        ] + [
            pltpu.make_async_copy(lum_h.at[rows, pl.ds(t * 128, 128)], raw.at[0, t, rows], in_sem.at[i, 3 + t])
            for t in range(4)
        ])
    for group in loads:
        for one in group:
            one.start()
    consts = [
        pltpu.make_async_copy(a, b, const_sem.at[i])
        for i, (a, b) in enumerate([(ct_h, ct), (tab_h, tab), (dist_h, dist)])
    ]

    src = lax.broadcasted_iota(jnp.int32, (W0, 128), 0)
    dst = 4 * lax.broadcasted_iota(jnp.int32, (W0, 128), 1)
    back_src = 4 * lax.broadcasted_iota(jnp.int32, (128, W0), 0)
    back_dst = lax.broadcasted_iota(jnp.int32, (128, W0), 1)
    src_s = lax.broadcasted_iota(jnp.int32, (128, 128), 0)
    lane_s = lax.broadcasted_iota(jnp.int32, (128, 128), 1)
    outer = (lane_s < 4) | (lane_s >= 124)
    for pc in range(4):
        part = pl.ds(pc * 128, 128)
        perm[:, part] = jnp.where(src == dst + pc, 1.0, 0.0).astype(BF)
        permt[part, :] = jnp.where(back_src + pc == back_dst, 1.0, 0.0).astype(BF)
        side[:, part] = jnp.where(outer & (src_s == lax.rem(4 * lane_s + pc, 128)), 1.0, 0.0).astype(BF)

    ri = lax.broadcasted_iota(jnp.int32, (ER, EC), 0)
    li = lax.broadcasted_iota(jnp.int32, (ER, EC), 1)
    out_rows = ((r == 0) & (ri >= 68)) | ((r == NR - 1) & (ri >= 64) & (ri < 68))
    out_cols = ((c == 0) & (li >= 192)) | ((c == NC - 1) & (li >= 128) & (li < 192))
    inside = jnp.where(out_rows | out_cols, 0.0, 1.0).astype(F32)
    edge_rows = [((r == 0) & (ri == 0)), None, ((r == NR - 1) & (ri == QR - 1))]
    edge_cols = [((c == 0) & (li == 0)), None, ((c == NC - 1) & (li == QC - 1))]
    for a in range(3):
        for b in range(3):
            deg = jnp.full((ER, EC), 4.0, F32)
            if a != 1:
                deg = deg - jnp.where(edge_rows[a], 1.0, 0.0)
            if b != 1:
                deg = deg - jnp.where(edge_cols[b], 1.0, 0.0)
            for wr, dr_, coef in ((w0, d0, 1.0), (w1, d1, 0.5)):
                if coef == 0.5 and (a == 1 or b == 1):
                    continue
                dr_[3 * a + b] = coef * deg
                wr[3 * a + b] = inside * (OMEGA / (SCREEN + coef * deg))
    xs[...] = jnp.zeros_like(xs)
    fields = (lum, selx, sely)
    for field in fields:
        for i in range(16):
            field[i, pl.ds(QR, 8), pl.ds(0, QC)] = jnp.zeros((8, QC), F32)
            field[i, :, pl.ds(QC, 128)] = jnp.zeros((ER, 128), F32)

    lane8 = lax.broadcasted_iota(jnp.int32, (8, 128), 1)
    sub8 = lax.broadcasted_iota(jnp.int32, (8, 128), 0)
    for i in range(H0 // CH):
        for one in loads[i]:
            one.wait()

        def select(s, carry, i=i):
            row = pl.multiple_of(i * CH + s * 8, 8)
            rows = pl.ds(row, 8)
            last_row = (r == NR - 1) & (sub8 + row == H0 - 1)
            for t in range(4):
                cols = pl.ds(t * 128, 128)
                lb = lab[rows, cols]
                is0, is1, is2 = lb == 0, lb == 1, lb == 2

                def pick(g):
                    return jnp.where(is0, g[0, rows, cols], jnp.where(
                        is1, g[1, rows, cols], jnp.where(is2, g[2, rows, cols], g[3, rows, cols])))

                sx, sy = pick(gx), pick(gy)
                if t == 3:
                    sx = jnp.where((c == NC - 1) & (lane8 == 127), 0.0, sx)
                raw[1, t, rows, :] = sx
                raw[2, t, rows, :] = jnp.where(last_row, 0.0, sy)
            return carry

        lax.fori_loop(0, CH // 8, select, 0, unroll=2)
    for one in consts:
        one.start()

    def by_phase(a, rows):
        return jnp.concatenate([raw[a, t, rows, :] for t in range(4)], axis=1)

    for a in range(3):
        x = jnp.concatenate([by_phase(a, pl.ds(rp, QR, stride=4)) for rp in range(4)], axis=0)
        y = permuted(x, perm[...])
        for rp in range(4):
            for pc in range(4):
                fields[a][rp * 4 + pc, pl.ds(0, QR), pl.ds(0, 128)] = y[rp * QR:(rp + 1) * QR, pc * 128:(pc + 1) * 128]

    def down():
        for pr in range(4):
            for pc in range(4):
                i = pr * 4 + pc
                left = selx[i - 1] if pc > 0 else roll(selx[pr * 4 + 3], 1, 1)
                up = sely[i - 4] if pr > 0 else roll(sely[12 + pc], 1, 0)
                rhs[i] = SCREEN * lum[i] + (left - selx[i]) + (up - sely[i])
        sweep(lum, fa, rhs, w0, 4, 1.0)
        sweep(fa, fb, rhs, w0, 4, 1.0)
        for a in range(2):
            for b in range(2):
                total = None
                for pr in (2 * a, 2 * a + 1):
                    for pc in (2 * b, 2 * b + 1):
                        i = pr * 4 + pc
                        res = (rhs[i] - SCREEN * fb[i]) + (around(fb, pr, pc, 4) - d0[which(pr, pc, 4)] * fb[i])
                        total = res if total is None else total + res
                f1[a * 2 + b] = 0.25 * total
                ea[a * 2 + b] = w1[which(a, b, 2)] * (0.25 * total)
        sweep(ea, eb, f1, w1, 2, 0.5)

    down()
    total = None
    for a in range(2):
        for b in range(2):
            i = a * 2 + b
            res = (f1[i] - SCREEN * eb[i]) + (0.5 * around(eb, a, b, 2) - d1[which(a, b, 2)] * eb[i])
            total = res if total is None else total + res
    total = (0.25 * total) * inside
    turned = jnp.concatenate([total[:, QC:EC], jnp.zeros((128 - ER, 128), F32)], axis=0).T
    strip[r] = jnp.concatenate([total[:, 0:QC], jnp.where(sub8 < 4, turned[0:8], turned[120:128])], axis=0)

    pl.semaphore_wait(barrier, len(peers))

    def send(src, dst, send_sem, recv_sem, device):
        copy = pltpu.make_async_remote_copy(
            src_ref=src, dst_ref=dst, send_sem=send_sem, recv_sem=recv_sem,
            device_id=device, device_id_type=MESH,
        )
        copy.start()
        return copy

    far = [
        send(strip.at[r], strip.at[r], r_send.at[i], r_recv.at[i], (row_peer(d), c)) for i, d in enumerate((4, 2, 6))
    ]
    near = [send(strip.at[r], strip.at[r], r_send.at[3], r_recv.at[3], (sibling, c))]

    lane = lax.broadcasted_iota(jnp.int32, (QR, 128), 1)
    group = lane // 16
    for tile in range(2):
        packed_r = jnp.zeros((QR, 128), F32)
        packed_l = jnp.zeros((QR, 128), F32)
        for g in range(8):
            idx = tile * 8 + g
            if idx >= 12:
                break
            a, rp = divmod(idx, 4)
            edge = raw[a, 3, pl.ds(rp, QR, stride=4), :]
            packed_r = jnp.where(group == g, roll(edge, 16 * g - 112, 1), packed_r)
            edge = raw[a, 0, pl.ds(rp, QR, stride=4), :]
            packed_l = jnp.where(group == g, roll(edge, 16 * g, 1), packed_l)
        to_right[:, pl.ds(tile * 128, 128)] = packed_r
        to_left[:, pl.ds(tile * 128, 128)] = packed_l
    top, bottom = pl.ds(0, 16), pl.ds(H0 - 16, 16)
    body, lo, hi = pl.ds(0, QR), pl.ds(0, 8), pl.ds(QR - 8, 8)
    below, above = pl.ds(QR, 8), pl.ds(QR + 8, 8)
    halo = [
        send(src, dst, h_send.at[i], h_recv.at[i], (row_peer(dr), col_peer(dc)))
        for i, (src, dst, dr, dc) in enumerate([
            (to_right.at[hi], from_l.at[above], 1, 1),
            (to_left.at[hi], from_r.at[above], 1, -1),
            (to_right.at[lo], from_l.at[below], -1, 1),
            (to_left.at[lo], from_r.at[below], -1, -1),
            (to_right, from_l.at[body], 0, 1),
            (to_left, from_r.at[body], 0, -1),
            (raw.at[:, :, bottom], raw.at[:, :, pl.ds(H0 + 16, 16)], 1, 0),
            (raw.at[:, :, top], raw.at[:, :, pl.ds(H0, 16)], -1, 0),
        ])
    ]

    for i, d in ((1, 2), (2, 6), (0, 4)):
        far[i].wait_recv()
        block = row_peer(-d)
        near.append(send(strip.at[block], strip.at[block], r_send.at[4 + i], r_recv.at[4 + i], (sibling, c)))
    for one in consts:
        one.wait()
    for copy in near:
        copy.wait()
    for copy in far:
        copy.wait_send()

    pieces = []
    for o in range(NR):
        first, last = strip[o, pl.ds(0, 8), :], strip[o, pl.ds(QR - 8, 8), :]
        if o > 0:
            first = first + jnp.where(sub8 < 2, strip[o - 1, pl.ds(QR, 8), :], 0.0)
        if o < NR - 1:
            last = last + jnp.where(sub8 >= 6, strip[o + 1, pl.ds(QR, 8), :], 0.0)
        pieces += [first, strip[o, pl.ds(8, QR - 16), :], last]
    whole = jnp.concatenate(pieces, axis=0)
    beside = [strip[o, pl.ds(ER, 8), :] for o in range(NR)]
    pieces = []
    for t in range(4):
        even, odd = beside[2 * t], beside[2 * t + 1]
        x = jnp.where(lane8 < 66, even, 0.0) + jnp.where(lane8 >= 64, roll(odd, 64, 1), 0.0)
        x = x + jnp.where((lane8 >= 62) & (lane8 < 64), roll(odd, -8, 1), 0.0)
        if t < 3:
            x = x + jnp.where(lane8 >= 126, roll(beside[2 * t + 2], 56, 1), 0.0)
        if t > 0:
            x = x + jnp.where(lane8 < 2, roll(beside[2 * t - 1], 64, 1), 0.0)
        pieces.append(x)
    xt = jnp.concatenate([whole.T, jnp.concatenate(pieces, axis=1), jnp.zeros((8, NR * QR), F32)], axis=0)

    xh, xm, xl = split3(xt)
    inner = pl.ds(16, NR * QR)
    ch, cm, cl = ct[0, inner, :], ct[1, inner, :], ct[2, inner, :]
    g = mm(xh, ch) + ((mm(xh, cm) + mm(xm, ch)) + (mm(xm, cm) + (mm(xh, cl) + mm(xl, ch))))
    r1, r2, l2, l1 = (g[QC + i:QC + i + 1] for i in (0, 1, 6, 7))
    g = g[0:QC]

    def small(i):
        return tab[pl.ds(2 * QC + i, 1), :]

    jrow = lax.broadcasted_iota(jnp.int32, (QC, NR * QR), 0)
    fwd, bwd = g, g
    for i, s in enumerate((1, 2, 4, 8, 16, 32, 64)):
        p = small(i)
        fwd = fwd + jnp.where(jrow >= s, roll(fwd, s, 0) * p, 0.0)
        bwd = bwd + jnp.where(jrow < QC - s, roll(bwd, -s, 0) * p, 0.0)
    end, start = fwd[QC - 1:QC], bwd[0:1]
    to_r = end + (small(11) * l1 + small(9) * l2) + (small(12) * r1 + small(13) * r2)
    to_l = start + (small(11) * r1 + small(9) * r2) + (small(12) * l1 + small(13) * l2)
    none = jnp.zeros((1, NR * QR), F32)
    lines = [g[QC - 1:QC], r1, r2, none, to_r, to_l, g[0:1], l1, l2, none]
    mom[c] = jnp.concatenate([x[:, t * 128:(t + 1) * 128] for x in lines for t in range(4)], axis=0)

    copies = []
    for d in range(1, NC):
        part = pl.ds(0, 24) if d == 1 else pl.ds(16, 24) if d == NC - 1 else pl.ds(16, 8)
        copies.append(send(mom.at[c, part], mom.at[c, part], c_send.at[d], c_recv.at[d], (r, col_peer(d))))

    own = small(7) * (fwd + bwd - g)
    near_a = small(7) * (l1 + small(0) * l2)
    near_b = small(7) * (r1 + small(0) * r2)

    for copy in halo:
        copy.wait()
    x = jnp.concatenate([by_phase(a, pl.ds(H0 + rp, 8, stride=4)) for a in range(3) for rp in range(4)], axis=0)
    y = permuted(x, perm[...])
    for a in range(3):
        for rp in range(4):
            i = (a * 4 + rp) * 8
            for pc in range(4):
                fields[a][rp * 4 + pc, pl.ds(QR, 8), pl.ds(0, 128)] = y[i:i + 8, pc * 128:(pc + 1) * 128]
    low8 = sub8 < 4
    lane_e = lax.broadcasted_iota(jnp.int32, (ER, 128), 1)

    def from_side(ref, tile):
        cols = pl.ds(tile * 128, 128)
        return jnp.concatenate(
            [ref[body, cols], jnp.where(low8, ref[below, cols], ref[above, cols])], axis=0
        )

    for a in range(3):
        pieces = []
        for rp in range(4):
            tile, gi = divmod(a * 4 + rp, 8)
            side_l, side_r = from_side(from_l, tile), from_side(from_r, tile)
            pieces.append(jnp.where(lane_e < 64, roll(side_r, -16 * gi, 1), roll(side_l, 112 - 16 * gi, 1)))
        y = permuted(jnp.concatenate(pieces, axis=0), side[...])
        for rp in range(4):
            for pc in range(4):
                fields[a][rp * 4 + pc, :, pl.ds(128, 128)] = y[rp * ER:(rp + 1) * ER, pc * 128:(pc + 1) * 128]
    for i in range(16):
        lum[i] = lum[i] * inside
        if i % 4 == 3:
            selx[i] = selx[i] * inside
        if i // 4 == 3:
            sely[i] = sely[i] * inside
    down()

    for copy in copies:
        copy.wait()

    low = lax.broadcasted_iota(jnp.int32, (8, 128), 0) < 4
    sum_a = jnp.zeros((8, 128), F32)
    sum_b = jnp.zeros((8, 128), F32)
    for o in range(NC):
        m = mom[o, pl.ds(16, 8), :]
        sum_a = sum_a + m * jnp.where(low, dist[lax.rem(c - o + 63, 32)], dist[c + o])
        sum_b = sum_b + m * jnp.where(low, dist[lax.rem(62 - c - o, 32)], dist[lax.rem(o - c + 63, 32)])

    def as_row(x):
        x = x[0:4] + x[4:8]
        return jnp.concatenate([x[t:t + 1] for t in range(4)], axis=1)

    left_m, right_m = mom[col_peer(-1), pl.ds(0, 16), :], mom[col_peer(1), pl.ds(24, 16), :]

    def line(m, i):
        return jnp.concatenate([m[4 * i + t:4 * i + t + 1] for t in range(4)], axis=1)

    a_in, b_in = as_row(sum_a) + near_a, as_row(sum_b) + near_b
    own = own + tab[pl.ds(0, QC), :] * a_in + tab[pl.ds(QC, QC), :] * b_in
    x0 = own[0:1] - 4.0 * line(left_m, 2)
    x127 = own[QC - 1:QC] - 4.0 * line(right_m, 2)
    xs[pl.ds(0, QC), :] = own
    xs[pl.ds(0, 1), :] = x0
    xs[pl.ds(QC - 1, 1), :] = x127
    left1 = a_in + small(8) * start + small(9) * b_in - 4.0 * (line(left_m, 1) + small(10) * line(left_m, 2))
    right1 = b_in + small(8) * end + small(9) * a_in - 4.0 * (line(right_m, 1) + small(10) * line(right_m, 2))
    left2 = small(10) * left1 - x0 - 4.0 * (l1 + line(left_m, 0))
    right2 = small(10) * right1 - x127 - 4.0 * (r1 + line(right_m, 0))
    zero6 = jnp.zeros((6, NR * QR), F32)
    xs[pl.ds(QC, 8), :] = jnp.concatenate([right1, right2, zero6], axis=0)
    xs[pl.ds(EC - 8, 8), :] = jnp.concatenate([zero6, left2, left1], axis=0)

    base = pl.multiple_of(r * QR, QR)
    sub16 = lax.broadcasted_iota(jnp.int32, (16, NR * QR), 0)
    back = []
    for i in range(3):
        tail = jnp.where(
            sub16 < 8,
            ct[i, pl.ds(base + QR + 16, 16), :].astype(F32),
            ct[i, pl.ds(base, 16), :].astype(F32),
        ).astype(BF)
        back.append(jnp.concatenate([ct[i, pl.ds(base + 16, QR), :], tail], axis=0))
    th, tm, tl = back
    xh, xm, xl = split3(xs[...])
    nt = ((1,), (1,))
    e2 = mm(th, xh, nt) + ((mm(th, xm, nt) + mm(tm, xh, nt)) + (mm(tm, xm, nt) + (mm(th, xl, nt) + mm(tl, xh, nt))))
    sub8 = lax.broadcasted_iota(jnp.int32, (8, EC), 0)
    e2 = jnp.concatenate([e2[0:QR], jnp.where(sub8 < 4, e2[QR:QR + 8], e2[QR + 8:QR + 16])], axis=0)
    e2 = e2 * inside

    for i in range(4):
        ea[i] = eb[i] + e2
    sweep(ea, ec, f1, w1, 2, 0.5)
    sweep(ec, ea, f1, w1, 2, 0.5)
    for pr in range(4):
        for pc in range(4):
            fa[pr * 4 + pc] = fb[pr * 4 + pc] + ea[(pr // 2) * 2 + pc // 2]
    sweep(fa, lum, rhs, w0, 4, 1.0)
    sweep(lum, fb, rhs, w0, 4, 1.0)
    x = jnp.concatenate([
        jnp.concatenate([fb[pr * 4 + pc, pl.ds(0, QR), pl.ds(0, QC)] for pc in range(4)], axis=1)
        for pr in range(4)
    ], axis=0)
    y = permuted(x, permt[...])
    for pr in range(4):
        for t in range(4):
            out[t, pl.ds(pr, QR, stride=4), :] = y[pr * QR:(pr + 1) * QR, t * 128:(t + 1) * 128]
    copies = [
        pltpu.make_async_copy(out.at[t], out_h.at[:, pl.ds(t * 128, 128)], out_sem.at[t]) for t in range(4)
    ]
    for copy in copies:
        copy.start()
    for copy in copies:
        copy.wait()


def shards(luminance, grad_x, grad_y, labels):
    consts = tables()
    vmem = pltpu.VMEM
    phases = vmem((16, ER, EC), F32)
    quarter = vmem((4, ER, EC), F32)
    nine = vmem((9, ER, EC), F32)
    dma = pltpu.SemaphoreType.DMA
    return pl.pallas_call(
        kernel,
        out_shape=jax.ShapeDtypeStruct((H0, W0), F32),
        in_specs=[pl.BlockSpec(memory_space=pl.ANY)] * 7,
        out_specs=pl.BlockSpec(memory_space=pl.ANY),
        scratch_shapes=[
            vmem((4, H0, W0), F32),
            vmem((4, H0, W0), F32),
            vmem((H0, W0), jnp.int32),
            vmem((3, 4, H0 + 32, 128), F32),
            vmem((W0, W0), BF),
            vmem((W0, W0), BF),
            vmem((128, W0), BF),
            vmem(consts[0].shape, BF),
            vmem(consts[1].shape, F32),
            vmem(consts[2].shape, F32),
            vmem((QR, 256), F32),
            vmem((QR, 256), F32),
            vmem((QR + 16, 256), F32),
            vmem((QR + 16, 256), F32),
            phases, phases, phases, phases, phases, phases,
            nine, nine, nine, nine,
            quarter, quarter, quarter, quarter,
            vmem((NR, ER + 8, QC), F32),
            vmem((NC, 40, 128), F32),
            vmem((EC, NR * QR), F32),
            vmem((4, H0, 128), F32),
            dma((4, 7)),
            dma((3,)),
            dma((4,)),
            dma((8,)),
            dma((8,)),
            dma((NR,)),
            dma((NR,)),
            dma((NC,)),
            dma((NC,)),
        ],
        compiler_params=pltpu.CompilerParams(
            collective_id=0, has_side_effects=True, vmem_limit_bytes=56 * 1024 * 1024
        ),
    )(luminance, grad_x, grad_y, labels, *[jnp.asarray(x) for x in consts])


def solution(mesh):
    return jax.shard_map(
        shards,
        mesh=mesh,
        in_specs=(
            P("rows", "cols"),
            P(None, "rows", "cols"),
            P(None, "rows", "cols"),
            P("rows", "cols"),
        ),
        out_specs=P("rows", "cols"),
        check_vma=False,
    )
```

```python
import functools
import math

import jax
import jax.numpy as jnp
import ml_dtypes
import numpy as np
from jax import lax
from jax.experimental import pallas as pl
from jax.experimental.pallas import tpu as pltpu
from jax.sharding import PartitionSpec as P

MESH = pl.DeviceIdType.MESH
SCREEN = 4e-06
OMEGA = 0.8
NR, NC = 8, 16
H0, W0 = 256, 512
QR, QC = 64, 128
ER, EC = 72, 256
BF, F32 = jnp.bfloat16, jnp.float32


def bf16_parts(x, parts):
    out = []
    rest = np.asarray(x, np.float64)
    for _ in range(parts):
        piece = rest.astype(ml_dtypes.bfloat16)
        out.append(piece)
        rest = rest - piece.astype(np.float64)
    return out


@functools.lru_cache(maxsize=None)
def tables():
    rows, cols = NR * QR, NC * QC
    k = np.arange(rows)
    place = np.arange(rows)
    phase = ((2 * place[:, None] + 1) * k[None, :]) % (4 * rows)
    scale = np.where(k == 0, math.sqrt(1.0 / rows), math.sqrt(2.0 / rows))
    ct = np.zeros((rows + 32, rows))
    ct[16:-16] = scale[None, :] * np.cos(phase * (math.pi / (2 * rows)))
    ct[:16] = ct[31:15:-1]
    ct[-16:] = ct[-17:-33:-1]
    ct = np.stack(bf16_parts(ct, 3))
    mu = SCREEN + 0.25 * 4 * np.sin(np.pi * k / (2 * rows)) ** 2
    half = 1 + 2 * mu
    rho = half - np.sqrt(4 * mu + 4 * mu * mu)
    g0 = 1 / (0.25 * (1 / rho - rho))
    t = np.arange(QC)
    from_left = rho[None, :] ** (t[:, None] + 1)
    from_right = rho[None, :] ** (QC - t[:, None])
    small = np.zeros((16, rows))
    for i in range(7):
        small[i] = rho ** (2**i)
    small[7] = g0
    small[8] = g0 * rho
    small[9] = rho ** (QC + 1)
    small[10] = 2 + 4 * mu
    small[11] = rho**QC
    small[12] = 1 / rho
    small[13] = rho**-2.0
    tab = np.concatenate([from_left, from_right, small]).astype(np.float32)
    dist = g0 / (1 - rho ** (2 * cols)) * rho ** (QC * np.arange(32)[:, None])
    dist = dist.reshape(32, 4, 128)
    dist = np.concatenate([dist, dist], axis=1).astype(np.float32)
    return ct, tab, dist


def split2(x):
    hi = x.astype(BF)
    return hi, (x - hi.astype(F32)).astype(BF)


def split3(x):
    hi = x.astype(BF)
    rest = x - hi.astype(F32)
    mid = rest.astype(BF)
    return hi, mid, (rest - mid.astype(F32)).astype(BF)


def mm(a, b, dims=((1,), (0,))):
    return lax.dot_general(a, b, (dims, ((), ())), preferred_element_type=F32)


def permuted(x, table):
    hi, mid = split2(x)
    return mm(hi, table) + mm(mid, table)


def roll(x, shift, axis):
    return pltpu.roll(x, shift % x.shape[axis], axis)


def around(ref, pr, pc, n):
    up = ref[(pr - 1) * n + pc] if pr > 0 else roll(ref[(n - 1) * n + pc], 1, 0)
    down = ref[(pr + 1) * n + pc] if pr < n - 1 else roll(ref[pc], -1, 0)
    left = ref[pr * n + pc - 1] if pc > 0 else roll(ref[pr * n + n - 1], 1, 1)
    right = ref[pr * n + pc + 1] if pc < n - 1 else roll(ref[pr * n], -1, 1)
    return (up + down) + (left + right)


def klass(p, n):
    return 0 if p == 0 else (2 if p == n - 1 else 1)


def which(pr, pc, n):
    return 3 * klass(pr, n) + klass(pc, n)


def sweep(src, dst, f, w, n, c):
    for pr in range(n):
        for pc in range(n):
            i = pr * n + pc
            nb = around(src, pr, pc, n)
            nb = nb if c == 1.0 else c * nb
            dst[i] = (1 - OMEGA) * src[i] + w[which(pr, pc, n)] * (f[i] + nb)


def distance(d):
    ring = (0, 1, 2, 1, 0)
    dy, dz = divmod(d, 4)
    return ring[dz] + ((4 - dz) * ring[dy] + dz * ring[dy + 1]) / 4


def kernel(
    lum_h, gx_h, gy_h, lab_h, ct_h, tab_h, dist_h,
    out_h,
    gx, gy, lab, raw, perm, permt, side, ct, tab, dist,
    to_right, to_left, from_l, from_r,
    lum, selx, sely, rhs, fa, fb, w0, d0, w1, d1, f1, ea, eb, ec,
    strip, share_m, mom, out,
    in_sem, const_sem, out_sem, h_send, h_recv, r_send, r_recv, m_send, m_recv, c_send, c_recv,
):
    r = lax.axis_index("rows")
    c = lax.axis_index("cols")

    def row_peer(d):
        return lax.rem(r + d + NR, NR)

    def col_peer(d):
        return lax.rem(c + d + NC, NC)

    sibling = r + 1 - 2 * lax.rem(r, 2)
    barrier = pltpu.get_barrier_semaphore()
    row_order = (4, 3, 5, 2, 6, 1, 7)
    col_order = sorted(range(1, NC), key=lambda d: -distance(d))
    peers = [(0, d) for d in col_order] + [(1, 1), (1, -1), (-1, 1), (-1, -1)] + [(d, 0) for d in row_order]
    for dr, dc in peers:
        pl.semaphore_signal(
            barrier, inc=1, device_id=(row_peer(dr), col_peer(dc)), device_id_type=MESH
        )

    CH = 64
    loads = []
    for i in range(H0 // CH):
        rows = pl.ds(i * CH, CH)
        loads.append([
            pltpu.make_async_copy(gx_h.at[:, rows], gx.at[:, rows], in_sem.at[i, 0]),
            pltpu.make_async_copy(gy_h.at[:, rows], gy.at[:, rows], in_sem.at[i, 1]),
            pltpu.make_async_copy(lab_h.at[rows], lab.at[rows], in_sem.at[i, 2]),
        ] + [
            pltpu.make_async_copy(lum_h.at[rows, pl.ds(t * 128, 128)], raw.at[0, t, rows], in_sem.at[i, 3 + t])
            for t in range(4)
        ])
    for group in loads:
        for one in group:
            one.start()
    consts = [
        pltpu.make_async_copy(a, b, const_sem.at[i])
        for i, (a, b) in enumerate([(ct_h, ct), (tab_h, tab), (dist_h, dist)])
    ]

    src = lax.broadcasted_iota(jnp.int32, (W0, 128), 0)
    dst = 4 * lax.broadcasted_iota(jnp.int32, (W0, 128), 1)
    back_src = 4 * lax.broadcasted_iota(jnp.int32, (128, W0), 0)
    back_dst = lax.broadcasted_iota(jnp.int32, (128, W0), 1)
    src_s = lax.broadcasted_iota(jnp.int32, (128, 128), 0)
    lane_s = lax.broadcasted_iota(jnp.int32, (128, 128), 1)
    outer = (lane_s < 4) | (lane_s >= 124)
    for pc in range(4):
        part = pl.ds(pc * 128, 128)
        perm[:, part] = jnp.where(src == dst + pc, 1.0, 0.0).astype(BF)
        permt[part, :] = jnp.where(back_src + pc == back_dst, 1.0, 0.0).astype(BF)
        side[:, part] = jnp.where(outer & (src_s == lax.rem(4 * lane_s + pc, 128)), 1.0, 0.0).astype(BF)

    ri = lax.broadcasted_iota(jnp.int32, (ER, EC), 0)
    li = lax.broadcasted_iota(jnp.int32, (ER, EC), 1)
    out_rows = ((r == 0) & (ri >= 68)) | ((r == NR - 1) & (ri >= 64) & (ri < 68))
    out_cols = ((c == 0) & (li >= 192)) | ((c == NC - 1) & (li >= 128) & (li < 192))
    inside = jnp.where(out_rows | out_cols, 0.0, 1.0).astype(F32)
    edge_rows = [((r == 0) & (ri == 0)), None, ((r == NR - 1) & (ri == QR - 1))]
    edge_cols = [((c == 0) & (li == 0)), None, ((c == NC - 1) & (li == QC - 1))]
    for a in range(3):
        for b in range(3):
            deg = jnp.full((ER, EC), 4.0, F32)
            if a != 1:
                deg = deg - jnp.where(edge_rows[a], 1.0, 0.0)
            if b != 1:
                deg = deg - jnp.where(edge_cols[b], 1.0, 0.0)
            for wr, dr_, coef in ((w0, d0, 1.0), (w1, d1, 0.5)):
                if coef == 0.5 and (a == 1 or b == 1):
                    continue
                dr_[3 * a + b] = coef * deg
                wr[3 * a + b] = inside * (OMEGA / (SCREEN + coef * deg))
    fields = (lum, selx, sely)
    for field in fields:
        for i in range(16):
            field[i, pl.ds(QR, 8), pl.ds(0, QC)] = jnp.zeros((8, QC), F32)
            field[i, :, pl.ds(QC, 128)] = jnp.zeros((ER, 128), F32)

    lane8 = lax.broadcasted_iota(jnp.int32, (8, 128), 1)
    sub8 = lax.broadcasted_iota(jnp.int32, (8, 128), 0)
    for i in range(H0 // CH):
        for one in loads[i]:
            one.wait()

        def select(s, carry, i=i):
            row = pl.multiple_of(i * CH + s * 8, 8)
            rows = pl.ds(row, 8)
            last_row = (r == NR - 1) & (sub8 + row == H0 - 1)
            for t in range(4):
                cols = pl.ds(t * 128, 128)
                lb = lab[rows, cols]
                is0, is1, is2 = lb == 0, lb == 1, lb == 2

                def pick(g):
                    return jnp.where(is0, g[0, rows, cols], jnp.where(
                        is1, g[1, rows, cols], jnp.where(is2, g[2, rows, cols], g[3, rows, cols])))

                sx, sy = pick(gx), pick(gy)
                if t == 3:
                    sx = jnp.where((c == NC - 1) & (lane8 == 127), 0.0, sx)
                raw[1, t, rows, :] = sx
                raw[2, t, rows, :] = jnp.where(last_row, 0.0, sy)
            return carry

        lax.fori_loop(0, CH // 8, select, 0, unroll=2)
    for one in consts:
        one.start()

    def by_phase(a, rows):
        return jnp.concatenate([raw[a, t, rows, :] for t in range(4)], axis=1)

    for a in range(3):
        x = jnp.concatenate([by_phase(a, pl.ds(rp, QR, stride=4)) for rp in range(4)], axis=0)
        y = permuted(x, perm[...])
        for rp in range(4):
            for pc in range(4):
                fields[a][rp * 4 + pc, pl.ds(0, QR), pl.ds(0, 128)] = y[rp * QR:(rp + 1) * QR, pc * 128:(pc + 1) * 128]

    def down():
        for pr in range(4):
            for pc in range(4):
                i = pr * 4 + pc
                left = selx[i - 1] if pc > 0 else roll(selx[pr * 4 + 3], 1, 1)
                up = sely[i - 4] if pr > 0 else roll(sely[12 + pc], 1, 0)
                rhs[i] = SCREEN * lum[i] + (left - selx[i]) + (up - sely[i])
        sweep(lum, fa, rhs, w0, 4, 1.0)
        sweep(fa, fb, rhs, w0, 4, 1.0)
        for a in range(2):
            for b in range(2):
                total = None
                for pr in (2 * a, 2 * a + 1):
                    for pc in (2 * b, 2 * b + 1):
                        i = pr * 4 + pc
                        res = (rhs[i] - SCREEN * fb[i]) + (around(fb, pr, pc, 4) - d0[which(pr, pc, 4)] * fb[i])
                        total = res if total is None else total + res
                f1[a * 2 + b] = 0.25 * total
                ea[a * 2 + b] = w1[which(a, b, 2)] * (0.25 * total)
        sweep(ea, eb, f1, w1, 2, 0.5)

    def coarsest():
        total = None
        for a in range(2):
            for b in range(2):
                i = a * 2 + b
                res = (f1[i] - SCREEN * eb[i]) + (0.5 * around(eb, a, b, 2) - d1[which(a, b, 2)] * eb[i])
                total = res if total is None else total + res
        return 0.25 * total

    down()
    total = coarsest() * inside
    tail = total[QR:ER]
    tall = jnp.concatenate([
        total[0:QR],
        jnp.where(sub8[:, :1] < 4, tail, 0.0), jnp.where(sub8[:, :1] >= 4, tail, 0.0),
        jnp.zeros((48, EC), F32),
    ], axis=0)
    turned = tall[:, QC:EC].T
    beside = jnp.where(sub8 < 4, turned[0:8], turned[120:128])
    strip[r] = jnp.concatenate([total[:, 0:QC], beside], axis=0)
    own_t = jnp.concatenate([tall[:, 0:QC].T, beside, jnp.zeros((8, 128), F32)], axis=0)
    for one in consts:
        one.wait()

    def small(i):
        return tab[pl.ds(2 * QC + i, 1), :]

    def six(xs_, cs_, dims=((1,), (0,))):
        (xh, xm, xl), (ch, cm, cl) = xs_, cs_
        return mm(xh, ch, dims) + (
            (mm(xh, cm, dims) + mm(xm, ch, dims)) + (mm(xm, cm, dims) + (mm(xh, cl, dims) + mm(xl, ch, dims)))
        )

    base = pl.multiple_of(r * QR, QR)
    sub16 = lax.broadcasted_iota(jnp.int32, (16, NR * QR), 0)
    back = []
    for i in range(3):
        tail = jnp.where(
            sub16 < 8,
            ct[i, pl.ds(base + QR + 16, 16), :].astype(F32),
            ct[i, pl.ds(base, 16), :].astype(F32),
        ).astype(BF)
        back.append(jnp.concatenate([ct[i, pl.ds(base + 16, QR), :], tail], axis=0))
    pad = jnp.zeros((48, NR * QR), BF)
    share = six(split3(own_t), [jnp.concatenate([x, pad], axis=0) for x in back])
    r1, r2, l2, l1 = (share[QC + i:QC + i + 1] for i in (0, 1, 6, 7))
    share = share[0:QC]
    to_r = jnp.sum(share * tab[pl.ds(QC, QC), :], axis=0, keepdims=True)
    to_l = jnp.sum(share * tab[pl.ds(0, QC), :], axis=0, keepdims=True)
    to_r = small(12) * (to_r + r1 + small(12) * r2) + (small(11) * l1 + small(9) * l2)
    to_l = small(12) * (to_l + l1 + small(12) * l2) + (small(11) * r1 + small(9) * r2)
    def in_rows(xs_):
        return jnp.concatenate([x[:, t * 128:(t + 1) * 128] for x in xs_ for t in range(4)], axis=0)

    share_m[r] = in_rows([to_r, to_l, r2, l2])

    pl.semaphore_wait(barrier, len(peers))

    def send(src, dst, send_sem, recv_sem, device):
        copy = pltpu.make_async_remote_copy(
            src_ref=src, dst_ref=dst, send_sem=send_sem, recv_sem=recv_sem,
            device_id=device, device_id_type=MESH,
        )
        copy.start()
        return copy

    copies = [send(share_m.at[r], share_m.at[r], m_send.at[d], m_recv.at[d], (row_peer(d), c)) for d in row_order]

    far = [
        send(strip.at[r], strip.at[r], r_send.at[i], r_recv.at[i], (row_peer(d), c)) for i, d in enumerate((4, 2, 6))
    ]
    near = [send(strip.at[r], strip.at[r], r_send.at[3], r_recv.at[3], (sibling, c))]

    lane = lax.broadcasted_iota(jnp.int32, (QR, 128), 1)
    group = lane // 16
    for tile in range(2):
        packed_r = jnp.zeros((QR, 128), F32)
        packed_l = jnp.zeros((QR, 128), F32)
        for g in range(8):
            idx = tile * 8 + g
            if idx >= 12:
                break
            a, rp = divmod(idx, 4)
            edge = raw[a, 3, pl.ds(rp, QR, stride=4), :]
            packed_r = jnp.where(group == g, roll(edge, 16 * g - 112, 1), packed_r)
            edge = raw[a, 0, pl.ds(rp, QR, stride=4), :]
            packed_l = jnp.where(group == g, roll(edge, 16 * g, 1), packed_l)
        to_right[:, pl.ds(tile * 128, 128)] = packed_r
        to_left[:, pl.ds(tile * 128, 128)] = packed_l
    top, bottom = pl.ds(0, 16), pl.ds(H0 - 16, 16)
    body, lo, hi = pl.ds(0, QR), pl.ds(0, 8), pl.ds(QR - 8, 8)
    below, above = pl.ds(QR, 8), pl.ds(QR + 8, 8)
    halo = [
        send(src, dst, h_send.at[i], h_recv.at[i], (row_peer(dr), col_peer(dc)))
        for i, (src, dst, dr, dc) in enumerate([
            (to_right.at[hi], from_l.at[above], 1, 1),
            (to_left.at[hi], from_r.at[above], 1, -1),
            (to_right.at[lo], from_l.at[below], -1, 1),
            (to_left.at[lo], from_r.at[below], -1, -1),
            (to_right, from_l.at[body], 0, 1),
            (to_left, from_r.at[body], 0, -1),
            (raw.at[:, :, bottom], raw.at[:, :, pl.ds(H0 + 16, 16)], 1, 0),
            (raw.at[:, :, top], raw.at[:, :, pl.ds(H0, 16)], -1, 0),
        ])
    ]

    for copy in copies:
        copy.wait()
    m = share_m[...]
    mom[c] = ((m[0] + m[1]) + (m[2] + m[3])) + ((m[4] + m[5]) + (m[6] + m[7]))
    copies = []
    for d in col_order:
        block = mom.at[c, pl.ds(0, 16 if d in (1, NC - 1) else 8)]
        copies.append(send(block, block, c_send.at[d], c_recv.at[d], (r, col_peer(d))))

    for i, d in ((1, 2), (2, 6), (0, 4)):
        far[i].wait_recv()
        block = row_peer(-d)
        near.append(send(strip.at[block], strip.at[block], r_send.at[4 + i], r_recv.at[4 + i], (sibling, c)))
    for copy in near:
        copy.wait()
    for copy in far:
        copy.wait_send()

    pieces = []
    for o in range(NR):
        first, last = strip[o, pl.ds(0, 8), :], strip[o, pl.ds(QR - 8, 8), :]
        if o > 0:
            first = first + jnp.where(sub8 < 2, strip[o - 1, pl.ds(QR, 8), :], 0.0)
        if o < NR - 1:
            last = last + jnp.where(sub8 >= 6, strip[o + 1, pl.ds(QR, 8), :], 0.0)
        pieces += [first, strip[o, pl.ds(8, QR - 16), :], last]
    whole = jnp.concatenate(pieces, axis=0)
    beside = [strip[o, pl.ds(ER, 8), :] for o in range(NR)]
    pieces = []
    for t in range(4):
        even, odd = beside[2 * t], beside[2 * t + 1]
        x = jnp.where(lane8 < 66, even, 0.0) + jnp.where(lane8 >= 64, roll(odd, 64, 1), 0.0)
        x = x + jnp.where((lane8 >= 62) & (lane8 < 64), roll(odd, -16, 1), 0.0)
        if t < 3:
            x = x + jnp.where(lane8 >= 126, roll(beside[2 * t + 2], 48, 1), 0.0)
        if t > 0:
            x = x + jnp.where(lane8 < 2, roll(beside[2 * t - 1], 64, 1), 0.0)
        pieces.append(x)
    xt = jnp.concatenate([whole.T, jnp.concatenate(pieces, axis=1), jnp.zeros((8, NR * QR), F32)], axis=0)

    inner = pl.ds(16, NR * QR)
    g = six(split3(xt), [ct[i, inner, :] for i in range(3)])
    r1, r2, l2, l1 = (g[QC + i:QC + i + 1] for i in (0, 1, 6, 7))
    g = g[0:QC]

    jrow = lax.broadcasted_iota(jnp.int32, (QC, NR * QR), 0)
    fwd, bwd = g, g
    for i, s in enumerate((1, 2, 4, 8, 16, 32, 64)):
        p = small(i)
        fwd = fwd + jnp.where(jrow >= s, roll(fwd, s, 0) * p, 0.0)
        bwd = bwd + jnp.where(jrow < QC - s, roll(bwd, -s, 0) * p, 0.0)
    end, start = fwd[QC - 1:QC], bwd[0:1]
    own = small(7) * (fwd + bwd - g)
    near_a = small(7) * (l1 + small(0) * l2)
    near_b = small(7) * (r1 + small(0) * r2)
    for copy in halo:
        copy.wait()
    x = jnp.concatenate([by_phase(a, pl.ds(H0 + rp, 8, stride=4)) for a in range(3) for rp in range(4)], axis=0)
    y = permuted(x, perm[...])
    for a in range(3):
        for rp in range(4):
            i = (a * 4 + rp) * 8
            for pc in range(4):
                fields[a][rp * 4 + pc, pl.ds(QR, 8), pl.ds(0, 128)] = y[i:i + 8, pc * 128:(pc + 1) * 128]
    low8 = sub8 < 4
    lane_e = lax.broadcasted_iota(jnp.int32, (ER, 128), 1)

    def from_side(ref, tile):
        cols = pl.ds(tile * 128, 128)
        return jnp.concatenate(
            [ref[body, cols], jnp.where(low8, ref[below, cols], ref[above, cols])], axis=0
        )

    for a in range(3):
        pieces = []
        for rp in range(4):
            tile, gi = divmod(a * 4 + rp, 8)
            side_l, side_r = from_side(from_l, tile), from_side(from_r, tile)
            pieces.append(jnp.where(lane_e < 64, roll(side_r, -16 * gi, 1), roll(side_l, 112 - 16 * gi, 1)))
        y = permuted(jnp.concatenate(pieces, axis=0), side[...])
        for rp in range(4):
            for pc in range(4):
                fields[a][rp * 4 + pc, :, pl.ds(128, 128)] = y[rp * ER:(rp + 1) * ER, pc * 128:(pc + 1) * 128]
    for i in range(16):
        lum[i] = lum[i] * inside
        if i % 4 == 3:
            selx[i] = selx[i] * inside
        if i // 4 == 3:
            sely[i] = sely[i] * inside
    down()
    f2 = coarsest()
    f2 = jnp.concatenate([f2, f2[QR:ER]], axis=0)

    for copy in copies:
        copy.wait()
    low = sub8 < 4
    sum_a = jnp.zeros((8, 128), F32)
    sum_b = jnp.zeros((8, 128), F32)
    for o in range(NC):
        m = mom[o, pl.ds(0, 8), :]
        sum_a = sum_a + m * jnp.where(low, dist[lax.rem(c - o + 63, 32)], dist[c + o])
        sum_b = sum_b + m * jnp.where(low, dist[lax.rem(62 - c - o, 32)], dist[lax.rem(o - c + 63, 32)])

    def line(m, i):
        return jnp.concatenate([m[4 * i + t:4 * i + t + 1] for t in range(4)], axis=1)

    a_in = line(sum_a[0:4] + sum_a[4:8], 0) + near_a
    b_in = line(sum_b[0:4] + sum_b[4:8], 0) + near_b
    own = own + tab[pl.ds(0, QC), :] * a_in + tab[pl.ds(QC, QC), :] * b_in
    own = own - 4.0 * jnp.concatenate([
        line(mom[col_peer(-1), pl.ds(8, 8), :], 0), jnp.zeros((QC - 2, NR * QR), F32),
        line(mom[col_peer(1), pl.ds(8, 8), :], 1),
    ], axis=0)

    e2 = six(back, split3(own), ((1,), (1,)))

    lane = lax.broadcasted_iota(jnp.int32, (ER + 8, 128), 1)

    row = lax.broadcasted_iota(jnp.int32, (ER + 8, 128), 0)

    def beyond(inner, at, f):
        up = jnp.where((r == 0) & (row == 0), at, roll(at, 1, 0))
        down = jnp.where((r == NR - 1) & (row == QR - 1), at, roll(at, -1, 0))
        return 4.0 * ((1 + SCREEN) * at - f) - (up + down) - inner

    one = beyond(jnp.where(lane < 64, roll(e2, -1, 1), roll(e2, 1, 1)), e2, f2[:, 0:QC])
    side_f = f2[:, QC:EC]
    two = beyond(e2, one, jnp.where(lane < 64, roll(side_f, 1, 1), roll(side_f, -1, 1)))
    outer = jnp.where(lane == 0, roll(one, 1, 1), jnp.where(lane == 1, roll(two, 2, 1), 0.0))
    outer = jnp.where(lane == 127, roll(one, -1, 1), jnp.where(lane == 126, roll(two, -2, 1), outer))
    e2 = jnp.concatenate([e2, outer], axis=1)
    sub8 = lax.broadcasted_iota(jnp.int32, (8, EC), 0)
    e2 = jnp.concatenate([e2[0:QR], jnp.where(sub8 < 4, e2[QR:QR + 8], e2[QR + 8:QR + 16])], axis=0)
    e2 = e2 * inside

    for i in range(4):
        ea[i] = eb[i] + e2
    sweep(ea, ec, f1, w1, 2, 0.5)
    sweep(ec, ea, f1, w1, 2, 0.5)
    for pr in range(4):
        for pc in range(4):
            fa[pr * 4 + pc] = fb[pr * 4 + pc] + ea[(pr // 2) * 2 + pc // 2]
    sweep(fa, lum, rhs, w0, 4, 1.0)
    sweep(lum, fb, rhs, w0, 4, 1.0)
    x = jnp.concatenate([
        jnp.concatenate([fb[pr * 4 + pc, pl.ds(0, QR), pl.ds(0, QC)] for pc in range(4)], axis=1)
        for pr in range(4)
    ], axis=0)
    y = permuted(x, permt[...])
    for pr in range(4):
        for t in range(4):
            out[t, pl.ds(pr, QR, stride=4), :] = y[pr * QR:(pr + 1) * QR, t * 128:(t + 1) * 128]
    copies = [
        pltpu.make_async_copy(out.at[t], out_h.at[:, pl.ds(t * 128, 128)], out_sem.at[t]) for t in range(4)
    ]
    for copy in copies:
        copy.start()
    for copy in copies:
        copy.wait()


def shards(luminance, grad_x, grad_y, labels):
    consts = tables()
    vmem = pltpu.VMEM
    phases = vmem((16, ER, EC), F32)
    quarter = vmem((4, ER, EC), F32)
    nine = vmem((9, ER, EC), F32)
    dma = pltpu.SemaphoreType.DMA
    return pl.pallas_call(
        kernel,
        out_shape=jax.ShapeDtypeStruct((H0, W0), F32),
        in_specs=[pl.BlockSpec(memory_space=pl.ANY)] * 7,
        out_specs=pl.BlockSpec(memory_space=pl.ANY),
        scratch_shapes=[
            vmem((4, H0, W0), F32),
            vmem((4, H0, W0), F32),
            vmem((H0, W0), jnp.int32),
            vmem((3, 4, H0 + 32, 128), F32),
            vmem((W0, W0), BF),
            vmem((W0, W0), BF),
            vmem((128, W0), BF),
            vmem(consts[0].shape, BF),
            vmem(consts[1].shape, F32),
            vmem(consts[2].shape, F32),
            vmem((QR, 256), F32),
            vmem((QR, 256), F32),
            vmem((QR + 16, 256), F32),
            vmem((QR + 16, 256), F32),
            phases, phases, phases, phases, phases, phases,
            nine, nine, nine, nine,
            quarter, quarter, quarter, quarter,
            vmem((NR, ER + 8, QC), F32),
            vmem((NR, 16, 128), F32),
            vmem((NC, 16, 128), F32),
            vmem((4, H0, 128), F32),
            dma((4, 7)),
            dma((3,)),
            dma((4,)),
            dma((8,)),
            dma((8,)),
            dma((NR,)),
            dma((NR,)),
            dma((NR,)),
            dma((NR,)),
            dma((NC,)),
            dma((NC,)),
        ],
        compiler_params=pltpu.CompilerParams(
            collective_id=0, has_side_effects=True, vmem_limit_bytes=56 * 1024 * 1024
        ),
    )(luminance, grad_x, grad_y, labels, *[jnp.asarray(x) for x in consts])


def solution(mesh):
    return jax.shard_map(
        shards,
        mesh=mesh,
        in_specs=(
            P("rows", "cols"),
            P(None, "rows", "cols"),
            P(None, "rows", "cols"),
            P("rows", "cols"),
        ),
        out_specs=P("rows", "cols"),
        check_vma=False,
    )
```

```python
import functools
import math

import jax
import jax.numpy as jnp
import ml_dtypes
import numpy as np
from jax import lax
from jax.experimental import pallas as pl
from jax.experimental.pallas import tpu as pltpu
from jax.sharding import PartitionSpec as P

MESH = pl.DeviceIdType.MESH
SCREEN = 4e-06
OMEGA = 0.8
NR, NC = 8, 16
H0, W0 = 256, 512
QR, QC = 64, 128
ER, EC = 72, 256
BF, F32 = jnp.bfloat16, jnp.float32


def bf16_parts(x, parts):
    out = []
    rest = np.asarray(x, np.float64)
    for _ in range(parts):
        piece = rest.astype(ml_dtypes.bfloat16)
        out.append(piece)
        rest = rest - piece.astype(np.float64)
    return out


@functools.lru_cache(maxsize=None)
def tables():
    rows, cols = NR * QR, NC * QC
    k = np.arange(rows)
    place = np.arange(rows)
    phase = ((2 * place[:, None] + 1) * k[None, :]) % (4 * rows)
    scale = np.where(k == 0, math.sqrt(1.0 / rows), math.sqrt(2.0 / rows))
    ct = np.zeros((rows + 32, rows))
    ct[16:-16] = scale[None, :] * np.cos(phase * (math.pi / (2 * rows)))
    ct[:16] = ct[31:15:-1]
    ct[-16:] = ct[-17:-33:-1]
    ct = np.stack(bf16_parts(ct, 3))
    mu = SCREEN + 0.25 * 4 * np.sin(np.pi * k / (2 * rows)) ** 2
    half = 1 + 2 * mu
    rho = half - np.sqrt(4 * mu + 4 * mu * mu)
    g0 = 1 / (0.25 * (1 / rho - rho))
    t = np.arange(QC)
    from_left = rho[None, :] ** (t[:, None] + 1)
    from_right = rho[None, :] ** (QC - t[:, None])
    small = np.zeros((16, rows))
    for i in range(7):
        small[i] = rho ** (2**i)
    small[7] = g0
    small[8] = g0 * rho
    small[9] = rho ** (QC + 1)
    small[10] = 2 + 4 * mu
    small[11] = rho**QC
    small[12] = 1 / rho
    small[13] = rho**-2.0
    tab = np.concatenate([from_left, from_right, small]).astype(np.float32)
    dist = g0 / (1 - rho ** (2 * cols)) * rho ** (QC * np.arange(32)[:, None])
    dist = dist.reshape(32, 4, 128)
    dist = np.concatenate([dist, dist], axis=1).astype(np.float32)
    return ct, tab, dist


def split2(x):
    hi = x.astype(BF)
    return hi, (x - hi.astype(F32)).astype(BF)


def split3(x):
    hi = x.astype(BF)
    rest = x - hi.astype(F32)
    mid = rest.astype(BF)
    return hi, mid, (rest - mid.astype(F32)).astype(BF)


def mm(a, b, dims=((1,), (0,))):
    return lax.dot_general(a, b, (dims, ((), ())), preferred_element_type=F32)


def permuted(x, table):
    hi, mid = split2(x)
    return mm(hi, table) + mm(mid, table)


def roll(x, shift, axis):
    return pltpu.roll(x, shift % x.shape[axis], axis)


def around(ref, pr, pc, n):
    up = ref[(pr - 1) * n + pc] if pr > 0 else roll(ref[(n - 1) * n + pc], 1, 0)
    down = ref[(pr + 1) * n + pc] if pr < n - 1 else roll(ref[pc], -1, 0)
    left = ref[pr * n + pc - 1] if pc > 0 else roll(ref[pr * n + n - 1], 1, 1)
    right = ref[pr * n + pc + 1] if pc < n - 1 else roll(ref[pr * n], -1, 1)
    return (up + down) + (left + right)


def klass(p, n):
    return 0 if p == 0 else (2 if p == n - 1 else 1)


def which(pr, pc, n):
    return 3 * klass(pr, n) + klass(pc, n)


def sweep(src, dst, f, w, n, c):
    for pr in range(n):
        for pc in range(n):
            i = pr * n + pc
            nb = around(src, pr, pc, n)
            nb = nb if c == 1.0 else c * nb
            dst[i] = (1 - OMEGA) * src[i] + w[which(pr, pc, n)] * (f[i] + nb)


def distance(d):
    ring = (0, 1, 2, 1, 0)
    dy, dz = divmod(d, 4)
    return ring[dz] + ((4 - dz) * ring[dy] + dz * ring[dy + 1]) / 4


def kernel(
    lum_h, gx_h, gy_h, lab_h, ct_h, tab_h, dist_h,
    out_h,
    gx, gy, lab, raw, perm, permt, side, ct, tab, dist,
    to_right, to_left, from_l, from_r,
    lum, selx, sely, rhs, fa, fb, w0, d0, w1, d1, f1, ea, eb, ec,
    strip, share_m, mom, out,
    in_sem, const_sem, out_sem, h_send, h_recv, r_send, r_recv, m_send, m_recv, c_send, c_recv,
):
    r = lax.axis_index("rows")
    c = lax.axis_index("cols")

    def row_peer(d):
        return lax.rem(r + d + NR, NR)

    def col_peer(d):
        return lax.rem(c + d + NC, NC)

    sibling = r + 1 - 2 * lax.rem(r, 2)
    barrier = pltpu.get_barrier_semaphore()
    row_order = (4, 3, 5, 2, 6, 1, 7)
    col_order = sorted(range(1, NC), key=lambda d: -distance(d))
    peers = [(0, d) for d in col_order] + [(1, 1), (1, -1), (-1, 1), (-1, -1)] + [(d, 0) for d in row_order]
    for dr, dc in peers:
        pl.semaphore_signal(
            barrier, inc=1, device_id=(row_peer(dr), col_peer(dc)), device_id_type=MESH
        )

    CH = 64
    loads = []
    for i in range(H0 // CH):
        rows = pl.ds(i * CH, CH)
        loads.append([
            pltpu.make_async_copy(gx_h.at[:, rows], gx.at[:, rows], in_sem.at[i, 0]),
            pltpu.make_async_copy(gy_h.at[:, rows], gy.at[:, rows], in_sem.at[i, 1]),
            pltpu.make_async_copy(lab_h.at[rows], lab.at[rows], in_sem.at[i, 2]),
        ])
    lum_loads = [
        pltpu.make_async_copy(lum_h.at[:, pl.ds(t * 128, 128)], raw.at[0, t, pl.ds(0, H0)], in_sem.at[t, 3])
        for t in range(4)
    ]
    for one in lum_loads + [one for group in loads for one in group]:
        one.start()
    consts = [
        pltpu.make_async_copy(a, b, const_sem.at[i])
        for i, (a, b) in enumerate([(ct_h, ct), (tab_h, tab), (dist_h, dist)])
    ]

    src = lax.broadcasted_iota(jnp.int32, (W0, 128), 0)
    dst = 4 * lax.broadcasted_iota(jnp.int32, (W0, 128), 1)
    back_src = 4 * lax.broadcasted_iota(jnp.int32, (128, W0), 0)
    back_dst = lax.broadcasted_iota(jnp.int32, (128, W0), 1)
    src_s = lax.broadcasted_iota(jnp.int32, (128, 128), 0)
    lane_s = lax.broadcasted_iota(jnp.int32, (128, 128), 1)
    outer = (lane_s < 4) | (lane_s >= 124)
    for pc in range(4):
        part = pl.ds(pc * 128, 128)
        perm[:, part] = jnp.where(src == dst + pc, 1.0, 0.0).astype(BF)
        permt[part, :] = jnp.where(back_src + pc == back_dst, 1.0, 0.0).astype(BF)
        side[:, part] = jnp.where(outer & (src_s == lax.rem(4 * lane_s + pc, 128)), 1.0, 0.0).astype(BF)

    ri = lax.broadcasted_iota(jnp.int32, (ER, EC), 0)
    li = lax.broadcasted_iota(jnp.int32, (ER, EC), 1)
    out_rows = ((r == 0) & (ri >= 68)) | ((r == NR - 1) & (ri >= 64) & (ri < 68))
    out_cols = ((c == 0) & (li >= 192)) | ((c == NC - 1) & (li >= 128) & (li < 192))
    inside = jnp.where(out_rows | out_cols, 0.0, 1.0).astype(F32)
    edge_rows = [((r == 0) & (ri == 0)), None, ((r == NR - 1) & (ri == QR - 1))]
    edge_cols = [((c == 0) & (li == 0)), None, ((c == NC - 1) & (li == QC - 1))]
    for a in range(3):
        for b in range(3):
            deg = jnp.full((ER, EC), 4.0, F32)
            if a != 1:
                deg = deg - jnp.where(edge_rows[a], 1.0, 0.0)
            if b != 1:
                deg = deg - jnp.where(edge_cols[b], 1.0, 0.0)
            for wr, dr_, coef in ((w0, d0, 1.0), (w1, d1, 0.5)):
                if coef == 0.5 and (a == 1 or b == 1):
                    continue
                dr_[3 * a + b] = coef * deg
                wr[3 * a + b] = inside * (OMEGA / (SCREEN + coef * deg))
    fields = (lum, selx, sely)
    for field in fields:
        for i in range(16):
            field[i, pl.ds(QR, 8), pl.ds(0, QC)] = jnp.zeros((8, QC), F32)
            field[i, :, pl.ds(QC, 128)] = jnp.zeros((ER, 128), F32)

    def by_phase(a, rows):
        return jnp.concatenate([raw[a, t, rows, :] for t in range(4)], axis=1)

    def own_by_phase(a):
        x = jnp.concatenate([by_phase(a, pl.ds(rp, QR, stride=4)) for rp in range(4)], axis=0)
        y = permuted(x, perm[...])
        for rp in range(4):
            for pc in range(4):
                fields[a][rp * 4 + pc, pl.ds(0, QR), pl.ds(0, 128)] = y[rp * QR:(rp + 1) * QR, pc * 128:(pc + 1) * 128]

    for one in lum_loads:
        one.wait()
    own_by_phase(0)

    lane8 = lax.broadcasted_iota(jnp.int32, (8, 128), 1)
    sub8 = lax.broadcasted_iota(jnp.int32, (8, 128), 0)
    for i in range(H0 // CH):
        for one in loads[i]:
            one.wait()

        def select(s, carry, i=i):
            row = pl.multiple_of(i * CH + s * 8, 8)
            rows = pl.ds(row, 8)
            last_row = (r == NR - 1) & (sub8 + row == H0 - 1)
            for t in range(4):
                cols = pl.ds(t * 128, 128)
                lb = lab[rows, cols]
                is0, is1, is2 = lb == 0, lb == 1, lb == 2

                def pick(g):
                    return jnp.where(is0, g[0, rows, cols], jnp.where(
                        is1, g[1, rows, cols], jnp.where(is2, g[2, rows, cols], g[3, rows, cols])))

                sx, sy = pick(gx), pick(gy)
                if t == 3:
                    sx = jnp.where((c == NC - 1) & (lane8 == 127), 0.0, sx)
                raw[1, t, rows, :] = sx
                raw[2, t, rows, :] = jnp.where(last_row, 0.0, sy)
            return carry

        lax.fori_loop(0, CH // 8, select, 0, unroll=2)
    for one in consts:
        one.start()

    own_by_phase(1)
    own_by_phase(2)

    def down():
        for pr in range(4):
            for pc in range(4):
                i = pr * 4 + pc
                left = selx[i - 1] if pc > 0 else roll(selx[pr * 4 + 3], 1, 1)
                up = sely[i - 4] if pr > 0 else roll(sely[12 + pc], 1, 0)
                rhs[i] = SCREEN * lum[i] + (left - selx[i]) + (up - sely[i])
        sweep(lum, fa, rhs, w0, 4, 1.0)
        sweep(fa, fb, rhs, w0, 4, 1.0)
        for a in range(2):
            for b in range(2):
                total = None
                for pr in (2 * a, 2 * a + 1):
                    for pc in (2 * b, 2 * b + 1):
                        i = pr * 4 + pc
                        res = (rhs[i] - SCREEN * fb[i]) + (around(fb, pr, pc, 4) - d0[which(pr, pc, 4)] * fb[i])
                        total = res if total is None else total + res
                f1[a * 2 + b] = 0.25 * total
                ea[a * 2 + b] = w1[which(a, b, 2)] * (0.25 * total)
        sweep(ea, eb, f1, w1, 2, 0.5)

    def coarsest():
        total = None
        for a in range(2):
            for b in range(2):
                i = a * 2 + b
                res = (f1[i] - SCREEN * eb[i]) + (0.5 * around(eb, a, b, 2) - d1[which(a, b, 2)] * eb[i])
                total = res if total is None else total + res
        return 0.25 * total

    down()
    total = coarsest() * inside
    tail = total[QR:ER]
    tall = jnp.concatenate([
        total[0:QR],
        jnp.where(sub8[:, :1] < 4, tail, 0.0), jnp.where(sub8[:, :1] >= 4, tail, 0.0),
        jnp.zeros((48, EC), F32),
    ], axis=0)
    turned = tall[:, QC:EC].T
    beside = jnp.where(sub8 < 4, turned[0:8], turned[120:128])
    strip[r] = jnp.concatenate([total[:, 0:QC], beside], axis=0)
    own_t = jnp.concatenate([tall[:, 0:QC].T, beside, jnp.zeros((8, 128), F32)], axis=0)
    for one in consts:
        one.wait()

    def small(i):
        return tab[pl.ds(2 * QC + i, 1), :]

    def six(xs_, cs_, dims=((1,), (0,))):
        (xh, xm, xl), (ch, cm, cl) = xs_, cs_
        return mm(xh, ch, dims) + (
            (mm(xh, cm, dims) + mm(xm, ch, dims)) + (mm(xm, cm, dims) + (mm(xh, cl, dims) + mm(xl, ch, dims)))
        )

    base = pl.multiple_of(r * QR, QR)
    sub16 = lax.broadcasted_iota(jnp.int32, (16, NR * QR), 0)
    back = []
    for i in range(3):
        tail = jnp.where(
            sub16 < 8,
            ct[i, pl.ds(base + QR + 16, 16), :].astype(F32),
            ct[i, pl.ds(base, 16), :].astype(F32),
        ).astype(BF)
        back.append(jnp.concatenate([ct[i, pl.ds(base + 16, QR), :], tail], axis=0))
    pad = jnp.zeros((48, NR * QR), BF)
    share = six(split3(own_t), [jnp.concatenate([x, pad], axis=0) for x in back])
    r1, r2, l2, l1 = (share[QC + i:QC + i + 1] for i in (0, 1, 6, 7))
    share = share[0:QC]
    to_r = jnp.sum(share * tab[pl.ds(QC, QC), :], axis=0, keepdims=True)
    to_l = jnp.sum(share * tab[pl.ds(0, QC), :], axis=0, keepdims=True)
    to_r = small(12) * (to_r + r1 + small(12) * r2) + (small(11) * l1 + small(9) * l2)
    to_l = small(12) * (to_l + l1 + small(12) * l2) + (small(11) * r1 + small(9) * r2)
    def in_rows(xs_):
        return jnp.concatenate([x[:, t * 128:(t + 1) * 128] for x in xs_ for t in range(4)], axis=0)

    share_m[r] = in_rows([to_r, to_l, r2, l2])

    pl.semaphore_wait(barrier, len(peers))

    def send(src, dst, send_sem, recv_sem, device):
        copy = pltpu.make_async_remote_copy(
            src_ref=src, dst_ref=dst, send_sem=send_sem, recv_sem=recv_sem,
            device_id=device, device_id_type=MESH,
        )
        copy.start()
        return copy

    copies = [send(share_m.at[r], share_m.at[r], m_send.at[d], m_recv.at[d], (row_peer(d), c)) for d in row_order]

    far = [
        send(strip.at[r], strip.at[r], r_send.at[i], r_recv.at[i], (row_peer(d), c)) for i, d in enumerate((4, 2, 6))
    ]
    near = [send(strip.at[r], strip.at[r], r_send.at[3], r_recv.at[3], (sibling, c))]

    lane = lax.broadcasted_iota(jnp.int32, (QR, 128), 1)
    group = lane // 16
    for tile in range(2):
        packed_r = jnp.zeros((QR, 128), F32)
        packed_l = jnp.zeros((QR, 128), F32)
        for g in range(8):
            idx = tile * 8 + g
            if idx >= 12:
                break
            a, rp = divmod(idx, 4)
            edge = raw[a, 3, pl.ds(rp, QR, stride=4), :]
            packed_r = jnp.where(group == g, roll(edge, 16 * g - 112, 1), packed_r)
            edge = raw[a, 0, pl.ds(rp, QR, stride=4), :]
            packed_l = jnp.where(group == g, roll(edge, 16 * g, 1), packed_l)
        to_right[:, pl.ds(tile * 128, 128)] = packed_r
        to_left[:, pl.ds(tile * 128, 128)] = packed_l
    top, bottom = pl.ds(0, 16), pl.ds(H0 - 16, 16)
    body, lo, hi = pl.ds(0, QR), pl.ds(0, 8), pl.ds(QR - 8, 8)
    below, above = pl.ds(QR, 8), pl.ds(QR + 8, 8)
    halo = [
        send(src, dst, h_send.at[i], h_recv.at[i], (row_peer(dr), col_peer(dc)))
        for i, (src, dst, dr, dc) in enumerate([
            (to_right.at[hi], from_l.at[above], 1, 1),
            (to_left.at[hi], from_r.at[above], 1, -1),
            (to_right.at[lo], from_l.at[below], -1, 1),
            (to_left.at[lo], from_r.at[below], -1, -1),
            (to_right, from_l.at[body], 0, 1),
            (to_left, from_r.at[body], 0, -1),
            (raw.at[:, :, bottom], raw.at[:, :, pl.ds(H0 + 16, 16)], 1, 0),
            (raw.at[:, :, top], raw.at[:, :, pl.ds(H0, 16)], -1, 0),
        ])
    ]

    for copy in copies:
        copy.wait()
    m = share_m[...]
    mom[c] = ((m[0] + m[1]) + (m[2] + m[3])) + ((m[4] + m[5]) + (m[6] + m[7]))
    copies = []
    for d in col_order:
        block = mom.at[c, pl.ds(0, 16 if d in (1, NC - 1) else 8)]
        copies.append(send(block, block, c_send.at[d], c_recv.at[d], (r, col_peer(d))))

    for i, d in ((1, 2), (2, 6), (0, 4)):
        far[i].wait_recv()
        block = row_peer(-d)
        near.append(send(strip.at[block], strip.at[block], r_send.at[4 + i], r_recv.at[4 + i], (sibling, c)))
    for copy in near:
        copy.wait()
    for copy in far:
        copy.wait_send()

    pieces = []
    for o in range(NR):
        first, last = strip[o, pl.ds(0, 8), :], strip[o, pl.ds(QR - 8, 8), :]
        if o > 0:
            first = first + jnp.where(sub8 < 2, strip[o - 1, pl.ds(QR, 8), :], 0.0)
        if o < NR - 1:
            last = last + jnp.where(sub8 >= 6, strip[o + 1, pl.ds(QR, 8), :], 0.0)
        pieces += [first, strip[o, pl.ds(8, QR - 16), :], last]
    whole = jnp.concatenate(pieces, axis=0)
    beside = [strip[o, pl.ds(ER, 8), :] for o in range(NR)]
    pieces = []
    for t in range(4):
        even, odd = beside[2 * t], beside[2 * t + 1]
        x = jnp.where(lane8 < 66, even, 0.0) + jnp.where(lane8 >= 64, roll(odd, 64, 1), 0.0)
        x = x + jnp.where((lane8 >= 62) & (lane8 < 64), roll(odd, -16, 1), 0.0)
        if t < 3:
            x = x + jnp.where(lane8 >= 126, roll(beside[2 * t + 2], 48, 1), 0.0)
        if t > 0:
            x = x + jnp.where(lane8 < 2, roll(beside[2 * t - 1], 64, 1), 0.0)
        pieces.append(x)
    xt = jnp.concatenate([whole.T, jnp.concatenate(pieces, axis=1), jnp.zeros((8, NR * QR), F32)], axis=0)

    inner = pl.ds(16, NR * QR)
    g = six(split3(xt), [ct[i, inner, :] for i in range(3)])
    r1, r2, l2, l1 = (g[QC + i:QC + i + 1] for i in (0, 1, 6, 7))
    g = g[0:QC]

    jrow = lax.broadcasted_iota(jnp.int32, (QC, NR * QR), 0)
    fwd, bwd = g, g
    for i, s in enumerate((1, 2, 4, 8, 16, 32, 64)):
        p = small(i)
        fwd = fwd + jnp.where(jrow >= s, roll(fwd, s, 0) * p, 0.0)
        bwd = bwd + jnp.where(jrow < QC - s, roll(bwd, -s, 0) * p, 0.0)
    end, start = fwd[QC - 1:QC], bwd[0:1]
    own = small(7) * (fwd + bwd - g)
    near_a = small(7) * (l1 + small(0) * l2)
    near_b = small(7) * (r1 + small(0) * r2)
    for copy in halo:
        copy.wait()
    x = jnp.concatenate([by_phase(a, pl.ds(H0 + rp, 8, stride=4)) for a in range(3) for rp in range(4)], axis=0)
    y = permuted(x, perm[...])
    for a in range(3):
        for rp in range(4):
            i = (a * 4 + rp) * 8
            for pc in range(4):
                fields[a][rp * 4 + pc, pl.ds(QR, 8), pl.ds(0, 128)] = y[i:i + 8, pc * 128:(pc + 1) * 128]
    low8 = sub8 < 4
    lane_e = lax.broadcasted_iota(jnp.int32, (ER, 128), 1)

    def from_side(ref, tile):
        cols = pl.ds(tile * 128, 128)
        return jnp.concatenate(
            [ref[body, cols], jnp.where(low8, ref[below, cols], ref[above, cols])], axis=0
        )

    for a in range(3):
        pieces = []
        for rp in range(4):
            tile, gi = divmod(a * 4 + rp, 8)
            side_l, side_r = from_side(from_l, tile), from_side(from_r, tile)
            pieces.append(jnp.where(lane_e < 64, roll(side_r, -16 * gi, 1), roll(side_l, 112 - 16 * gi, 1)))
        y = permuted(jnp.concatenate(pieces, axis=0), side[...])
        for rp in range(4):
            for pc in range(4):
                fields[a][rp * 4 + pc, :, pl.ds(128, 128)] = y[rp * ER:(rp + 1) * ER, pc * 128:(pc + 1) * 128]
    for i in range(16):
        lum[i] = lum[i] * inside
        if i % 4 == 3:
            selx[i] = selx[i] * inside
        if i // 4 == 3:
            sely[i] = sely[i] * inside
    down()
    f2 = coarsest()
    f2 = jnp.concatenate([f2, f2[QR:ER]], axis=0)

    for copy in copies:
        copy.wait()
    low = sub8 < 4
    sum_a = jnp.zeros((8, 128), F32)
    sum_b = jnp.zeros((8, 128), F32)
    for o in range(NC):
        m = mom[o, pl.ds(0, 8), :]
        sum_a = sum_a + m * jnp.where(low, dist[lax.rem(c - o + 63, 32)], dist[c + o])
        sum_b = sum_b + m * jnp.where(low, dist[lax.rem(62 - c - o, 32)], dist[lax.rem(o - c + 63, 32)])

    def line(m, i):
        return jnp.concatenate([m[4 * i + t:4 * i + t + 1] for t in range(4)], axis=1)

    a_in = line(sum_a[0:4] + sum_a[4:8], 0) + near_a
    b_in = line(sum_b[0:4] + sum_b[4:8], 0) + near_b
    own = own + tab[pl.ds(0, QC), :] * a_in + tab[pl.ds(QC, QC), :] * b_in
    own = own - 4.0 * jnp.concatenate([
        line(mom[col_peer(-1), pl.ds(8, 8), :], 0), jnp.zeros((QC - 2, NR * QR), F32),
        line(mom[col_peer(1), pl.ds(8, 8), :], 1),
    ], axis=0)

    e2 = six(back, split3(own), ((1,), (1,)))

    lane = lax.broadcasted_iota(jnp.int32, (ER + 8, 128), 1)

    row = lax.broadcasted_iota(jnp.int32, (ER + 8, 128), 0)

    def beyond(inner, at, f):
        up = jnp.where((r == 0) & (row == 0), at, roll(at, 1, 0))
        down = jnp.where((r == NR - 1) & (row == QR - 1), at, roll(at, -1, 0))
        return 4.0 * ((1 + SCREEN) * at - f) - (up + down) - inner

    one = beyond(jnp.where(lane < 64, roll(e2, -1, 1), roll(e2, 1, 1)), e2, f2[:, 0:QC])
    side_f = f2[:, QC:EC]
    two = beyond(e2, one, jnp.where(lane < 64, roll(side_f, 1, 1), roll(side_f, -1, 1)))
    outer = jnp.where(lane == 0, roll(one, 1, 1), jnp.where(lane == 1, roll(two, 2, 1), 0.0))
    outer = jnp.where(lane == 127, roll(one, -1, 1), jnp.where(lane == 126, roll(two, -2, 1), outer))
    e2 = jnp.concatenate([e2, outer], axis=1)
    sub8 = lax.broadcasted_iota(jnp.int32, (8, EC), 0)
    e2 = jnp.concatenate([e2[0:QR], jnp.where(sub8 < 4, e2[QR:QR + 8], e2[QR + 8:QR + 16])], axis=0)
    e2 = e2 * inside

    for i in range(4):
        ea[i] = eb[i] + e2
    sweep(ea, ec, f1, w1, 2, 0.5)
    sweep(ec, ea, f1, w1, 2, 0.5)
    for pr in range(4):
        for pc in range(4):
            fa[pr * 4 + pc] = fb[pr * 4 + pc] + ea[(pr // 2) * 2 + pc // 2]
    sweep(fa, lum, rhs, w0, 4, 1.0)
    sweep(lum, fb, rhs, w0, 4, 1.0)
    x = jnp.concatenate([
        jnp.concatenate([fb[pr * 4 + pc, pl.ds(0, QR), pl.ds(0, QC)] for pc in range(4)], axis=1)
        for pr in range(4)
    ], axis=0)
    y = permuted(x, permt[...])
    for pr in range(4):
        for t in range(4):
            out[t, pl.ds(pr, QR, stride=4), :] = y[pr * QR:(pr + 1) * QR, t * 128:(t + 1) * 128]
    copies = [
        pltpu.make_async_copy(out.at[t], out_h.at[:, pl.ds(t * 128, 128)], out_sem.at[t]) for t in range(4)
    ]
    for copy in copies:
        copy.start()
    for copy in copies:
        copy.wait()


def shards(luminance, grad_x, grad_y, labels):
    consts = tables()
    vmem = pltpu.VMEM
    phases = vmem((16, ER, EC), F32)
    quarter = vmem((4, ER, EC), F32)
    nine = vmem((9, ER, EC), F32)
    dma = pltpu.SemaphoreType.DMA
    return pl.pallas_call(
        kernel,
        out_shape=jax.ShapeDtypeStruct((H0, W0), F32),
        in_specs=[pl.BlockSpec(memory_space=pl.ANY)] * 7,
        out_specs=pl.BlockSpec(memory_space=pl.ANY),
        scratch_shapes=[
            vmem((4, H0, W0), F32),
            vmem((4, H0, W0), F32),
            vmem((H0, W0), jnp.int32),
            vmem((3, 4, H0 + 32, 128), F32),
            vmem((W0, W0), BF),
            vmem((W0, W0), BF),
            vmem((128, W0), BF),
            vmem(consts[0].shape, BF),
            vmem(consts[1].shape, F32),
            vmem(consts[2].shape, F32),
            vmem((QR, 256), F32),
            vmem((QR, 256), F32),
            vmem((QR + 16, 256), F32),
            vmem((QR + 16, 256), F32),
            phases, phases, phases, phases, phases, phases,
            nine, nine, nine, nine,
            quarter, quarter, quarter, quarter,
            vmem((NR, ER + 8, QC), F32),
            vmem((NR, 16, 128), F32),
            vmem((NC, 16, 128), F32),
            vmem((4, H0, 128), F32),
            dma((4, 4)),
            dma((3,)),
            dma((4,)),
            dma((8,)),
            dma((8,)),
            dma((NR,)),
            dma((NR,)),
            dma((NR,)),
            dma((NR,)),
            dma((NC,)),
            dma((NC,)),
        ],
        compiler_params=pltpu.CompilerParams(
            collective_id=0, has_side_effects=True, vmem_limit_bytes=56 * 1024 * 1024
        ),
    )(luminance, grad_x, grad_y, labels, *[jnp.asarray(x) for x in consts])


def solution(mesh):
    return jax.shard_map(
        shards,
        mesh=mesh,
        in_specs=(
            P("rows", "cols"),
            P(None, "rows", "cols"),
            P(None, "rows", "cols"),
            P("rows", "cols"),
        ),
        out_specs=P("rows", "cols"),
        check_vma=False,
    )
```

```python
import functools
import math

import jax
import jax.numpy as jnp
import ml_dtypes
import numpy as np
from jax import lax
from jax.experimental import pallas as pl
from jax.experimental.pallas import tpu as pltpu
from jax.sharding import PartitionSpec as P

MESH = pl.DeviceIdType.MESH
SCREEN = 4e-06
OMEGA = 0.8
NR, NC = 8, 16
H0, W0 = 256, 512
QR, QC = 64, 128
ER, EC = 72, 256
BF, F32 = jnp.bfloat16, jnp.float32


def bf16_parts(x, parts):
    out = []
    rest = np.asarray(x, np.float64)
    for _ in range(parts):
        piece = rest.astype(ml_dtypes.bfloat16)
        out.append(piece)
        rest = rest - piece.astype(np.float64)
    return out


@functools.lru_cache(maxsize=None)
def tables():
    rows, cols = NR * QR, NC * QC
    k = np.arange(rows)
    place = np.arange(rows)
    phase = ((2 * place[:, None] + 1) * k[None, :]) % (4 * rows)
    scale = np.where(k == 0, math.sqrt(1.0 / rows), math.sqrt(2.0 / rows))
    ct = np.zeros((rows + 32, rows))
    ct[16:-16] = scale[None, :] * np.cos(phase * (math.pi / (2 * rows)))
    ct[:16] = ct[31:15:-1]
    ct[-16:] = ct[-17:-33:-1]
    ct = np.stack(bf16_parts(ct, 3))
    mu = SCREEN + 0.25 * 4 * np.sin(np.pi * k / (2 * rows)) ** 2
    half = 1 + 2 * mu
    rho = half - np.sqrt(4 * mu + 4 * mu * mu)
    g0 = 1 / (0.25 * (1 / rho - rho))
    t = np.arange(QC)
    from_left = rho[None, :] ** (t[:, None] + 1)
    from_right = rho[None, :] ** (QC - t[:, None])
    small = np.zeros((16, rows))
    for i in range(7):
        small[i] = rho ** (2**i)
    small[7] = g0
    small[8] = g0 * rho
    small[9] = rho ** (QC + 1)
    small[10] = 2 + 4 * mu
    small[11] = rho**QC
    small[12] = 1 / rho
    small[13] = rho**-2.0
    tab = np.concatenate([from_left, from_right, small]).astype(np.float32)
    dist = g0 / (1 - rho ** (2 * cols)) * rho ** (QC * np.arange(32)[:, None])
    dist = dist.reshape(32, 4, 128)
    dist = np.concatenate([dist, dist], axis=1).astype(np.float32)
    return ct, tab, dist


def split2(x):
    hi = x.astype(BF)
    return hi, (x - hi.astype(F32)).astype(BF)


def split3(x):
    hi = x.astype(BF)
    rest = x - hi.astype(F32)
    mid = rest.astype(BF)
    return hi, mid, (rest - mid.astype(F32)).astype(BF)


def mm(a, b, dims=((1,), (0,))):
    return lax.dot_general(a, b, (dims, ((), ())), preferred_element_type=F32)


def permuted(x, table):
    hi, mid = split2(x)
    return mm(hi, table) + mm(mid, table)


def roll(x, shift, axis):
    return pltpu.roll(x, shift % x.shape[axis], axis)


def around(ref, pr, pc, n):
    up = ref[(pr - 1) * n + pc] if pr > 0 else roll(ref[(n - 1) * n + pc], 1, 0)
    down = ref[(pr + 1) * n + pc] if pr < n - 1 else roll(ref[pc], -1, 0)
    left = ref[pr * n + pc - 1] if pc > 0 else roll(ref[pr * n + n - 1], 1, 1)
    right = ref[pr * n + pc + 1] if pc < n - 1 else roll(ref[pr * n], -1, 1)
    return (up + down) + (left + right)


def klass(p, n):
    return 0 if p == 0 else (2 if p == n - 1 else 1)


def which(pr, pc, n):
    return 3 * klass(pr, n) + klass(pc, n)


def sweep(src, dst, f, w, n, c):
    for pr in range(n):
        for pc in range(n):
            i = pr * n + pc
            nb = around(src, pr, pc, n)
            nb = nb if c == 1.0 else c * nb
            dst[i] = (1 - OMEGA) * src[i] + w[which(pr, pc, n)] * (f[i] + nb)


def distance(d):
    ring = (0, 1, 2, 1, 0)
    dy, dz = divmod(d, 4)
    return ring[dz] + ((4 - dz) * ring[dy] + dz * ring[dy + 1]) / 4


def last_sweep(src, dst, f, w):
    own = (pl.ds(0, QR), pl.ds(0, QC))

    def rolled(i, shift, axis):
        return roll(src[i], shift, axis)[0:QR, 0:QC]

    for pr in range(4):
        for pc in range(4):
            i = pr * 4 + pc
            up = src[(i - 4, *own)] if pr > 0 else rolled(12 + pc, 1, 0)
            down = src[(i + 4, *own)] if pr < 3 else rolled(pc, -1, 0)
            left = src[(i - 1, *own)] if pc > 0 else rolled(i + 3, 1, 1)
            right = src[(i + 1, *own)] if pc < 3 else rolled(i - 3, -1, 1)
            nb = (up + down) + (left + right)
            dst[(i, *own)] = (1 - OMEGA) * src[(i, *own)] + w[(which(pr, pc, 4), *own)] * (f[(i, *own)] + nb)


def kernel(
    lum_h, gx_h, gy_h, lab_h, ct_h, tab_h, dist_h,
    out_h,
    gx, gy, lab, raw, perm, permt, side, ct, tab, dist,
    to_right, to_left, from_l, from_r,
    lum, selx, sely, rhs, fa, fb, w0, d0, w1, d1, f1, ea, eb, ec,
    strip, share_m, mom, out,
    in_sem, const_sem, out_sem, h_send, h_recv, r_send, r_recv, m_send, m_recv, c_send, c_recv,
):
    r = lax.axis_index("rows")
    c = lax.axis_index("cols")

    def row_peer(d):
        return lax.rem(r + d + NR, NR)

    def col_peer(d):
        return lax.rem(c + d + NC, NC)

    sibling = r + 1 - 2 * lax.rem(r, 2)
    barrier = pltpu.get_barrier_semaphore()
    row_order = (4, 3, 5, 2, 6, 1, 7)
    col_order = sorted(range(1, NC), key=lambda d: -distance(d))
    peers = [(0, d) for d in col_order] + [(1, 1), (1, -1), (-1, 1), (-1, -1)] + [(d, 0) for d in row_order]
    for dr, dc in peers:
        pl.semaphore_signal(
            barrier, inc=1, device_id=(row_peer(dr), col_peer(dc)), device_id_type=MESH
        )

    CH = 64
    loads = []
    for i in range(H0 // CH):
        rows = pl.ds(i * CH, CH)
        loads.append([
            pltpu.make_async_copy(gx_h.at[:, rows], gx.at[:, rows], in_sem.at[i, 0]),
            pltpu.make_async_copy(gy_h.at[:, rows], gy.at[:, rows], in_sem.at[i, 1]),
            pltpu.make_async_copy(lab_h.at[rows], lab.at[rows], in_sem.at[i, 2]),
        ])
    lum_loads = [
        pltpu.make_async_copy(lum_h.at[:, pl.ds(t * 128, 128)], raw.at[0, t, pl.ds(0, H0)], in_sem.at[t, 3])
        for t in range(4)
    ]
    for one in lum_loads + [one for group in loads for one in group]:
        one.start()
    consts = [
        pltpu.make_async_copy(a, b, const_sem.at[i])
        for i, (a, b) in enumerate([(ct_h, ct), (tab_h, tab), (dist_h, dist)])
    ]

    src = lax.broadcasted_iota(jnp.int32, (W0, 128), 0)
    dst = 4 * lax.broadcasted_iota(jnp.int32, (W0, 128), 1)
    back_src = 4 * lax.broadcasted_iota(jnp.int32, (128, W0), 0)
    back_dst = lax.broadcasted_iota(jnp.int32, (128, W0), 1)
    src_s = lax.broadcasted_iota(jnp.int32, (128, 128), 0)
    lane_s = lax.broadcasted_iota(jnp.int32, (128, 128), 1)
    outer = (lane_s < 4) | (lane_s >= 124)
    for pc in range(4):
        part = pl.ds(pc * 128, 128)
        perm[:, part] = jnp.where(src == dst + pc, 1.0, 0.0).astype(BF)
        permt[part, :] = jnp.where(back_src + pc == back_dst, 1.0, 0.0).astype(BF)
        side[:, part] = jnp.where(outer & (src_s == lax.rem(4 * lane_s + pc, 128)), 1.0, 0.0).astype(BF)

    ri = lax.broadcasted_iota(jnp.int32, (ER, EC), 0)
    li = lax.broadcasted_iota(jnp.int32, (ER, EC), 1)
    out_rows = ((r == 0) & (ri >= 68)) | ((r == NR - 1) & (ri >= 64) & (ri < 68))
    out_cols = ((c == 0) & (li >= 192)) | ((c == NC - 1) & (li >= 128) & (li < 192))
    inside = jnp.where(out_rows | out_cols, 0.0, 1.0).astype(F32)
    edge_rows = [((r == 0) & (ri == 0)), None, ((r == NR - 1) & (ri == QR - 1))]
    edge_cols = [((c == 0) & (li == 0)), None, ((c == NC - 1) & (li == QC - 1))]
    for a in range(3):
        for b in range(3):
            deg = jnp.full((ER, EC), 4.0, F32)
            if a != 1:
                deg = deg - jnp.where(edge_rows[a], 1.0, 0.0)
            if b != 1:
                deg = deg - jnp.where(edge_cols[b], 1.0, 0.0)
            for wr, dr_, coef in ((w0, d0, 1.0), (w1, d1, 0.5)):
                if coef == 0.5 and (a == 1 or b == 1):
                    continue
                dr_[3 * a + b] = coef * deg
                wr[3 * a + b] = inside * (OMEGA / (SCREEN + coef * deg))
    fields = (lum, selx, sely)
    for field in fields:
        for i in range(16):
            field[i, pl.ds(QR, 8), pl.ds(0, QC)] = jnp.zeros((8, QC), F32)
            field[i, :, pl.ds(QC, 128)] = jnp.zeros((ER, 128), F32)

    def by_phase(a, rows):
        return jnp.concatenate([raw[a, t, rows, :] for t in range(4)], axis=1)

    def own_by_phase(a):
        x = jnp.concatenate([by_phase(a, pl.ds(rp, QR, stride=4)) for rp in range(4)], axis=0)
        y = permuted(x, perm[...])
        for rp in range(4):
            for pc in range(4):
                fields[a][rp * 4 + pc, pl.ds(0, QR), pl.ds(0, 128)] = y[rp * QR:(rp + 1) * QR, pc * 128:(pc + 1) * 128]

    for one in lum_loads:
        one.wait()
    own_by_phase(0)

    lane8 = lax.broadcasted_iota(jnp.int32, (8, 128), 1)
    sub8 = lax.broadcasted_iota(jnp.int32, (8, 128), 0)
    for i in range(H0 // CH):
        for one in loads[i]:
            one.wait()

        def select(s, carry, i=i):
            row = pl.multiple_of(i * CH + s * 8, 8)
            rows = pl.ds(row, 8)
            last_row = (r == NR - 1) & (sub8 + row == H0 - 1)
            for t in range(4):
                cols = pl.ds(t * 128, 128)
                lb = lab[rows, cols]
                is0, is1, is2 = lb == 0, lb == 1, lb == 2

                def pick(g):
                    return jnp.where(is0, g[0, rows, cols], jnp.where(
                        is1, g[1, rows, cols], jnp.where(is2, g[2, rows, cols], g[3, rows, cols])))

                sx, sy = pick(gx), pick(gy)
                if t == 3:
                    sx = jnp.where((c == NC - 1) & (lane8 == 127), 0.0, sx)
                raw[1, t, rows, :] = sx
                raw[2, t, rows, :] = jnp.where(last_row, 0.0, sy)
            return carry

        lax.fori_loop(0, CH // 8, select, 0, unroll=2)
    for one in consts:
        one.start()

    own_by_phase(1)
    own_by_phase(2)

    def down():
        for pr in range(4):
            for pc in range(4):
                i = pr * 4 + pc
                left = selx[i - 1] if pc > 0 else roll(selx[pr * 4 + 3], 1, 1)
                up = sely[i - 4] if pr > 0 else roll(sely[12 + pc], 1, 0)
                rhs[i] = SCREEN * lum[i] + (left - selx[i]) + (up - sely[i])
        sweep(lum, fa, rhs, w0, 4, 1.0)
        sweep(fa, fb, rhs, w0, 4, 1.0)
        for a in range(2):
            for b in range(2):
                total = None
                for pr in (2 * a, 2 * a + 1):
                    for pc in (2 * b, 2 * b + 1):
                        i = pr * 4 + pc
                        res = (rhs[i] - SCREEN * fb[i]) + (around(fb, pr, pc, 4) - d0[which(pr, pc, 4)] * fb[i])
                        total = res if total is None else total + res
                f1[a * 2 + b] = 0.25 * total
                ea[a * 2 + b] = w1[which(a, b, 2)] * (0.25 * total)
        sweep(ea, eb, f1, w1, 2, 0.5)

    def coarsest():
        total = None
        for a in range(2):
            for b in range(2):
                i = a * 2 + b
                res = (f1[i] - SCREEN * eb[i]) + (0.5 * around(eb, a, b, 2) - d1[which(a, b, 2)] * eb[i])
                total = res if total is None else total + res
        return 0.25 * total

    down()
    total = coarsest() * inside
    tail = total[QR:ER]
    tall = jnp.concatenate([
        total[0:QR],
        jnp.where(sub8[:, :1] < 4, tail, 0.0), jnp.where(sub8[:, :1] >= 4, tail, 0.0),
        jnp.zeros((48, EC), F32),
    ], axis=0)
    turned = tall[:, QC:EC].T
    beside = jnp.where(sub8 < 4, turned[0:8], turned[120:128])
    strip[r] = jnp.concatenate([total[:, 0:QC], beside], axis=0)
    own_t = jnp.concatenate([tall[:, 0:QC].T, beside, jnp.zeros((8, 128), F32)], axis=0)
    for one in consts:
        one.wait()

    def small(i):
        return tab[pl.ds(2 * QC + i, 1), :]

    def six(xs_, cs_, dims=((1,), (0,))):
        (xh, xm, xl), (ch, cm, cl) = xs_, cs_
        return mm(xh, ch, dims) + (
            (mm(xh, cm, dims) + mm(xm, ch, dims)) + (mm(xm, cm, dims) + (mm(xh, cl, dims) + mm(xl, ch, dims)))
        )

    base = pl.multiple_of(r * QR, QR)
    sub16 = lax.broadcasted_iota(jnp.int32, (16, NR * QR), 0)
    back = []
    for i in range(3):
        tail = jnp.where(
            sub16 < 8,
            ct[i, pl.ds(base + QR + 16, 16), :].astype(F32),
            ct[i, pl.ds(base, 16), :].astype(F32),
        ).astype(BF)
        back.append(jnp.concatenate([ct[i, pl.ds(base + 16, QR), :], tail], axis=0))
    pad = jnp.zeros((48, NR * QR), BF)
    share = six(split3(own_t), [jnp.concatenate([x, pad], axis=0) for x in back])
    r1, r2, l2, l1 = (share[QC + i:QC + i + 1] for i in (0, 1, 6, 7))
    share = share[0:QC]
    to_r = jnp.sum(share * tab[pl.ds(QC, QC), :], axis=0, keepdims=True)
    to_l = jnp.sum(share * tab[pl.ds(0, QC), :], axis=0, keepdims=True)
    to_r = small(12) * (to_r + r1 + small(12) * r2) + (small(11) * l1 + small(9) * l2)
    to_l = small(12) * (to_l + l1 + small(12) * l2) + (small(11) * r1 + small(9) * r2)
    def in_rows(xs_):
        return jnp.concatenate([x[:, t * 128:(t + 1) * 128] for x in xs_ for t in range(4)], axis=0)

    share_m[r] = in_rows([to_r, to_l, r2, l2])

    pl.semaphore_wait(barrier, len(peers))

    def send(src, dst, send_sem, recv_sem, device):
        copy = pltpu.make_async_remote_copy(
            src_ref=src, dst_ref=dst, send_sem=send_sem, recv_sem=recv_sem,
            device_id=device, device_id_type=MESH,
        )
        copy.start()
        return copy

    copies = [send(share_m.at[r], share_m.at[r], m_send.at[d], m_recv.at[d], (row_peer(d), c)) for d in row_order]

    far = [
        send(strip.at[r], strip.at[r], r_send.at[i], r_recv.at[i], (row_peer(d), c)) for i, d in enumerate((4, 2, 6))
    ]
    near = [send(strip.at[r], strip.at[r], r_send.at[3], r_recv.at[3], (sibling, c))]

    lane = lax.broadcasted_iota(jnp.int32, (QR, 128), 1)
    group = lane // 16
    for tile in range(2):
        packed_r = jnp.zeros((QR, 128), F32)
        packed_l = jnp.zeros((QR, 128), F32)
        for g in range(8):
            idx = tile * 8 + g
            if idx >= 12:
                break
            a, rp = divmod(idx, 4)
            edge = raw[a, 3, pl.ds(rp, QR, stride=4), :]
            packed_r = jnp.where(group == g, roll(edge, 16 * g - 112, 1), packed_r)
            edge = raw[a, 0, pl.ds(rp, QR, stride=4), :]
            packed_l = jnp.where(group == g, roll(edge, 16 * g, 1), packed_l)
        to_right[:, pl.ds(tile * 128, 128)] = packed_r
        to_left[:, pl.ds(tile * 128, 128)] = packed_l
    top, bottom = pl.ds(0, 16), pl.ds(H0 - 16, 16)
    body, lo, hi = pl.ds(0, QR), pl.ds(0, 8), pl.ds(QR - 8, 8)
    below, above = pl.ds(QR, 8), pl.ds(QR + 8, 8)
    halo = [
        send(src, dst, h_send.at[i], h_recv.at[i], (row_peer(dr), col_peer(dc)))
        for i, (src, dst, dr, dc) in enumerate([
            (to_right.at[hi], from_l.at[above], 1, 1),
            (to_left.at[hi], from_r.at[above], 1, -1),
            (to_right.at[lo], from_l.at[below], -1, 1),
            (to_left.at[lo], from_r.at[below], -1, -1),
            (to_right, from_l.at[body], 0, 1),
            (to_left, from_r.at[body], 0, -1),
            (raw.at[:, :, bottom], raw.at[:, :, pl.ds(H0 + 16, 16)], 1, 0),
            (raw.at[:, :, top], raw.at[:, :, pl.ds(H0, 16)], -1, 0),
        ])
    ]

    for copy in copies:
        copy.wait()
    m = share_m[...]
    mom[c] = ((m[0] + m[1]) + (m[2] + m[3])) + ((m[4] + m[5]) + (m[6] + m[7]))
    copies = []
    for d in col_order:
        block = mom.at[c, pl.ds(0, 16 if d in (1, NC - 1) else 8)]
        copies.append(send(block, block, c_send.at[d], c_recv.at[d], (r, col_peer(d))))

    for i, d in ((1, 2), (2, 6), (0, 4)):
        far[i].wait_recv()
        block = row_peer(-d)
        near.append(send(strip.at[block], strip.at[block], r_send.at[4 + i], r_recv.at[4 + i], (sibling, c)))
    for copy in near:
        copy.wait()
    for copy in far:
        copy.wait_send()

    pieces = []
    for o in range(NR):
        first, last = strip[o, pl.ds(0, 8), :], strip[o, pl.ds(QR - 8, 8), :]
        if o > 0:
            first = first + jnp.where(sub8 < 2, strip[o - 1, pl.ds(QR, 8), :], 0.0)
        if o < NR - 1:
            last = last + jnp.where(sub8 >= 6, strip[o + 1, pl.ds(QR, 8), :], 0.0)
        pieces += [first, strip[o, pl.ds(8, QR - 16), :], last]
    whole = jnp.concatenate(pieces, axis=0)
    beside = [strip[o, pl.ds(ER, 8), :] for o in range(NR)]
    pieces = []
    for t in range(4):
        even, odd = beside[2 * t], beside[2 * t + 1]
        x = jnp.where(lane8 < 66, even, 0.0) + jnp.where(lane8 >= 64, roll(odd, 64, 1), 0.0)
        x = x + jnp.where((lane8 >= 62) & (lane8 < 64), roll(odd, -16, 1), 0.0)
        if t < 3:
            x = x + jnp.where(lane8 >= 126, roll(beside[2 * t + 2], 48, 1), 0.0)
        if t > 0:
            x = x + jnp.where(lane8 < 2, roll(beside[2 * t - 1], 64, 1), 0.0)
        pieces.append(x)
    xt = jnp.concatenate([whole.T, jnp.concatenate(pieces, axis=1), jnp.zeros((8, NR * QR), F32)], axis=0)

    inner = pl.ds(16, NR * QR)
    g = six(split3(xt), [ct[i, inner, :] for i in range(3)])
    r1, r2, l2, l1 = (g[QC + i:QC + i + 1] for i in (0, 1, 6, 7))
    g = g[0:QC]

    jrow = lax.broadcasted_iota(jnp.int32, (QC, NR * QR), 0)
    fwd, bwd = g, g
    for i, s in enumerate((1, 2, 4, 8, 16, 32, 64)):
        p = small(i)
        fwd = fwd + jnp.where(jrow >= s, roll(fwd, s, 0) * p, 0.0)
        bwd = bwd + jnp.where(jrow < QC - s, roll(bwd, -s, 0) * p, 0.0)
    end, start = fwd[QC - 1:QC], bwd[0:1]
    own = small(7) * (fwd + bwd - g)
    near_a = small(7) * (l1 + small(0) * l2)
    near_b = small(7) * (r1 + small(0) * r2)
    for copy in halo:
        copy.wait()
    x = jnp.concatenate([by_phase(a, pl.ds(H0 + rp, 8, stride=4)) for a in range(3) for rp in range(4)], axis=0)
    y = permuted(x, perm[...])
    for a in range(3):
        for rp in range(4):
            i = (a * 4 + rp) * 8
            for pc in range(4):
                fields[a][rp * 4 + pc, pl.ds(QR, 8), pl.ds(0, 128)] = y[i:i + 8, pc * 128:(pc + 1) * 128]
    low8 = sub8 < 4
    lane_e = lax.broadcasted_iota(jnp.int32, (ER, 128), 1)

    def from_side(ref, tile):
        cols = pl.ds(tile * 128, 128)
        return jnp.concatenate(
            [ref[body, cols], jnp.where(low8, ref[below, cols], ref[above, cols])], axis=0
        )

    for a in range(3):
        pieces = []
        for rp in range(4):
            tile, gi = divmod(a * 4 + rp, 8)
            side_l, side_r = from_side(from_l, tile), from_side(from_r, tile)
            pieces.append(jnp.where(lane_e < 64, roll(side_r, -16 * gi, 1), roll(side_l, 112 - 16 * gi, 1)))
        y = permuted(jnp.concatenate(pieces, axis=0), side[...])
        for rp in range(4):
            for pc in range(4):
                fields[a][rp * 4 + pc, :, pl.ds(128, 128)] = y[rp * ER:(rp + 1) * ER, pc * 128:(pc + 1) * 128]
    for i in range(16):
        lum[i] = lum[i] * inside
        if i % 4 == 3:
            selx[i] = selx[i] * inside
        if i // 4 == 3:
            sely[i] = sely[i] * inside
    down()
    f2 = coarsest()
    f2 = jnp.concatenate([f2, f2[QR:ER]], axis=0)

    for copy in copies:
        copy.wait()
    low = sub8 < 4
    sum_a = jnp.zeros((8, 128), F32)
    sum_b = jnp.zeros((8, 128), F32)
    for o in range(NC):
        m = mom[o, pl.ds(0, 8), :]
        sum_a = sum_a + m * jnp.where(low, dist[lax.rem(c - o + 63, 32)], dist[c + o])
        sum_b = sum_b + m * jnp.where(low, dist[lax.rem(62 - c - o, 32)], dist[lax.rem(o - c + 63, 32)])

    def line(m, i):
        return jnp.concatenate([m[4 * i + t:4 * i + t + 1] for t in range(4)], axis=1)

    a_in = line(sum_a[0:4] + sum_a[4:8], 0) + near_a
    b_in = line(sum_b[0:4] + sum_b[4:8], 0) + near_b
    own = own + tab[pl.ds(0, QC), :] * a_in + tab[pl.ds(QC, QC), :] * b_in
    own = own - 4.0 * jnp.concatenate([
        line(mom[col_peer(-1), pl.ds(8, 8), :], 0), jnp.zeros((QC - 2, NR * QR), F32),
        line(mom[col_peer(1), pl.ds(8, 8), :], 1),
    ], axis=0)

    e2 = six(back, split3(own), ((1,), (1,)))

    lane = lax.broadcasted_iota(jnp.int32, (ER + 8, 128), 1)

    row = lax.broadcasted_iota(jnp.int32, (ER + 8, 128), 0)

    def beyond(inner, at, f):
        up = jnp.where((r == 0) & (row == 0), at, roll(at, 1, 0))
        down = jnp.where((r == NR - 1) & (row == QR - 1), at, roll(at, -1, 0))
        return 4.0 * ((1 + SCREEN) * at - f) - (up + down) - inner

    one = beyond(jnp.where(lane < 64, roll(e2, -1, 1), roll(e2, 1, 1)), e2, f2[:, 0:QC])
    side_f = f2[:, QC:EC]
    two = beyond(e2, one, jnp.where(lane < 64, roll(side_f, 1, 1), roll(side_f, -1, 1)))
    outer = jnp.where(lane == 0, roll(one, 1, 1), jnp.where(lane == 1, roll(two, 2, 1), 0.0))
    outer = jnp.where(lane == 127, roll(one, -1, 1), jnp.where(lane == 126, roll(two, -2, 1), outer))
    e2 = jnp.concatenate([e2, outer], axis=1)
    sub8 = lax.broadcasted_iota(jnp.int32, (8, EC), 0)
    e2 = jnp.concatenate([e2[0:QR], jnp.where(sub8 < 4, e2[QR:QR + 8], e2[QR + 8:QR + 16])], axis=0)
    e2 = e2 * inside

    for i in range(4):
        ea[i] = eb[i] + e2
    sweep(ea, ec, f1, w1, 2, 0.5)
    sweep(ec, ea, f1, w1, 2, 0.5)
    for pr in range(4):
        for pc in range(4):
            fa[pr * 4 + pc] = fb[pr * 4 + pc] + ea[(pr // 2) * 2 + pc // 2]
    sweep(fa, lum, rhs, w0, 4, 1.0)
    last_sweep(lum, fb, rhs, w0)
    copies = []
    half = QR // 2
    for h in range(2):
        x = jnp.concatenate([
            jnp.concatenate([fb[pr * 4 + pc, pl.ds(h * half, half), pl.ds(0, QC)] for pc in range(4)], axis=1)
            for pr in range(4)
        ], axis=0)
        y = permuted(x, permt[...])
        rows = pl.ds(h * 4 * half, 4 * half)
        for pr in range(4):
            for t in range(4):
                out[t, pl.ds(h * 4 * half + pr, half, stride=4), :] = y[pr * half:(pr + 1) * half, t * 128:(t + 1) * 128]
        for t in range(4):
            copy = pltpu.make_async_copy(out.at[t, rows], out_h.at[rows, pl.ds(t * 128, 128)], out_sem.at[h, t])
            copy.start()
            copies.append(copy)
    for copy in copies:
        copy.wait()


def shards(luminance, grad_x, grad_y, labels):
    consts = tables()
    vmem = pltpu.VMEM
    phases = vmem((16, ER, EC), F32)
    quarter = vmem((4, ER, EC), F32)
    nine = vmem((9, ER, EC), F32)
    dma = pltpu.SemaphoreType.DMA
    return pl.pallas_call(
        kernel,
        out_shape=jax.ShapeDtypeStruct((H0, W0), F32),
        in_specs=[pl.BlockSpec(memory_space=pl.ANY)] * 7,
        out_specs=pl.BlockSpec(memory_space=pl.ANY),
        scratch_shapes=[
            vmem((4, H0, W0), F32),
            vmem((4, H0, W0), F32),
            vmem((H0, W0), jnp.int32),
            vmem((3, 4, H0 + 32, 128), F32),
            vmem((W0, W0), BF),
            vmem((W0, W0), BF),
            vmem((128, W0), BF),
            vmem(consts[0].shape, BF),
            vmem(consts[1].shape, F32),
            vmem(consts[2].shape, F32),
            vmem((QR, 256), F32),
            vmem((QR, 256), F32),
            vmem((QR + 16, 256), F32),
            vmem((QR + 16, 256), F32),
            phases, phases, phases, phases, phases, phases,
            nine, nine, nine, nine,
            quarter, quarter, quarter, quarter,
            vmem((NR, ER + 8, QC), F32),
            vmem((NR, 16, 128), F32),
            vmem((NC, 16, 128), F32),
            vmem((4, H0, 128), F32),
            dma((4, 4)),
            dma((3,)),
            dma((2, 4)),
            dma((8,)),
            dma((8,)),
            dma((NR,)),
            dma((NR,)),
            dma((NR,)),
            dma((NR,)),
            dma((NC,)),
            dma((NC,)),
        ],
        compiler_params=pltpu.CompilerParams(
            collective_id=0, has_side_effects=True, vmem_limit_bytes=56 * 1024 * 1024
        ),
    )(luminance, grad_x, grad_y, labels, *[jnp.asarray(x) for x in consts])


def solution(mesh):
    return jax.shard_map(
        shards,
        mesh=mesh,
        in_specs=(
            P("rows", "cols"),
            P(None, "rows", "cols"),
            P(None, "rows", "cols"),
            P("rows", "cols"),
        ),
        out_specs=P("rows", "cols"),
        check_vma=False,
    )
```

```python
import functools
import math

import jax
import jax.numpy as jnp
import ml_dtypes
import numpy as np
from jax import lax
from jax.experimental import pallas as pl
from jax.experimental.pallas import tpu as pltpu
from jax.sharding import PartitionSpec as P

MESH = pl.DeviceIdType.MESH
SCREEN = 4e-06
OMEGA = 0.8
NR, NC = 8, 16
H0, W0 = 256, 512
QR, QC = 64, 128
ER, EC = 72, 256
BF, F32 = jnp.bfloat16, jnp.float32


def bf16_parts(x, parts):
    out = []
    rest = np.asarray(x, np.float64)
    for _ in range(parts):
        piece = rest.astype(ml_dtypes.bfloat16)
        out.append(piece)
        rest = rest - piece.astype(np.float64)
    return out


@functools.lru_cache(maxsize=None)
def tables():
    rows, cols = NR * QR, NC * QC
    k = np.arange(rows)
    place = np.arange(rows)
    phase = ((2 * place[:, None] + 1) * k[None, :]) % (4 * rows)
    scale = np.where(k == 0, math.sqrt(1.0 / rows), math.sqrt(2.0 / rows))
    ct = np.zeros((rows + 32, rows))
    ct[16:-16] = scale[None, :] * np.cos(phase * (math.pi / (2 * rows)))
    ct[:16] = ct[31:15:-1]
    ct[-16:] = ct[-17:-33:-1]
    ct = np.stack(bf16_parts(ct, 3))
    mu = SCREEN + 0.25 * 4 * np.sin(np.pi * k / (2 * rows)) ** 2
    half = 1 + 2 * mu
    rho = half - np.sqrt(4 * mu + 4 * mu * mu)
    g0 = 1 / (0.25 * (1 / rho - rho))
    t = np.arange(QC)
    from_left = rho[None, :] ** (t[:, None] + 1)
    from_right = rho[None, :] ** (QC - t[:, None])
    small = np.zeros((16, rows))
    for i in range(7):
        small[i] = rho ** (2**i)
    small[7] = g0
    small[8] = g0 * rho
    small[9] = rho ** (QC + 1)
    small[10] = 2 + 4 * mu
    small[11] = rho**QC
    small[12] = 1 / rho
    small[13] = rho**-2.0
    tab = np.concatenate([from_left, from_right, small]).astype(np.float32)
    dist = g0 / (1 - rho ** (2 * cols)) * rho ** (QC * np.arange(32)[:, None])
    dist = dist.reshape(32, 4, 128)
    dist = np.concatenate([dist, dist], axis=1).astype(np.float32)
    return ct, tab, dist


def split2(x):
    hi = x.astype(BF)
    return hi, (x - hi.astype(F32)).astype(BF)


def split3(x):
    hi = x.astype(BF)
    rest = x - hi.astype(F32)
    mid = rest.astype(BF)
    return hi, mid, (rest - mid.astype(F32)).astype(BF)


def mm(a, b, dims=((1,), (0,))):
    return lax.dot_general(a, b, (dims, ((), ())), preferred_element_type=F32)


def permuted(x, table):
    hi, mid = split2(x)
    return mm(hi, table) + mm(mid, table)


def roll(x, shift, axis):
    return pltpu.roll(x, shift % x.shape[axis], axis)


def around(ref, pr, pc, n):
    up = ref[(pr - 1) * n + pc] if pr > 0 else roll(ref[(n - 1) * n + pc], 1, 0)
    down = ref[(pr + 1) * n + pc] if pr < n - 1 else roll(ref[pc], -1, 0)
    left = ref[pr * n + pc - 1] if pc > 0 else roll(ref[pr * n + n - 1], 1, 1)
    right = ref[pr * n + pc + 1] if pc < n - 1 else roll(ref[pr * n], -1, 1)
    return (up + down) + (left + right)


def klass(p, n):
    return 0 if p == 0 else (2 if p == n - 1 else 1)


def which(pr, pc, n):
    return 3 * klass(pr, n) + klass(pc, n)


def sweep(src, dst, f, w, n, c):
    for pr in range(n):
        for pc in range(n):
            i = pr * n + pc
            nb = around(src, pr, pc, n)
            nb = nb if c == 1.0 else c * nb
            dst[i] = (1 - OMEGA) * src[i] + w[which(pr, pc, n)] * (f[i] + nb)


def distance(d):
    ring = (0, 1, 2, 1, 0)
    dy, dz = divmod(d, 4)
    return ring[dz] + ((4 - dz) * ring[dy] + dz * ring[dy + 1]) / 4


def kernel(
    lum_h, gx_h, gy_h, lab_h, ct_h, tab_h, dist_h,
    out_h,
    gx, gy, lab, raw, perm, permt, side, ct, tab, dist,
    to_right, to_left, from_l, from_r, fold_r, fold_l, fold_from_l, fold_from_r,
    lum, selx, sely, rhs, fa, fb, w0, d0, w1, d1, f1, ea, eb, ec,
    strip, share_m, mom, out,
    in_sem, const_sem, out_sem, h_send, h_recv, r_send, r_recv, m_send, m_recv, c_send, c_recv,
):
    r = lax.axis_index("rows")
    c = lax.axis_index("cols")

    def row_peer(d):
        return lax.rem(r + d + NR, NR)

    def col_peer(d):
        return lax.rem(c + d + NC, NC)

    sibling = r + 1 - 2 * lax.rem(r, 2)
    barrier = pltpu.get_barrier_semaphore()
    row_order = (4, 3, 5, 2, 6, 1, 7)
    col_order = sorted(range(1, NC), key=lambda d: -distance(d))
    peers = [(0, d) for d in col_order] + [(1, 1), (1, -1), (-1, 1), (-1, -1)] + [(d, 0) for d in row_order]
    for dr, dc in peers:
        pl.semaphore_signal(
            barrier, inc=1, device_id=(row_peer(dr), col_peer(dc)), device_id_type=MESH
        )

    CH = 64
    loads = []
    for i in range(H0 // CH):
        rows = pl.ds(i * CH, CH)
        loads.append([
            pltpu.make_async_copy(gx_h.at[:, rows], gx.at[:, rows], in_sem.at[i, 0]),
            pltpu.make_async_copy(gy_h.at[:, rows], gy.at[:, rows], in_sem.at[i, 1]),
            pltpu.make_async_copy(lab_h.at[rows], lab.at[rows], in_sem.at[i, 2]),
        ])
    lum_loads = [
        pltpu.make_async_copy(lum_h.at[:, pl.ds(t * 128, 128)], raw.at[0, t, pl.ds(0, H0)], in_sem.at[t, 3])
        for t in range(4)
    ]
    for one in lum_loads + [one for group in loads for one in group]:
        one.start()
    consts = [
        pltpu.make_async_copy(a, b, const_sem.at[i])
        for i, (a, b) in enumerate([(ct_h, ct), (tab_h, tab), (dist_h, dist)])
    ]

    src = lax.broadcasted_iota(jnp.int32, (W0, 128), 0)
    dst = 4 * lax.broadcasted_iota(jnp.int32, (W0, 128), 1)
    back_src = 4 * lax.broadcasted_iota(jnp.int32, (128, W0), 0)
    back_dst = lax.broadcasted_iota(jnp.int32, (128, W0), 1)
    src_s = lax.broadcasted_iota(jnp.int32, (128, 128), 0)
    lane_s = lax.broadcasted_iota(jnp.int32, (128, 128), 1)
    outer = (lane_s < 4) | (lane_s >= 124)
    for pc in range(4):
        part = pl.ds(pc * 128, 128)
        perm[:, part] = jnp.where(src == dst + pc, 1.0, 0.0).astype(BF)
        permt[part, :] = jnp.where(back_src + pc == back_dst, 1.0, 0.0).astype(BF)
        side[:, part] = jnp.where(outer & (src_s == lax.rem(4 * lane_s + pc, 128)), 1.0, 0.0).astype(BF)

    ri = lax.broadcasted_iota(jnp.int32, (ER, EC), 0)
    li = lax.broadcasted_iota(jnp.int32, (ER, EC), 1)
    out_rows = ((r == 0) & (ri >= 68)) | ((r == NR - 1) & (ri >= 64) & (ri < 68))
    out_cols = ((c == 0) & (li >= 192)) | ((c == NC - 1) & (li >= 128) & (li < 192))
    inside = jnp.where(out_rows | out_cols, 0.0, 1.0).astype(F32)
    edge_rows = [((r == 0) & (ri == 0)), None, ((r == NR - 1) & (ri == QR - 1))]
    edge_cols = [((c == 0) & (li == 0)), None, ((c == NC - 1) & (li == QC - 1))]
    for a in range(3):
        for b in range(3):
            deg = jnp.full((ER, EC), 4.0, F32)
            if a != 1:
                deg = deg - jnp.where(edge_rows[a], 1.0, 0.0)
            if b != 1:
                deg = deg - jnp.where(edge_cols[b], 1.0, 0.0)
            for wr, dr_, coef in ((w0, d0, 1.0), (w1, d1, 0.5)):
                if coef == 0.5 and (a == 1 or b == 1):
                    continue
                dr_[3 * a + b] = coef * deg
                wr[3 * a + b] = inside * (OMEGA / (SCREEN + coef * deg))
    fields = (lum, selx, sely)
    for field in fields:
        for i in range(16):
            field[i, pl.ds(QR, 8), pl.ds(0, QC)] = jnp.zeros((8, QC), F32)
            field[i, :, pl.ds(QC, 128)] = jnp.zeros((ER, 128), F32)

    def by_phase(a, rows):
        return jnp.concatenate([raw[a, t, rows, :] for t in range(4)], axis=1)

    def own_by_phase(a):
        x = jnp.concatenate([by_phase(a, pl.ds(rp, QR, stride=4)) for rp in range(4)], axis=0)
        y = permuted(x, perm[...])
        for rp in range(4):
            for pc in range(4):
                fields[a][rp * 4 + pc, pl.ds(0, QR), pl.ds(0, 128)] = y[rp * QR:(rp + 1) * QR, pc * 128:(pc + 1) * 128]

    for one in lum_loads:
        one.wait()
    own_by_phase(0)

    lane8 = lax.broadcasted_iota(jnp.int32, (8, 128), 1)
    sub8 = lax.broadcasted_iota(jnp.int32, (8, 128), 0)
    for i in range(H0 // CH):
        for one in loads[i]:
            one.wait()

        def select(s, carry, i=i):
            row = pl.multiple_of(i * CH + s * 8, 8)
            rows = pl.ds(row, 8)
            last_row = (r == NR - 1) & (sub8 + row == H0 - 1)
            for t in range(4):
                cols = pl.ds(t * 128, 128)
                lb = lab[rows, cols]
                is0, is1, is2 = lb == 0, lb == 1, lb == 2

                def pick(g):
                    return jnp.where(is0, g[0, rows, cols], jnp.where(
                        is1, g[1, rows, cols], jnp.where(is2, g[2, rows, cols], g[3, rows, cols])))

                sx, sy = pick(gx), pick(gy)
                if t == 3:
                    sx = jnp.where((c == NC - 1) & (lane8 == 127), 0.0, sx)
                raw[1, t, rows, :] = sx
                raw[2, t, rows, :] = jnp.where(last_row, 0.0, sy)
            return carry

        lax.fori_loop(0, CH // 8, select, 0, unroll=2)
    for one in consts:
        one.start()

    own_by_phase(1)
    own_by_phase(2)

    def down():
        for pr in range(4):
            for pc in range(4):
                i = pr * 4 + pc
                left = selx[i - 1] if pc > 0 else roll(selx[pr * 4 + 3], 1, 1)
                up = sely[i - 4] if pr > 0 else roll(sely[12 + pc], 1, 0)
                rhs[i] = SCREEN * lum[i] + (left - selx[i]) + (up - sely[i])
        sweep(lum, fa, rhs, w0, 4, 1.0)
        sweep(fa, fb, rhs, w0, 4, 1.0)
        for a in range(2):
            for b in range(2):
                total = None
                for pr in (2 * a, 2 * a + 1):
                    for pc in (2 * b, 2 * b + 1):
                        i = pr * 4 + pc
                        res = (rhs[i] - SCREEN * fb[i]) + (around(fb, pr, pc, 4) - d0[which(pr, pc, 4)] * fb[i])
                        total = res if total is None else total + res
                f1[a * 2 + b] = 0.25 * total
                ea[a * 2 + b] = w1[which(a, b, 2)] * (0.25 * total)
        sweep(ea, eb, f1, w1, 2, 0.5)

    def coarsest():
        total = None
        for a in range(2):
            for b in range(2):
                i = a * 2 + b
                res = (f1[i] - SCREEN * eb[i]) + (0.5 * around(eb, a, b, 2) - d1[which(a, b, 2)] * eb[i])
                total = res if total is None else total + res
        return 0.25 * total

    down()
    total = coarsest() * inside
    tail = total[QR:ER]
    tall = jnp.concatenate([
        total[0:QR],
        jnp.where(sub8[:, :1] < 4, tail, 0.0), jnp.where(sub8[:, :1] >= 4, tail, 0.0),
        jnp.zeros((48, EC), F32),
    ], axis=0)
    turned = tall[:, QC:EC].T
    beside = jnp.where(sub8 < 4, turned[0:8], turned[120:128])
    strip[r] = jnp.concatenate([total[:, 0:QC], beside], axis=0)
    own_t = jnp.concatenate([tall[:, 0:QC].T, beside, jnp.zeros((8, 128), F32)], axis=0)
    for one in consts:
        one.wait()

    def small(i):
        return tab[pl.ds(2 * QC + i, 1), :]

    def six(xs_, cs_, dims=((1,), (0,))):
        (xh, xm, xl), (ch, cm, cl) = xs_, cs_
        return mm(xh, ch, dims) + (
            (mm(xh, cm, dims) + mm(xm, ch, dims)) + (mm(xm, cm, dims) + (mm(xh, cl, dims) + mm(xl, ch, dims)))
        )

    base = pl.multiple_of(r * QR, QR)
    sub16 = lax.broadcasted_iota(jnp.int32, (16, NR * QR), 0)
    back = []
    for i in range(3):
        tail = jnp.where(
            sub16 < 8,
            ct[i, pl.ds(base + QR + 16, 16), :].astype(F32),
            ct[i, pl.ds(base, 16), :].astype(F32),
        ).astype(BF)
        back.append(jnp.concatenate([ct[i, pl.ds(base + 16, QR), :], tail], axis=0))
    pad = jnp.zeros((48, NR * QR), BF)
    share = six(split3(own_t), [jnp.concatenate([x, pad], axis=0) for x in back])
    r1, r2, l2, l1 = (share[QC + i:QC + i + 1] for i in (0, 1, 6, 7))
    share = share[0:QC]
    to_r = jnp.sum(share * tab[pl.ds(QC, QC), :], axis=0, keepdims=True)
    to_l = jnp.sum(share * tab[pl.ds(0, QC), :], axis=0, keepdims=True)
    to_r = small(12) * (to_r + r1 + small(12) * r2) + (small(11) * l1 + small(9) * l2)
    to_l = small(12) * (to_l + l1 + small(12) * l2) + (small(11) * r1 + small(9) * r2)
    def in_rows(xs_):
        return jnp.concatenate([x[:, t * 128:(t + 1) * 128] for x in xs_ for t in range(4)], axis=0)

    share_m[r] = in_rows([to_r, to_l, r2, l2])

    pl.semaphore_wait(barrier, len(peers))

    def send(src, dst, send_sem, recv_sem, device):
        copy = pltpu.make_async_remote_copy(
            src_ref=src, dst_ref=dst, send_sem=send_sem, recv_sem=recv_sem,
            device_id=device, device_id_type=MESH,
        )
        copy.start()
        return copy

    copies = [send(share_m.at[r], share_m.at[r], m_send.at[d], m_recv.at[d], (row_peer(d), c)) for d in row_order]

    far = [
        send(strip.at[r], strip.at[r], r_send.at[i], r_recv.at[i], (row_peer(d), c)) for i, d in enumerate((4, 2, 6))
    ]
    near = [send(strip.at[r], strip.at[r], r_send.at[3], r_recv.at[3], (sibling, c))]

    lane = lax.broadcasted_iota(jnp.int32, (QR, 128), 1)
    group = lane // 16
    for tile in range(2):
        packed_r = jnp.zeros((QR, 128), F32)
        packed_l = jnp.zeros((QR, 128), F32)
        for g in range(8):
            idx = tile * 8 + g
            if idx >= 12:
                break
            a, rp = divmod(idx, 4)
            edge = raw[a, 3, pl.ds(rp, QR, stride=4), :]
            packed_r = jnp.where(group == g, roll(edge, 16 * g - 112, 1), packed_r)
            edge = raw[a, 0, pl.ds(rp, QR, stride=4), :]
            packed_l = jnp.where(group == g, roll(edge, 16 * g, 1), packed_l)
        to_right[:, pl.ds(tile * 128, 128)] = packed_r
        to_left[:, pl.ds(tile * 128, 128)] = packed_l
    half = QR // 2
    fold_r[...] = jnp.where(lane[0:half] < 64, packed_r[0:half], roll(packed_r[half:QR], 64, 1))
    fold_l[...] = jnp.where(lane[0:half] < 64, packed_l[0:half], roll(packed_l[half:QR], 64, 1))
    top, bottom = pl.ds(0, 16), pl.ds(H0 - 16, 16)
    body, lo, hi = pl.ds(0, QR), pl.ds(0, 8), pl.ds(QR - 8, 8)
    below, above = pl.ds(QR, 8), pl.ds(QR + 8, 8)
    halo = [
        send(src, dst, h_send.at[i], h_recv.at[i], (row_peer(dr), col_peer(dc)))
        for i, (src, dst, dr, dc) in enumerate([
            (to_right.at[hi], from_l.at[above], 1, 1),
            (to_left.at[hi], from_r.at[above], 1, -1),
            (to_right.at[lo], from_l.at[below], -1, 1),
            (to_left.at[lo], from_r.at[below], -1, -1),
            (to_right.at[:, pl.ds(0, 128)], from_l.at[body, pl.ds(0, 128)], 0, 1),
            (to_left.at[:, pl.ds(0, 128)], from_r.at[body, pl.ds(0, 128)], 0, -1),
            (fold_r, fold_from_l, 0, 1),
            (fold_l, fold_from_r, 0, -1),
            (raw.at[:, :, bottom], raw.at[:, :, pl.ds(H0 + 16, 16)], 1, 0),
            (raw.at[:, :, top], raw.at[:, :, pl.ds(H0, 16)], -1, 0),
        ])
    ]

    for copy in copies:
        copy.wait()
    m = share_m[...]
    mom[c] = ((m[0] + m[1]) + (m[2] + m[3])) + ((m[4] + m[5]) + (m[6] + m[7]))
    copies = []
    for d in col_order:
        block = mom.at[c, pl.ds(0, 16 if d in (1, NC - 1) else 8)]
        copies.append(send(block, block, c_send.at[d], c_recv.at[d], (r, col_peer(d))))

    for i, d in ((1, 2), (2, 6), (0, 4)):
        far[i].wait_recv()
        block = row_peer(-d)
        near.append(send(strip.at[block], strip.at[block], r_send.at[4 + i], r_recv.at[4 + i], (sibling, c)))
    for copy in near:
        copy.wait()
    for copy in far:
        copy.wait_send()

    pieces = []
    for o in range(NR):
        first, last = strip[o, pl.ds(0, 8), :], strip[o, pl.ds(QR - 8, 8), :]
        if o > 0:
            first = first + jnp.where(sub8 < 2, strip[o - 1, pl.ds(QR, 8), :], 0.0)
        if o < NR - 1:
            last = last + jnp.where(sub8 >= 6, strip[o + 1, pl.ds(QR, 8), :], 0.0)
        pieces += [first, strip[o, pl.ds(8, QR - 16), :], last]
    whole = jnp.concatenate(pieces, axis=0)
    beside = [strip[o, pl.ds(ER, 8), :] for o in range(NR)]
    pieces = []
    for t in range(4):
        even, odd = beside[2 * t], beside[2 * t + 1]
        x = jnp.where(lane8 < 66, even, 0.0) + jnp.where(lane8 >= 64, roll(odd, 64, 1), 0.0)
        x = x + jnp.where((lane8 >= 62) & (lane8 < 64), roll(odd, -16, 1), 0.0)
        if t < 3:
            x = x + jnp.where(lane8 >= 126, roll(beside[2 * t + 2], 48, 1), 0.0)
        if t > 0:
            x = x + jnp.where(lane8 < 2, roll(beside[2 * t - 1], 64, 1), 0.0)
        pieces.append(x)
    xt = jnp.concatenate([whole.T, jnp.concatenate(pieces, axis=1), jnp.zeros((8, NR * QR), F32)], axis=0)

    inner = pl.ds(16, NR * QR)
    g = six(split3(xt), [ct[i, inner, :] for i in range(3)])
    r1, r2, l2, l1 = (g[QC + i:QC + i + 1] for i in (0, 1, 6, 7))
    g = g[0:QC]

    jrow = lax.broadcasted_iota(jnp.int32, (QC, NR * QR), 0)
    fwd, bwd = g, g
    for i, s in enumerate((1, 2, 4, 8, 16, 32, 64)):
        p = small(i)
        fwd = fwd + jnp.where(jrow >= s, roll(fwd, s, 0) * p, 0.0)
        bwd = bwd + jnp.where(jrow < QC - s, roll(bwd, -s, 0) * p, 0.0)
    end, start = fwd[QC - 1:QC], bwd[0:1]
    own = small(7) * (fwd + bwd - g)
    near_a = small(7) * (l1 + small(0) * l2)
    near_b = small(7) * (r1 + small(0) * r2)
    for copy in halo:
        copy.wait()
    x = jnp.concatenate([by_phase(a, pl.ds(H0 + rp, 8, stride=4)) for a in range(3) for rp in range(4)], axis=0)
    y = permuted(x, perm[...])
    for a in range(3):
        for rp in range(4):
            i = (a * 4 + rp) * 8
            for pc in range(4):
                fields[a][rp * 4 + pc, pl.ds(QR, 8), pl.ds(0, 128)] = y[i:i + 8, pc * 128:(pc + 1) * 128]
    low8 = sub8 < 4
    lane_e = lax.broadcasted_iota(jnp.int32, (ER, 128), 1)

    def from_side(ref, folded, tile):
        cols = pl.ds(tile * 128, 128)
        rows = ref[body, cols] if tile == 0 else jnp.concatenate([folded[...], roll(folded[...], 64, 1)], axis=0)
        return jnp.concatenate([rows, jnp.where(low8, ref[below, cols], ref[above, cols])], axis=0)

    for a in range(3):
        pieces = []
        for rp in range(4):
            tile, gi = divmod(a * 4 + rp, 8)
            side_l, side_r = from_side(from_l, fold_from_l, tile), from_side(from_r, fold_from_r, tile)
            pieces.append(jnp.where(lane_e < 64, roll(side_r, -16 * gi, 1), roll(side_l, 112 - 16 * gi, 1)))
        y = permuted(jnp.concatenate(pieces, axis=0), side[...])
        for rp in range(4):
            for pc in range(4):
                fields[a][rp * 4 + pc, :, pl.ds(128, 128)] = y[rp * ER:(rp + 1) * ER, pc * 128:(pc + 1) * 128]
    for i in range(16):
        lum[i] = lum[i] * inside
        if i % 4 == 3:
            selx[i] = selx[i] * inside
        if i // 4 == 3:
            sely[i] = sely[i] * inside
    down()
    f2 = coarsest()
    f2 = jnp.concatenate([f2, f2[QR:ER]], axis=0)

    for copy in copies:
        copy.wait()
    low = sub8 < 4
    sum_a = jnp.zeros((8, 128), F32)
    sum_b = jnp.zeros((8, 128), F32)
    for o in range(NC):
        m = mom[o, pl.ds(0, 8), :]
        sum_a = sum_a + m * jnp.where(low, dist[lax.rem(c - o + 63, 32)], dist[c + o])
        sum_b = sum_b + m * jnp.where(low, dist[lax.rem(62 - c - o, 32)], dist[lax.rem(o - c + 63, 32)])

    def line(m, i):
        return jnp.concatenate([m[4 * i + t:4 * i + t + 1] for t in range(4)], axis=1)

    a_in = line(sum_a[0:4] + sum_a[4:8], 0) + near_a
    b_in = line(sum_b[0:4] + sum_b[4:8], 0) + near_b
    own = own + tab[pl.ds(0, QC), :] * a_in + tab[pl.ds(QC, QC), :] * b_in
    own = own - 4.0 * jnp.concatenate([
        line(mom[col_peer(-1), pl.ds(8, 8), :], 0), jnp.zeros((QC - 2, NR * QR), F32),
        line(mom[col_peer(1), pl.ds(8, 8), :], 1),
    ], axis=0)

    e2 = six(back, split3(own), ((1,), (1,)))

    lane = lax.broadcasted_iota(jnp.int32, (ER + 8, 128), 1)

    row = lax.broadcasted_iota(jnp.int32, (ER + 8, 128), 0)

    def beyond(inner, at, f):
        up = jnp.where((r == 0) & (row == 0), at, roll(at, 1, 0))
        down = jnp.where((r == NR - 1) & (row == QR - 1), at, roll(at, -1, 0))
        return 4.0 * ((1 + SCREEN) * at - f) - (up + down) - inner

    one = beyond(jnp.where(lane < 64, roll(e2, -1, 1), roll(e2, 1, 1)), e2, f2[:, 0:QC])
    side_f = f2[:, QC:EC]
    two = beyond(e2, one, jnp.where(lane < 64, roll(side_f, 1, 1), roll(side_f, -1, 1)))
    outer = jnp.where(lane == 0, roll(one, 1, 1), jnp.where(lane == 1, roll(two, 2, 1), 0.0))
    outer = jnp.where(lane == 127, roll(one, -1, 1), jnp.where(lane == 126, roll(two, -2, 1), outer))
    e2 = jnp.concatenate([e2, outer], axis=1)
    sub8 = lax.broadcasted_iota(jnp.int32, (8, EC), 0)
    e2 = jnp.concatenate([e2[0:QR], jnp.where(sub8 < 4, e2[QR:QR + 8], e2[QR + 8:QR + 16])], axis=0)
    e2 = e2 * inside

    for i in range(4):
        ea[i] = eb[i] + e2
    sweep(ea, ec, f1, w1, 2, 0.5)
    sweep(ec, ea, f1, w1, 2, 0.5)
    for pr in range(4):
        for pc in range(4):
            fa[pr * 4 + pc] = fb[pr * 4 + pc] + ea[(pr // 2) * 2 + pc // 2]
    sweep(fa, lum, rhs, w0, 4, 1.0)
    sweep(lum, fb, rhs, w0, 4, 1.0)
    x = jnp.concatenate([
        jnp.concatenate([fb[pr * 4 + pc, pl.ds(0, QR), pl.ds(0, QC)] for pc in range(4)], axis=1)
        for pr in range(4)
    ], axis=0)
    y = permuted(x, permt[...])
    for pr in range(4):
        for t in range(4):
            out[t, pl.ds(pr, QR, stride=4), :] = y[pr * QR:(pr + 1) * QR, t * 128:(t + 1) * 128]
    copies = [
        pltpu.make_async_copy(out.at[t], out_h.at[:, pl.ds(t * 128, 128)], out_sem.at[t]) for t in range(4)
    ]
    for copy in copies:
        copy.start()
    for copy in copies:
        copy.wait()


def shards(luminance, grad_x, grad_y, labels):
    consts = tables()
    vmem = pltpu.VMEM
    phases = vmem((16, ER, EC), F32)
    quarter = vmem((4, ER, EC), F32)
    nine = vmem((9, ER, EC), F32)
    dma = pltpu.SemaphoreType.DMA
    return pl.pallas_call(
        kernel,
        out_shape=jax.ShapeDtypeStruct((H0, W0), F32),
        in_specs=[pl.BlockSpec(memory_space=pl.ANY)] * 7,
        out_specs=pl.BlockSpec(memory_space=pl.ANY),
        scratch_shapes=[
            vmem((4, H0, W0), F32),
            vmem((4, H0, W0), F32),
            vmem((H0, W0), jnp.int32),
            vmem((3, 4, H0 + 32, 128), F32),
            vmem((W0, W0), BF),
            vmem((W0, W0), BF),
            vmem((128, W0), BF),
            vmem(consts[0].shape, BF),
            vmem(consts[1].shape, F32),
            vmem(consts[2].shape, F32),
            vmem((QR, 256), F32),
            vmem((QR, 256), F32),
            vmem((QR + 16, 256), F32),
            vmem((QR + 16, 256), F32),
            *([vmem((QR // 2, 128), F32)] * 4),
            phases, phases, phases, phases, phases, phases,
            nine, nine, nine, nine,
            quarter, quarter, quarter, quarter,
            vmem((NR, ER + 8, QC), F32),
            vmem((NR, 16, 128), F32),
            vmem((NC, 16, 128), F32),
            vmem((4, H0, 128), F32),
            dma((4, 4)),
            dma((3,)),
            dma((4,)),
            dma((10,)),
            dma((10,)),
            dma((NR,)),
            dma((NR,)),
            dma((NR,)),
            dma((NR,)),
            dma((NC,)),
            dma((NC,)),
        ],
        compiler_params=pltpu.CompilerParams(
            collective_id=0, has_side_effects=True, vmem_limit_bytes=56 * 1024 * 1024
        ),
    )(luminance, grad_x, grad_y, labels, *[jnp.asarray(x) for x in consts])


def solution(mesh):
    return jax.shard_map(
        shards,
        mesh=mesh,
        in_specs=(
            P("rows", "cols"),
            P(None, "rows", "cols"),
            P(None, "rows", "cols"),
            P("rows", "cols"),
        ),
        out_specs=P("rows", "cols"),
        check_vma=False,
    )
```

```python
import functools
import math

import jax
import jax.numpy as jnp
import ml_dtypes
import numpy as np
from jax import lax
from jax.experimental import pallas as pl
from jax.experimental.pallas import tpu as pltpu
from jax.sharding import PartitionSpec as P

MESH = pl.DeviceIdType.MESH
SCREEN = 4e-06
OMEGA = 0.8
NR, NC = 8, 16
H0, W0 = 256, 512
QR, QC = 64, 128
ER, EC = 72, 256
BF, F32 = jnp.bfloat16, jnp.float32


def bf16_parts(x, parts):
    out = []
    rest = np.asarray(x, np.float64)
    for _ in range(parts):
        piece = rest.astype(ml_dtypes.bfloat16)
        out.append(piece)
        rest = rest - piece.astype(np.float64)
    return out


@functools.lru_cache(maxsize=None)
def tables():
    rows, cols = NR * QR, NC * QC
    k = np.arange(rows)
    place = np.arange(rows)
    phase = ((2 * place[:, None] + 1) * k[None, :]) % (4 * rows)
    scale = np.where(k == 0, math.sqrt(1.0 / rows), math.sqrt(2.0 / rows))
    ct = np.zeros((rows + 32, rows))
    ct[16:-16] = scale[None, :] * np.cos(phase * (math.pi / (2 * rows)))
    ct[:16] = ct[31:15:-1]
    ct[-16:] = ct[-17:-33:-1]
    ct = np.stack(bf16_parts(ct, 3))
    mu = SCREEN + 0.25 * 4 * np.sin(np.pi * k / (2 * rows)) ** 2
    half = 1 + 2 * mu
    rho = half - np.sqrt(4 * mu + 4 * mu * mu)
    g0 = 1 / (0.25 * (1 / rho - rho))
    t = np.arange(QC)
    from_left = rho[None, :] ** (t[:, None] + 1)
    from_right = rho[None, :] ** (QC - t[:, None])
    small = np.zeros((16, rows))
    for i in range(7):
        small[i] = rho ** (2**i)
    small[7] = g0
    small[8] = g0 * rho
    small[9] = rho ** (QC + 1)
    small[10] = 2 + 4 * mu
    small[11] = rho**QC
    small[12] = 1 / rho
    small[13] = rho**-2.0
    tab = np.concatenate([from_left, from_right, small]).astype(np.float32)
    dist = g0 / (1 - rho ** (2 * cols)) * rho ** (QC * np.arange(32)[:, None])
    dist = dist.reshape(32, 4, 128)
    dist = np.concatenate([dist, dist], axis=1).astype(np.float32)
    return ct, tab, dist


def split2(x):
    hi = x.astype(BF)
    return hi, (x - hi.astype(F32)).astype(BF)


def split3(x):
    hi = x.astype(BF)
    rest = x - hi.astype(F32)
    mid = rest.astype(BF)
    return hi, mid, (rest - mid.astype(F32)).astype(BF)


def mm(a, b, dims=((1,), (0,))):
    return lax.dot_general(a, b, (dims, ((), ())), preferred_element_type=F32)


def permuted(x, table):
    hi, mid = split2(x)
    return mm(hi, table) + mm(mid, table)


def roll(x, shift, axis):
    return pltpu.roll(x, shift % x.shape[axis], axis)


def around(ref, pr, pc, n):
    up = ref[(pr - 1) * n + pc] if pr > 0 else roll(ref[(n - 1) * n + pc], 1, 0)
    down = ref[(pr + 1) * n + pc] if pr < n - 1 else roll(ref[pc], -1, 0)
    left = ref[pr * n + pc - 1] if pc > 0 else roll(ref[pr * n + n - 1], 1, 1)
    right = ref[pr * n + pc + 1] if pc < n - 1 else roll(ref[pr * n], -1, 1)
    return (up + down) + (left + right)


def klass(p, n):
    return 0 if p == 0 else (2 if p == n - 1 else 1)


def which(pr, pc, n):
    return 3 * klass(pr, n) + klass(pc, n)


def sweep(src, dst, f, w, n, c):
    for pr in range(n):
        for pc in range(n):
            i = pr * n + pc
            nb = around(src, pr, pc, n)
            nb = nb if c == 1.0 else c * nb
            dst[i] = (1 - OMEGA) * src[i] + w[which(pr, pc, n)] * (f[i] + nb)


def distance(d):
    ring = (0, 1, 2, 1, 0)
    dy, dz = divmod(d, 4)
    return ring[dz] + ((4 - dz) * ring[dy] + dz * ring[dy + 1]) / 4


def last_sweep(src, dst, f, w):
    own = (pl.ds(0, QR), pl.ds(0, QC))

    def rolled(i, shift, axis):
        return roll(src[i], shift, axis)[0:QR, 0:QC]

    for pr in range(4):
        for pc in range(4):
            i = pr * 4 + pc
            up = src[(i - 4, *own)] if pr > 0 else rolled(12 + pc, 1, 0)
            down = src[(i + 4, *own)] if pr < 3 else rolled(pc, -1, 0)
            left = src[(i - 1, *own)] if pc > 0 else rolled(i + 3, 1, 1)
            right = src[(i + 1, *own)] if pc < 3 else rolled(i - 3, -1, 1)
            nb = (up + down) + (left + right)
            dst[(i, *own)] = (1 - OMEGA) * src[(i, *own)] + w[(which(pr, pc, 4), *own)] * (f[(i, *own)] + nb)


def kernel(
    lum_h, gx_h, gy_h, lab_h, ct_h, tab_h, dist_h,
    out_h,
    gx, gy, lab, raw, perm, permt, side, ct, tab, dist,
    to_right, to_left, from_l, from_r,
    lum, selx, sely, rhs, fa, fb, w0, d0, w1, d1, f1, ea, eb, ec,
    strip, share_m, mom, out,
    in_sem, const_sem, out_sem, h_send, h_recv, r_send, r_recv, m_send, m_recv, c_send, c_recv,
):
    r = lax.axis_index("rows")
    c = lax.axis_index("cols")

    def row_peer(d):
        return lax.rem(r + d + NR, NR)

    def col_peer(d):
        return lax.rem(c + d + NC, NC)

    sibling = r + 1 - 2 * lax.rem(r, 2)
    barrier = pltpu.get_barrier_semaphore()
    row_order = (4, 3, 5, 2, 6, 1, 7)
    col_order = sorted(range(1, NC), key=lambda d: -distance(d))
    peers = [(0, d) for d in col_order] + [(1, 1), (1, -1), (-1, 1), (-1, -1)] + [(d, 0) for d in row_order]
    for dr, dc in peers:
        pl.semaphore_signal(
            barrier, inc=1, device_id=(row_peer(dr), col_peer(dc)), device_id_type=MESH
        )

    CH = 64
    loads = []
    for i in range(H0 // CH):
        rows = pl.ds(i * CH, CH)
        loads.append([
            pltpu.make_async_copy(gx_h.at[:, rows], gx.at[:, rows], in_sem.at[i, 0]),
            pltpu.make_async_copy(gy_h.at[:, rows], gy.at[:, rows], in_sem.at[i, 1]),
            pltpu.make_async_copy(lab_h.at[rows], lab.at[rows], in_sem.at[i, 2]),
        ])
    lum_loads = [
        pltpu.make_async_copy(lum_h.at[:, pl.ds(t * 128, 128)], raw.at[0, t, pl.ds(0, H0)], in_sem.at[t, 3])
        for t in range(4)
    ]
    for one in lum_loads + [one for group in loads for one in group]:
        one.start()
    consts = [
        pltpu.make_async_copy(a, b, const_sem.at[i])
        for i, (a, b) in enumerate([(ct_h, ct), (tab_h, tab), (dist_h, dist)])
    ]

    src = lax.broadcasted_iota(jnp.int32, (W0, 128), 0)
    dst = 4 * lax.broadcasted_iota(jnp.int32, (W0, 128), 1)
    back_src = 4 * lax.broadcasted_iota(jnp.int32, (128, W0), 0)
    back_dst = lax.broadcasted_iota(jnp.int32, (128, W0), 1)
    src_s = lax.broadcasted_iota(jnp.int32, (128, 128), 0)
    lane_s = lax.broadcasted_iota(jnp.int32, (128, 128), 1)
    outer = (lane_s < 4) | (lane_s >= 124)
    for pc in range(4):
        part = pl.ds(pc * 128, 128)
        perm[:, part] = jnp.where(src == dst + pc, 1.0, 0.0).astype(BF)
        permt[part, :] = jnp.where(back_src + pc == back_dst, 1.0, 0.0).astype(BF)
        side[:, part] = jnp.where(outer & (src_s == lax.rem(4 * lane_s + pc, 128)), 1.0, 0.0).astype(BF)

    ri = lax.broadcasted_iota(jnp.int32, (ER, EC), 0)
    li = lax.broadcasted_iota(jnp.int32, (ER, EC), 1)
    out_rows = ((r == 0) & (ri >= 68)) | ((r == NR - 1) & (ri >= 64) & (ri < 68))
    out_cols = ((c == 0) & (li >= 192)) | ((c == NC - 1) & (li >= 128) & (li < 192))
    inside = jnp.where(out_rows | out_cols, 0.0, 1.0).astype(F32)
    edge_rows = [((r == 0) & (ri == 0)), None, ((r == NR - 1) & (ri == QR - 1))]
    edge_cols = [((c == 0) & (li == 0)), None, ((c == NC - 1) & (li == QC - 1))]
    for a in range(3):
        for b in range(3):
            deg = jnp.full((ER, EC), 4.0, F32)
            if a != 1:
                deg = deg - jnp.where(edge_rows[a], 1.0, 0.0)
            if b != 1:
                deg = deg - jnp.where(edge_cols[b], 1.0, 0.0)
            for wr, dr_, coef in ((w0, d0, 1.0), (w1, d1, 0.5)):
                if coef == 0.5 and (a == 1 or b == 1):
                    continue
                dr_[3 * a + b] = coef * deg
                wr[3 * a + b] = inside * (OMEGA / (SCREEN + coef * deg))
    fields = (lum, selx, sely)
    for field in fields:
        for i in range(16):
            field[i, pl.ds(QR, 8), pl.ds(0, QC)] = jnp.zeros((8, QC), F32)
            field[i, :, pl.ds(QC, 128)] = jnp.zeros((ER, 128), F32)

    def by_phase(a, rows):
        return jnp.concatenate([raw[a, t, rows, :] for t in range(4)], axis=1)

    def own_by_phase(a):
        x = jnp.concatenate([by_phase(a, pl.ds(rp, QR, stride=4)) for rp in range(4)], axis=0)
        y = permuted(x, perm[...])
        for rp in range(4):
            for pc in range(4):
                fields[a][rp * 4 + pc, pl.ds(0, QR), pl.ds(0, 128)] = y[rp * QR:(rp + 1) * QR, pc * 128:(pc + 1) * 128]

    for one in lum_loads:
        one.wait()
    own_by_phase(0)

    lane8 = lax.broadcasted_iota(jnp.int32, (8, 128), 1)
    sub8 = lax.broadcasted_iota(jnp.int32, (8, 128), 0)
    for i in range(H0 // CH):
        for one in loads[i]:
            one.wait()

        def select(s, carry, i=i):
            row = pl.multiple_of(i * CH + s * 8, 8)
            rows = pl.ds(row, 8)
            last_row = (r == NR - 1) & (sub8 + row == H0 - 1)
            for t in range(4):
                cols = pl.ds(t * 128, 128)
                lb = lab[rows, cols]
                is0, is1, is2 = lb == 0, lb == 1, lb == 2

                def pick(g):
                    return jnp.where(is0, g[0, rows, cols], jnp.where(
                        is1, g[1, rows, cols], jnp.where(is2, g[2, rows, cols], g[3, rows, cols])))

                sx, sy = pick(gx), pick(gy)
                if t == 3:
                    sx = jnp.where((c == NC - 1) & (lane8 == 127), 0.0, sx)
                raw[1, t, rows, :] = sx
                raw[2, t, rows, :] = jnp.where(last_row, 0.0, sy)
            return carry

        lax.fori_loop(0, CH // 8, select, 0, unroll=2)
    for one in consts:
        one.start()

    own_by_phase(1)
    own_by_phase(2)

    def down():
        for pr in range(4):
            for pc in range(4):
                i = pr * 4 + pc
                left = selx[i - 1] if pc > 0 else roll(selx[pr * 4 + 3], 1, 1)
                up = sely[i - 4] if pr > 0 else roll(sely[12 + pc], 1, 0)
                rhs[i] = SCREEN * lum[i] + (left - selx[i]) + (up - sely[i])
        sweep(lum, fa, rhs, w0, 4, 1.0)
        sweep(fa, fb, rhs, w0, 4, 1.0)
        for a in range(2):
            for b in range(2):
                total = None
                for pr in (2 * a, 2 * a + 1):
                    for pc in (2 * b, 2 * b + 1):
                        i = pr * 4 + pc
                        res = (rhs[i] - SCREEN * fb[i]) + (around(fb, pr, pc, 4) - d0[which(pr, pc, 4)] * fb[i])
                        total = res if total is None else total + res
                f1[a * 2 + b] = 0.25 * total
                ea[a * 2 + b] = w1[which(a, b, 2)] * (0.25 * total)
        sweep(ea, eb, f1, w1, 2, 0.5)

    def coarsest():
        total = None
        for a in range(2):
            for b in range(2):
                i = a * 2 + b
                res = (f1[i] - SCREEN * eb[i]) + (0.5 * around(eb, a, b, 2) - d1[which(a, b, 2)] * eb[i])
                total = res if total is None else total + res
        return 0.25 * total

    down()
    total = coarsest() * inside
    tail = total[QR:ER]
    tall = jnp.concatenate([
        total[0:QR],
        jnp.where(sub8[:, :1] < 4, tail, 0.0), jnp.where(sub8[:, :1] >= 4, tail, 0.0),
        jnp.zeros((48, EC), F32),
    ], axis=0)
    turned = tall[:, QC:EC].T
    beside = jnp.where(sub8 < 4, turned[0:8], turned[120:128])
    strip[r] = jnp.concatenate([total[:, 0:QC], beside], axis=0)
    own_t = jnp.concatenate([tall[:, 0:QC].T, beside, jnp.zeros((8, 128), F32)], axis=0)
    for one in consts:
        one.wait()

    def small(i):
        return tab[pl.ds(2 * QC + i, 1), :]

    def six(xs_, cs_, dims=((1,), (0,))):
        (xh, xm, xl), (ch, cm, cl) = xs_, cs_
        return mm(xh, ch, dims) + (
            (mm(xh, cm, dims) + mm(xm, ch, dims)) + (mm(xm, cm, dims) + (mm(xh, cl, dims) + mm(xl, ch, dims)))
        )

    base = pl.multiple_of(r * QR, QR)
    sub16 = lax.broadcasted_iota(jnp.int32, (16, NR * QR), 0)
    back = []
    for i in range(3):
        tail = jnp.where(
            sub16 < 8,
            ct[i, pl.ds(base + QR + 16, 16), :].astype(F32),
            ct[i, pl.ds(base, 16), :].astype(F32),
        ).astype(BF)
        back.append(jnp.concatenate([ct[i, pl.ds(base + 16, QR), :], tail], axis=0))
    pad = jnp.zeros((48, NR * QR), BF)
    share = six(split3(own_t), [jnp.concatenate([x, pad], axis=0) for x in back])
    r1, r2, l2, l1 = (share[QC + i:QC + i + 1] for i in (0, 1, 6, 7))
    share = share[0:QC]
    to_r = jnp.sum(share * tab[pl.ds(QC, QC), :], axis=0, keepdims=True)
    to_l = jnp.sum(share * tab[pl.ds(0, QC), :], axis=0, keepdims=True)
    to_r = small(12) * (to_r + r1 + small(12) * r2) + (small(11) * l1 + small(9) * l2)
    to_l = small(12) * (to_l + l1 + small(12) * l2) + (small(11) * r1 + small(9) * r2)
    def in_rows(xs_):
        return jnp.concatenate([x[:, t * 128:(t + 1) * 128] for x in xs_ for t in range(4)], axis=0)

    share_m[r] = in_rows([to_r, to_l, r2, l2])

    lane = lax.broadcasted_iota(jnp.int32, (QR, 128), 1)
    group = lane // 16
    for tile in range(2):
        packed_r = jnp.zeros((QR, 128), F32)
        packed_l = jnp.zeros((QR, 128), F32)
        for g in range(8):
            idx = tile * 8 + g
            if idx >= 12:
                break
            a, rp = divmod(idx, 4)
            edge = raw[a, 3, pl.ds(rp, QR, stride=4), :]
            packed_r = jnp.where(group == g, roll(edge, 16 * g - 112, 1), packed_r)
            edge = raw[a, 0, pl.ds(rp, QR, stride=4), :]
            packed_l = jnp.where(group == g, roll(edge, 16 * g, 1), packed_l)
        to_right[:, pl.ds(tile * 128, 128)] = packed_r
        to_left[:, pl.ds(tile * 128, 128)] = packed_l
    pl.semaphore_wait(barrier, len(peers))

    def send(src, dst, send_sem, recv_sem, device):
        copy = pltpu.make_async_remote_copy(
            src_ref=src, dst_ref=dst, send_sem=send_sem, recv_sem=recv_sem,
            device_id=device, device_id_type=MESH,
        )
        copy.start()
        return copy

    copies = [send(share_m.at[r], share_m.at[r], m_send.at[d], m_recv.at[d], (row_peer(d), c)) for d in row_order]

    far = [
        send(strip.at[r], strip.at[r], r_send.at[i], r_recv.at[i], (row_peer(d), c)) for i, d in enumerate((4, 2, 6))
    ]
    near = [send(strip.at[r], strip.at[r], r_send.at[3], r_recv.at[3], (sibling, c))]

    top, bottom = pl.ds(0, 16), pl.ds(H0 - 16, 16)
    body, lo, hi = pl.ds(0, QR), pl.ds(0, 8), pl.ds(QR - 8, 8)
    below, above = pl.ds(QR, 8), pl.ds(QR + 8, 8)
    halo = [
        send(src, dst, h_send.at[i], h_recv.at[i], (row_peer(dr), col_peer(dc)))
        for i, (src, dst, dr, dc) in enumerate([
            (to_right.at[hi], from_l.at[above], 1, 1),
            (to_left.at[hi], from_r.at[above], 1, -1),
            (to_right.at[lo], from_l.at[below], -1, 1),
            (to_left.at[lo], from_r.at[below], -1, -1),
            (to_right, from_l.at[body], 0, 1),
            (to_left, from_r.at[body], 0, -1),
            (raw.at[:, :, bottom], raw.at[:, :, pl.ds(H0 + 16, 16)], 1, 0),
            (raw.at[:, :, top], raw.at[:, :, pl.ds(H0, 16)], -1, 0),
        ])
    ]

    for copy in copies:
        copy.wait()
    m = share_m[...]
    mom[c] = ((m[0] + m[1]) + (m[2] + m[3])) + ((m[4] + m[5]) + (m[6] + m[7]))
    copies = []
    for d in col_order:
        block = mom.at[c, pl.ds(0, 16 if d in (1, NC - 1) else 8)]
        copies.append(send(block, block, c_send.at[d], c_recv.at[d], (r, col_peer(d))))

    for i, d in ((1, 2), (2, 6), (0, 4)):
        far[i].wait_recv()
        block = row_peer(-d)
        near.append(send(strip.at[block], strip.at[block], r_send.at[4 + i], r_recv.at[4 + i], (sibling, c)))
    for copy in near:
        copy.wait()
    for copy in far:
        copy.wait_send()

    pieces = []
    for o in range(NR):
        first, last = strip[o, pl.ds(0, 8), :], strip[o, pl.ds(QR - 8, 8), :]
        if o > 0:
            first = first + jnp.where(sub8 < 2, strip[o - 1, pl.ds(QR, 8), :], 0.0)
        if o < NR - 1:
            last = last + jnp.where(sub8 >= 6, strip[o + 1, pl.ds(QR, 8), :], 0.0)
        pieces += [first, strip[o, pl.ds(8, QR - 16), :], last]
    whole = jnp.concatenate(pieces, axis=0)
    beside = [strip[o, pl.ds(ER, 8), :] for o in range(NR)]
    pieces = []
    for t in range(4):
        even, odd = beside[2 * t], beside[2 * t + 1]
        x = jnp.where(lane8 < 66, even, 0.0) + jnp.where(lane8 >= 64, roll(odd, 64, 1), 0.0)
        x = x + jnp.where((lane8 >= 62) & (lane8 < 64), roll(odd, -16, 1), 0.0)
        if t < 3:
            x = x + jnp.where(lane8 >= 126, roll(beside[2 * t + 2], 48, 1), 0.0)
        if t > 0:
            x = x + jnp.where(lane8 < 2, roll(beside[2 * t - 1], 64, 1), 0.0)
        pieces.append(x)
    xt = jnp.concatenate([whole.T, jnp.concatenate(pieces, axis=1), jnp.zeros((8, NR * QR), F32)], axis=0)

    inner = pl.ds(16, NR * QR)
    g = six(split3(xt), [ct[i, inner, :] for i in range(3)])
    r1, r2, l2, l1 = (g[QC + i:QC + i + 1] for i in (0, 1, 6, 7))
    g = g[0:QC]

    jrow = lax.broadcasted_iota(jnp.int32, (QC, NR * QR), 0)
    fwd, bwd = g, g
    for i, s in enumerate((1, 2, 4, 8, 16, 32, 64)):
        p = small(i)
        fwd = fwd + jnp.where(jrow >= s, roll(fwd, s, 0) * p, 0.0)
        bwd = bwd + jnp.where(jrow < QC - s, roll(bwd, -s, 0) * p, 0.0)
    end, start = fwd[QC - 1:QC], bwd[0:1]
    own = small(7) * (fwd + bwd - g)
    near_a = small(7) * (l1 + small(0) * l2)
    near_b = small(7) * (r1 + small(0) * r2)
    for copy in halo:
        copy.wait()
    x = jnp.concatenate([by_phase(a, pl.ds(H0 + rp, 8, stride=4)) for a in range(3) for rp in range(4)], axis=0)
    y = permuted(x, perm[...])
    for a in range(3):
        for rp in range(4):
            i = (a * 4 + rp) * 8
            for pc in range(4):
                fields[a][rp * 4 + pc, pl.ds(QR, 8), pl.ds(0, 128)] = y[i:i + 8, pc * 128:(pc + 1) * 128]
    low8 = sub8 < 4
    lane_e = lax.broadcasted_iota(jnp.int32, (ER, 128), 1)

    def from_side(ref, tile):
        cols = pl.ds(tile * 128, 128)
        return jnp.concatenate(
            [ref[body, cols], jnp.where(low8, ref[below, cols], ref[above, cols])], axis=0
        )

    for a in range(3):
        pieces = []
        for rp in range(4):
            tile, gi = divmod(a * 4 + rp, 8)
            side_l, side_r = from_side(from_l, tile), from_side(from_r, tile)
            pieces.append(jnp.where(lane_e < 64, roll(side_r, -16 * gi, 1), roll(side_l, 112 - 16 * gi, 1)))
        y = permuted(jnp.concatenate(pieces, axis=0), side[...])
        for rp in range(4):
            for pc in range(4):
                fields[a][rp * 4 + pc, :, pl.ds(128, 128)] = y[rp * ER:(rp + 1) * ER, pc * 128:(pc + 1) * 128]
    for i in range(16):
        lum[i] = lum[i] * inside
        if i % 4 == 3:
            selx[i] = selx[i] * inside
        if i // 4 == 3:
            sely[i] = sely[i] * inside
    down()
    f2 = coarsest()
    f2 = jnp.concatenate([f2, f2[QR:ER]], axis=0)

    for copy in copies:
        copy.wait()
    low = sub8 < 4
    sum_a = jnp.zeros((8, 128), F32)
    sum_b = jnp.zeros((8, 128), F32)
    for o in range(NC):
        m = mom[o, pl.ds(0, 8), :]
        sum_a = sum_a + m * jnp.where(low, dist[lax.rem(c - o + 63, 32)], dist[c + o])
        sum_b = sum_b + m * jnp.where(low, dist[lax.rem(62 - c - o, 32)], dist[lax.rem(o - c + 63, 32)])

    def line(m, i):
        return jnp.concatenate([m[4 * i + t:4 * i + t + 1] for t in range(4)], axis=1)

    a_in = line(sum_a[0:4] + sum_a[4:8], 0) + near_a
    b_in = line(sum_b[0:4] + sum_b[4:8], 0) + near_b
    own = own + tab[pl.ds(0, QC), :] * a_in + tab[pl.ds(QC, QC), :] * b_in
    own = own - 4.0 * jnp.concatenate([
        line(mom[col_peer(-1), pl.ds(8, 8), :], 0), jnp.zeros((QC - 2, NR * QR), F32),
        line(mom[col_peer(1), pl.ds(8, 8), :], 1),
    ], axis=0)

    e2 = six(back, split3(own), ((1,), (1,)))

    lane = lax.broadcasted_iota(jnp.int32, (ER + 8, 128), 1)

    row = lax.broadcasted_iota(jnp.int32, (ER + 8, 128), 0)

    def beyond(inner, at, f):
        up = jnp.where((r == 0) & (row == 0), at, roll(at, 1, 0))
        down = jnp.where((r == NR - 1) & (row == QR - 1), at, roll(at, -1, 0))
        return 4.0 * ((1 + SCREEN) * at - f) - (up + down) - inner

    one = beyond(jnp.where(lane < 64, roll(e2, -1, 1), roll(e2, 1, 1)), e2, f2[:, 0:QC])
    side_f = f2[:, QC:EC]
    two = beyond(e2, one, jnp.where(lane < 64, roll(side_f, 1, 1), roll(side_f, -1, 1)))
    outer = jnp.where(lane == 0, roll(one, 1, 1), jnp.where(lane == 1, roll(two, 2, 1), 0.0))
    outer = jnp.where(lane == 127, roll(one, -1, 1), jnp.where(lane == 126, roll(two, -2, 1), outer))
    e2 = jnp.concatenate([e2, outer], axis=1)
    sub8 = lax.broadcasted_iota(jnp.int32, (8, EC), 0)
    e2 = jnp.concatenate([e2[0:QR], jnp.where(sub8 < 4, e2[QR:QR + 8], e2[QR + 8:QR + 16])], axis=0)
    e2 = e2 * inside

    for i in range(4):
        ea[i] = eb[i] + e2
    sweep(ea, ec, f1, w1, 2, 0.5)
    sweep(ec, ea, f1, w1, 2, 0.5)
    for pr in range(4):
        for pc in range(4):
            fa[pr * 4 + pc] = fb[pr * 4 + pc] + ea[(pr // 2) * 2 + pc // 2]
    sweep(fa, lum, rhs, w0, 4, 1.0)
    last_sweep(lum, fb, rhs, w0)
    copies = []
    half = QR // 2
    for h in range(2):
        x = jnp.concatenate([
            jnp.concatenate([fb[pr * 4 + pc, pl.ds(h * half, half), pl.ds(0, QC)] for pc in range(4)], axis=1)
            for pr in range(4)
        ], axis=0)
        y = permuted(x, permt[...])
        rows = pl.ds(h * 4 * half, 4 * half)
        for pr in range(4):
            for t in range(4):
                out[t, pl.ds(h * 4 * half + pr, half, stride=4), :] = y[pr * half:(pr + 1) * half, t * 128:(t + 1) * 128]
        for t in range(4):
            copy = pltpu.make_async_copy(out.at[t, rows], out_h.at[rows, pl.ds(t * 128, 128)], out_sem.at[h, t])
            copy.start()
            copies.append(copy)
    for copy in copies:
        copy.wait()


def shards(luminance, grad_x, grad_y, labels):
    consts = tables()
    vmem = pltpu.VMEM
    phases = vmem((16, ER, EC), F32)
    quarter = vmem((4, ER, EC), F32)
    nine = vmem((9, ER, EC), F32)
    dma = pltpu.SemaphoreType.DMA
    return pl.pallas_call(
        kernel,
        out_shape=jax.ShapeDtypeStruct((H0, W0), F32),
        in_specs=[pl.BlockSpec(memory_space=pl.ANY)] * 7,
        out_specs=pl.BlockSpec(memory_space=pl.ANY),
        scratch_shapes=[
            vmem((4, H0, W0), F32),
            vmem((4, H0, W0), F32),
            vmem((H0, W0), jnp.int32),
            vmem((3, 4, H0 + 32, 128), F32),
            vmem((W0, W0), BF),
            vmem((W0, W0), BF),
            vmem((128, W0), BF),
            vmem(consts[0].shape, BF),
            vmem(consts[1].shape, F32),
            vmem(consts[2].shape, F32),
            vmem((QR, 256), F32),
            vmem((QR, 256), F32),
            vmem((QR + 16, 256), F32),
            vmem((QR + 16, 256), F32),
            phases, phases, phases, phases, phases, phases,
            nine, nine, nine, nine,
            quarter, quarter, quarter, quarter,
            vmem((NR, ER + 8, QC), F32),
            vmem((NR, 16, 128), F32),
            vmem((NC, 16, 128), F32),
            vmem((4, H0, 128), F32),
            dma((4, 4)),
            dma((3,)),
            dma((2, 4)),
            dma((8,)),
            dma((8,)),
            dma((NR,)),
            dma((NR,)),
            dma((NR,)),
            dma((NR,)),
            dma((NC,)),
            dma((NC,)),
        ],
        compiler_params=pltpu.CompilerParams(
            collective_id=0, has_side_effects=True, vmem_limit_bytes=56 * 1024 * 1024
        ),
    )(luminance, grad_x, grad_y, labels, *[jnp.asarray(x) for x in consts])


def solution(mesh):
    return jax.shard_map(
        shards,
        mesh=mesh,
        in_specs=(
            P("rows", "cols"),
            P(None, "rows", "cols"),
            P(None, "rows", "cols"),
            P("rows", "cols"),
        ),
        out_specs=P("rows", "cols"),
        check_vma=False,
    )
```
